32 devices in a mesh: dp: 16 (over z, x, core), mp: 2 (over y).
Axes of the slice: x: 2, y: 2, z: 4, core: 2. Of those that a mesh axis runs over, the one named last changes fastest.
Arguments:
- tokens: bfloat16 [16384, 512], P(('dp', 'mp')), may hold values from -6 to 6
- pos_table: bfloat16 [512, 512], replicated, may hold values from -3 to 3
- qkv_weight: bfloat16 [512, 3, 512], P(None, None, 'mp'), may hold values from -0.25 to 0.25
- out_weight: bfloat16 [512, 512], P('mp'), may hold values from -2 to 2
- out_bias: bfloat16 [512], replicated, may hold values from -3 to 3
- norm1_gain: bfloat16 [512], replicated, may hold values from 0.5 to 1.5
- norm1_shift: bfloat16 [512], replicated, may hold values from -2 to 2
- up_weight: bfloat16 [512, 2048], P(None, 'mp'), may hold values from -0.25 to 0.25
- up_bias: bfloat16 [2048], P('mp'), may hold values from -3 to 3
- down_weight: bfloat16 [2048, 512], P('mp'), may hold values from -0.125 to 0.125
- down_bias: bfloat16 [512], replicated, may hold values from -3 to 3
- norm2_gain: bfloat16 [512], replicated, may hold values from 0.5 to 1.5
- norm2_shift: bfloat16 [512], replicated, may hold values from -2 to 2
- window: int32 [16], P('dp'), may hold values from 256 to 512, as said below
- cotangent: bfloat16 [16384, 512], P(('dp', 'mp')), may hold values from -6 to 6
Outputs:
- layer_out: bfloat16 [16384, 512], P(('dp', 'mp'))
- grad_tokens: bfloat16 [16384, 512], P(('dp', 'mp'))
- grad_pos_table: float32 [512, 512], replicated
- grad_qkv_weight: float32 [512, 3, 512], P(None, None, 'mp')
- grad_out_weight: float32 [512, 512], P('mp')
- grad_out_bias: float32 [512], replicated
- grad_norm1_gain: float32 [512], replicated
- grad_norm1_shift: float32 [512], replicated
- grad_up_weight: float32 [512, 2048], P(None, 'mp')
- grad_up_bias: float32 [2048], P('mp')
- grad_down_weight: float32 [2048, 512], P('mp')
- grad_down_bias: float32 [512], replicated
- grad_norm2_gain: float32 [512], replicated
- grad_norm2_shift: float32 [512], replicated
The draws below stay inside these ranges and needn't reach their ends.
Inputs may be any that keep to these rules, and one draw needn't show every extreme that they name: `window`: every entry is 256 or 512, each for exactly half of the rows.
All inputs are finite; a program needn't handle non-finite values.
Results may differ from the reference program's by a relative error of at most 0.019.
The reference program's roundings to bfloat16 on the way count: a program that leaves them out, or rounds other values in their place, can miss the bound.
Values may be sent and summed in bfloat16 or wider, within the bound.
No kernel may reach another device: no remote copies, remote signals or barrier semaphores. Data moves between devices by JAX's collectives and lax.ppermute only.
A program may use at most 128 MiB of HBM per device.

```python
import math
import jax
import jax.numpy as jnp
from jax import lax

D = 512
H = 8
HD = 64
FF = 2048
W_SHORT = 256
W_LONG = 512
ROW = 1024
TOKENS = 16384
ROWS = 16


def draw_window(key, part):
    shuffled = jax.random.permutation(key, ROWS)
    return (W_SHORT + shuffled % 2 * (W_LONG - W_SHORT)).astype(jnp.int32)


def block_scale(rng, dims, cuts, least, largest):
    loudness = 1.0
    for dim, blocks in cuts:
        draws = jax.random.uniform(jax.random.fold_in(jax.random.fold_in(rng, 6), dim), (blocks,), jnp.float32, least / len(cuts), largest / len(cuts))
        loudness = loudness * jnp.repeat(jnp.exp(draws), dims[dim] // blocks).reshape((-1,) + (1,) * (len(dims) - 1 - dim))
    return loudness


def noise(rng, shape, deviation, reach, pieces=(), held_as=jnp.bfloat16):
    loudness = block_scale(rng, shape, pieces, -0.22, 0.18) if pieces else 1.0
    values = jax.random.normal(rng, shape, jnp.float32) * deviation * loudness
    return jnp.minimum(jnp.maximum(values, -reach), reach).astype(held_as)


def setup_inputs(seed: int = 0) -> dict:
    splits = jax.random.split(jax.random.key(seed), 16)
    return {
        "tokens": noise(splits[0], (TOKENS, D), 1.0, 6.0, ((0, 32),)),
        "pos_table": noise(splits[1], (W_LONG, D), 0.5, 3.0),
        "qkv_weight": noise(splits[2], (D, 3, D), D ** -0.5, 0.25, ((2, 2),)),
        "out_weight": noise(splits[3], (D, D), 8 ** -0.5, 2.0, ((0, 2),)),
        "out_bias": noise(splits[4], (D,), 0.5, 3.0),
        "norm1_gain": jnp.clip(1.0 + 0.1 * jax.random.normal(splits[5], (D,), jnp.float32), 0.5, 1.5).astype(jnp.bfloat16),
        "norm1_shift": noise(splits[6], (D,), 0.3, 2.0),
        "up_weight": noise(splits[7], (D, FF), D ** -0.5, 0.25, ((1, 2),)),
        "up_bias": noise(splits[8], (FF,), 0.5, 3.0, ((0, 2),)),
        "down_weight": noise(splits[9], (FF, D), FF ** -0.5, 0.125, ((0, 2),)),
        "down_bias": noise(splits[10], (D,), 0.5, 3.0),
        "norm2_gain": jnp.clip(1.0 + 0.1 * jax.random.normal(splits[11], (D,), jnp.float32), 0.5, 1.5).astype(jnp.bfloat16),
        "norm2_shift": noise(splits[12], (D,), 0.3, 2.0),
        "window": draw_window(jax.random.fold_in(splits[15], 71), 0),
        "cotangent": noise(splits[14], (TOKENS, D), 1.0, 6.0, ((0, 32),)),
    }


@jax.custom_vjp
def low(v):
    return lax.optimization_barrier(v.astype(jnp.bfloat16)).astype(jnp.float32)

@jax.custom_vjp
def low_back(v):
    return v

def low_keep(v):
    return (low(v), None)

def low_pass(kept, grad):
    return (grad,)

def back_keep(v):
    return (v, None)

def back_low(kept, grad):
    return (low(grad),)
low.defvjp(low_keep, low_pass)
low_back.defvjp(back_keep, back_low)
epsilon = 1e-05
highest = lax.Precision.HIGHEST

def layer_norm(values_in, norm_gain, norm_shift):
    average = lax.optimization_barrier(jnp.mean(values_in, axis=-1, keepdims=True))
    centred = values_in - average
    variance = lax.optimization_barrier(jnp.mean(centred * centred, axis=-1, keepdims=True))
    return centred * lax.rsqrt(variance + epsilon) * norm_gain + norm_shift

def causal_mask(window_size):
    offsets = jnp.arange(W_LONG, dtype=jnp.int32)
    window_int = window_size.astype(jnp.int32)
    causal = offsets[:, None] >= offsets[None, :]
    same_window = offsets[:, None] // window_int == offsets[None, :] // window_int
    return causal & same_window

def attend_block(block_items):
    query_block, key_block, value_block, window_size = block_items
    allowed = causal_mask(window_size)[None]
    scores = low_back(jnp.einsum('qhe,khe->hqk', query_block, key_block, precision=highest) * HD ** (-0.5))
    diagonal = lax.optimization_barrier(jnp.sum(jnp.where(jnp.eye(W_LONG, dtype=jnp.bool_)[None], scores, 0.0), axis=-1, keepdims=True))
    filled = jnp.where(allowed, scores, diagonal)
    highest_score = lax.optimization_barrier(jnp.max(filled, axis=-1, keepdims=True))
    weights = jnp.where(allowed, jnp.exp(filled - highest_score), 0.0)
    log_total = jnp.log(lax.optimization_barrier(jnp.sum(weights, axis=-1, keepdims=True))) + highest_score
    probs = low(jnp.where(allowed, jnp.exp(filled - log_total), 0.0))
    return jnp.einsum('hqk,khe->qhe', probs, value_block, precision=highest)

def position_rows(pos_table, block_wins):
    short_rows = jnp.concatenate([pos_table[:W_SHORT], pos_table[:W_SHORT]], axis=0)
    is_long = (block_wins == W_LONG)[:, None, None]
    chosen = jnp.where(is_long, pos_table[None], short_rows[None])
    return chosen.reshape(-1, pos_table.shape[1])

def layer(tokens, params, window_rows):
    pos_table, qkv_weight, out_weight, out_bias, norm1_gain, norm1_shift, up_weight, up_bias, down_weight, down_bias, norm2_gain, norm2_shift = params
    group_tokens = window_rows.shape[0] * ROW
    blocks = group_tokens // W_LONG
    block_wins = jnp.repeat(window_rows, ROW // W_LONG).astype(jnp.int32)
    hidden_in = tokens + position_rows(pos_table, block_wins)
    hidden_low = low(hidden_in)
    mixed = low_back(low(jnp.einsum('sd,dcf->scf', hidden_low, qkv_weight, precision=highest)))
    shaped = mixed.reshape(blocks, W_LONG, 3, H, HD)
    context = lax.map(jax.checkpoint(attend_block), (shaped[:, :, 0], shaped[:, :, 1], shaped[:, :, 2], block_wins))
    context = low_back(low(context.reshape(group_tokens, D)))
    attn_branch = low_back(jnp.dot(context, out_weight, precision=highest))
    resid1 = hidden_in + attn_branch + out_bias
    normed1 = layer_norm(resid1, norm1_gain, norm1_shift)
    pre_act = low_back(jnp.dot(low(normed1), up_weight, precision=highest) + up_bias)
    act_low = low(jax.nn.gelu(pre_act, approximate=False))
    ffn_branch = low_back(jnp.dot(act_low, down_weight, precision=highest))
    resid2 = normed1 + ffn_branch + down_bias
    return layer_norm(resid2, norm2_gain, norm2_shift)

def reference(tokens, pos_table, qkv_weight, out_weight, out_bias, norm1_gain, norm1_shift, up_weight, up_bias, down_weight, down_bias, norm2_gain, norm2_shift, window, cotangent):
    params = tuple((param_array.astype(jnp.float32) for param_array in (pos_table, qkv_weight, out_weight, out_bias, norm1_gain, norm1_shift, up_weight, up_bias, down_weight, down_bias, norm2_gain, norm2_shift)))
    window_int = window.astype(jnp.int32)
    group_rows = math.gcd(ROWS, 4)
    groups = ROWS // group_rows
    group_tokens = group_rows * ROW
    token_groups = tokens.astype(jnp.float32).reshape(groups, group_tokens, D)
    cotangent_groups = cotangent.astype(jnp.float32).reshape(groups, group_tokens, D)
    window_groups = window_int.reshape(groups, group_rows)

    def group_step(running, inputs):
        token_block, cotangent_block, window_block = inputs

        def layer_call(token_arg, param_arg):
            return layer(token_arg, param_arg, window_block)
        outputs, pullback = jax.vjp(layer_call, token_block, params)
        grad_tokens, grad_params = pullback(cotangent_block)
        running = jax.tree.map(jnp.add, running, grad_params)
        return (running, (outputs, grad_tokens))
    zero_grads = jax.tree.map(jnp.zeros_like, params)
    totals, (outputs, grad_tokens) = lax.scan(group_step, zero_grads, (token_groups, cotangent_groups, window_groups))
    return (outputs.reshape(TOKENS, D).astype(jnp.bfloat16), grad_tokens.reshape(TOKENS, D).astype(jnp.bfloat16), totals[0], totals[1], totals[2], totals[3], totals[4], totals[5], totals[6], totals[7], totals[8], totals[9], totals[10], totals[11])
```

```python
import functools

import jax
import jax.numpy as jnp
from jax import lax
from jax.experimental import pallas as pl
from jax.experimental.pallas import tpu as pltpu
from jax.sharding import PartitionSpec as P

HD = 64
W_SHORT = 256
W_LONG = 512
ROW = 1024
LANES = 128
EXTRA = 16
EPSILON = 1e-05
MASKED = -1e30
F32 = jnp.float32
BF16 = jnp.bfloat16
VMEM_BYTES = 48 * 1024 * 1024

vmem = pl.BlockSpec(memory_space=pltpu.VMEM)
smem = pl.BlockSpec(memory_space=pltpu.SMEM)


def call(kernel, outs, args, specs=None, scratch=(), flops=0, bytes_accessed=0, name=None):
    return pl.pallas_call(
        kernel,
        out_shape=[jax.ShapeDtypeStruct(shape, dtype) for shape, dtype in outs],
        in_specs=specs or [vmem] * len(args),
        out_specs=[vmem] * len(outs),
        scratch_shapes=list(scratch),
        compiler_params=pltpu.CompilerParams(vmem_limit_bytes=VMEM_BYTES),
        cost_estimate=pl.CostEstimate(
            flops=flops, bytes_accessed=bytes_accessed, transcendentals=0
        ),
        name=name,
    )(*args)


def mm(a, b):
    return lax.dot_general(a, b, (((1,), (0,)), ((), ())), preferred_element_type=F32)


def mm_nt(a, b):
    return lax.dot_general(a, b, (((1,), (1,)), ((), ())), preferred_element_type=F32)


def mm_tn(a, b):
    return lax.dot_general(a, b, (((0,), (0,)), ((), ())), preferred_element_type=F32)


def position_rows(pos_ref, is_long):
    first = pos_ref[0:W_SHORT, :].astype(F32)
    second = jnp.where(is_long, pos_ref[W_SHORT:W_LONG, :].astype(F32), first)
    return first, second


def hidden_rows(tokens_ref, pos_ref, windows):
    parts = []
    for block, is_long in enumerate(windows):
        first, second = position_rows(pos_ref, is_long)
        start = block * W_LONG
        parts.append(tokens_ref[start : start + W_SHORT, :].astype(F32) + first)
        parts.append(tokens_ref[start + W_SHORT : start + W_LONG, :].astype(F32) + second)
    return jnp.concatenate(parts, axis=0)


def read_windows(win_ref, blocks):
    return [win_ref[block] == W_LONG for block in range(blocks)]


def norm_stats(values):
    average = jnp.mean(values, axis=-1, keepdims=True)
    centred = values - average
    variance = jnp.mean(centred * centred, axis=-1, keepdims=True)
    scale = lax.rsqrt(variance + EPSILON)
    return centred * scale, scale


def norm_grad(grad_hat, hat, scale):
    mean_grad = jnp.mean(grad_hat, axis=-1, keepdims=True)
    mean_both = jnp.mean(grad_hat * hat, axis=-1, keepdims=True)
    return scale * (grad_hat - mean_grad - hat * mean_both)


def head_mask(rows):
    return lax.broadcasted_iota(jnp.int32, (rows, LANES), 1) < HD


def own_head(value, is_low, head):
    zero = jnp.zeros_like(value)
    return jnp.where(is_low, value, zero) if head == 0 else jnp.where(is_low, zero, value)


def attend_forward(hidden_low, weight_ref, windows, mixed_ref, probs_ref, context_ref):
    rows, width = context_ref.shape
    for c in range(3):
        part = mm(hidden_low, weight_ref[c]).astype(BF16)
        mixed_ref[c] = part * BF16(HD**-0.5) if c == 0 else part
    causal = lax.broadcasted_iota(jnp.int32, (W_SHORT, W_SHORT), 0) >= lax.broadcasted_iota(
        jnp.int32, (W_SHORT, W_SHORT), 1
    )
    is_low = head_mask(W_SHORT)
    for block, is_long in enumerate(windows):
        lo = slice(block * W_LONG, block * W_LONG + W_SHORT)
        hi = slice(block * W_LONG + W_SHORT, (block + 1) * W_LONG)
        for pair in range(width // LANES):
            lanes = slice(pair * LANES, (pair + 1) * LANES)
            key_lo, key_hi = mixed_ref[1, lo, lanes], mixed_ref[1, hi, lanes]
            val_lo, val_hi = mixed_ref[2, lo, lanes], mixed_ref[2, hi, lanes]
            query_lo, query_hi = mixed_ref[0, lo, lanes], mixed_ref[0, hi, lanes]
            results = []
            for head in range(2):
                slot = ((block * (width // LANES) + pair) * 2 + head) * 3
                q_lo = own_head(query_lo, is_low, head)
                q_hi = own_head(query_hi, is_low, head)
                s_a = jnp.where(causal, mm_nt(q_lo, key_lo), MASKED)
                e_a = jnp.exp(s_a - jnp.max(s_a, axis=-1, keepdims=True))
                p_a = (e_a * (1.0 / jnp.sum(e_a, axis=-1, keepdims=True))).astype(BF16)
                s_b = jnp.where(is_long, mm_nt(q_hi, key_lo), MASKED)
                s_c = jnp.where(causal, mm_nt(q_hi, key_hi), MASKED)
                top = jnp.max(jnp.maximum(s_b, s_c), axis=-1, keepdims=True)
                e_b = jnp.exp(s_b - top)
                e_c = jnp.exp(s_c - top)
                inverse = 1.0 / jnp.sum(e_b + e_c, axis=-1, keepdims=True)
                p_b = (e_b * inverse).astype(BF16)
                p_c = (e_c * inverse).astype(BF16)
                probs_ref[slot] = p_a
                probs_ref[slot + 1] = p_b
                probs_ref[slot + 2] = p_c
                results.append((mm(p_a, val_lo), mm(p_b, val_lo) + mm(p_c, val_hi)))
            context_ref[lo, lanes] = jnp.where(is_low, results[0][0], results[1][0]).astype(BF16)
            context_ref[hi, lanes] = jnp.where(is_low, results[0][1], results[1][1]).astype(BF16)


def attend_backward(grad_context, mixed_ref, probs_ref, blocks, grad_mixed_ref):
    width = mixed_ref.shape[2]
    is_low = head_mask(W_SHORT)
    for block in range(blocks):
        lo = slice(block * W_LONG, block * W_LONG + W_SHORT)
        hi = slice(block * W_LONG + W_SHORT, (block + 1) * W_LONG)
        for pair in range(width // LANES):
            lanes = slice(pair * LANES, (pair + 1) * LANES)
            q_lo, q_hi = mixed_ref[0, lo, lanes], mixed_ref[0, hi, lanes]
            k_lo, k_hi = mixed_ref[1, lo, lanes], mixed_ref[1, hi, lanes]
            v_lo, v_hi = mixed_ref[2, lo, lanes], mixed_ref[2, hi, lanes]
            g_lo, g_hi = grad_context[lo, lanes], grad_context[hi, lanes]
            results = []
            for head in range(2):
                slot = ((block * (width // LANES) + pair) * 2 + head) * 3
                gm_lo = own_head(g_lo, is_low, head)
                gm_hi = own_head(g_hi, is_low, head)
                pb_a, pb_b, pb_c = probs_ref[slot], probs_ref[slot + 1], probs_ref[slot + 2]
                p_a, p_b, p_c = pb_a.astype(F32), pb_b.astype(F32), pb_c.astype(F32)
                g_a = mm_nt(gm_lo, v_lo)
                g_b = mm_nt(gm_hi, v_lo)
                g_c = mm_nt(gm_hi, v_hi)
                inner_a = jnp.sum(p_a * g_a, axis=-1, keepdims=True)
                inner_b = jnp.sum(p_b * g_b + p_c * g_c, axis=-1, keepdims=True)
                s_a = (p_a * (g_a - inner_a)).astype(BF16)
                s_b = (p_b * (g_b - inner_b)).astype(BF16)
                s_c = (p_c * (g_c - inner_b)).astype(BF16)
                results.append(
                    (
                        mm(s_a, k_lo),
                        mm(s_b, k_lo) + mm(s_c, k_hi),
                        mm_tn(s_a, q_lo) + mm_tn(s_b, q_hi),
                        mm_tn(s_c, q_hi),
                        mm_tn(pb_a, g_lo) + mm_tn(pb_b, g_hi),
                        mm_tn(pb_c, g_hi),
                    )
                )
            both = [jnp.where(is_low, a, b) for a, b in zip(*results)]
            grad_mixed_ref[0, lo, lanes] = (both[0] * HD**-0.5).astype(BF16)
            grad_mixed_ref[0, hi, lanes] = (both[1] * HD**-0.5).astype(BF16)
            grad_mixed_ref[1, lo, lanes] = both[2].astype(BF16)
            grad_mixed_ref[1, hi, lanes] = both[3].astype(BF16)
            grad_mixed_ref[2, lo, lanes] = both[4].astype(BF16)
            grad_mixed_ref[2, hi, lanes] = both[5].astype(BF16)


def normal_parts(x):
    density = jnp.exp(x * x * -0.5)
    t = 1.0 / (1.0 + jnp.abs(x) * 0.23164189)
    poly = t * (
        0.127414796
        + t * (-0.142248368 + t * (0.7107068705 + t * (-0.7265760135 + t * 0.5307027145)))
    )
    tail = poly * density
    return jnp.where(x > 0, 1.0 - tail, tail), density * 0.3989422804


def first_kernel(win_ref, tokens_ref, pos_ref, weight_ref, mixed_ref, probs_ref, context_ref):
    windows = read_windows(win_ref, tokens_ref.shape[0] // W_LONG)
    hidden_low = hidden_rows(tokens_ref, pos_ref, windows).astype(BF16)
    attend_forward(hidden_low, weight_ref, windows, mixed_ref, probs_ref, context_ref)


def second_kernel(
    win_ref,
    tokens_ref,
    pos_ref,
    weight_ref,
    context_own_ref,
    out_own_ref,
    out_oth_ref,
    vec_ref,
    mixed_ref,
    probs_ref,
    context_ref,
    resid_ref,
):
    windows = read_windows(win_ref, tokens_ref.shape[0] // W_LONG)
    hidden_in = hidden_rows(tokens_ref, pos_ref, windows)
    attend_forward(
        hidden_in.astype(BF16), weight_ref, windows, mixed_ref, probs_ref, context_ref
    )
    branch = mm(context_own_ref[...], out_own_ref[...]) + mm(context_ref[...], out_oth_ref[...])
    hidden_in = hidden_rows(tokens_ref, pos_ref, windows)
    resid_ref[...] = hidden_in + branch + vec_ref[0:1, :]


def ffn_kernel(
    resid_ref,
    cot_ref,
    up_own_ref,
    up_oth_ref,
    down_own_ref,
    down_oth_ref,
    bias_ref,
    vec_ref,
    layer_ref,
    down_own_grad,
    down_oth_grad,
    up_own_grad,
    up_oth_grad,
    small_ref,
    bias_grad_ref,
    grad_resid_ref,
    act_ref,
    slope_ref,
    low_ref,
    hat_ref,
    grad_ref,
):
    rows, width = resid_ref.shape
    units = up_own_ref.shape[1]
    chunk = 256
    hat, scale = norm_stats(resid_ref[...])
    hat_ref[...] = hat
    normed = hat * vec_ref[1:2, :] + vec_ref[2:3, :]
    low_ref[...] = normed.astype(BF16)
    for half, up in enumerate((up_own_ref, up_oth_ref)):
        for start in range(0, units, chunk):
            cols = slice(start, start + chunk)
            pre = mm(low_ref[...], up[:, cols]) + bias_ref[half : half + 1, cols]
            total, density = normal_parts(pre)
            act_ref[half, :, cols] = (pre * total).astype(BF16)
            slope_ref[half, :, cols] = total + pre * density
    branch = mm(act_ref[0], down_own_ref[...]) + mm(act_ref[1], down_oth_ref[...])
    normed = hat_ref[...] * vec_ref[1:2, :] + vec_ref[2:3, :]
    hat2, scale2 = norm_stats(normed + branch + vec_ref[3:4, :])
    layer_ref[...] = (hat2 * vec_ref[4:5, :] + vec_ref[5:6, :]).astype(BF16)
    cot = cot_ref[...].astype(F32)
    small_ref[4:5, :] = jnp.sum(cot * hat2, axis=0, keepdims=True)
    small_ref[5:6, :] = jnp.sum(cot, axis=0, keepdims=True)
    grad = norm_grad(cot * vec_ref[4:5, :], hat2, scale2)
    small_ref[3:4, :] = jnp.sum(grad, axis=0, keepdims=True)
    grad_ref[...] = grad
    grad_low = grad.astype(BF16)
    for half, up, down, down_grad, up_grad in (
        (1, up_oth_ref, down_oth_ref, down_oth_grad, up_oth_grad),
        (0, up_own_ref, down_own_ref, down_own_grad, up_own_grad),
    ):
        for start in range(0, units, chunk):
            cols = slice(start, start + chunk)
            act = act_ref[half, :, cols]
            down_grad[cols, :] = mm_tn(act, grad_low).astype(BF16)
            pre_grad = (mm_nt(grad_low, down[cols, :]) * slope_ref[half, :, cols]).astype(BF16)
            act_ref[half, :, cols] = pre_grad
            bias_grad_ref[half : half + 1, cols] = jnp.sum(
                pre_grad.astype(F32), axis=0, keepdims=True
            )
        for start in range(0, units, width):
            cols = slice(start, start + width)
            up_grad[start : start + width, :] = mm_tn(low_ref[...], act_ref[half, :, cols]).astype(
                BF16
            )
        grad_ref[...] += mm_nt(act_ref[half], up[...])
    grad = grad_ref[...]
    hat, scale = norm_stats(resid_ref[...])
    small_ref[1:2, :] = jnp.sum(grad * hat, axis=0, keepdims=True)
    small_ref[2:3, :] = jnp.sum(grad, axis=0, keepdims=True)
    grad = norm_grad(grad * vec_ref[1:2, :], hat, scale)
    small_ref[0:1, :] = jnp.sum(grad, axis=0, keepdims=True)
    small_ref[6:8, :] = jnp.zeros((2, width), F32)
    grad_resid_ref[...] = grad


def last_kernel(
    win_ref,
    tokens_ref,
    pos_ref,
    grad_resid_ref,
    w_own_ref,
    w_oth_ref,
    out_own_ref,
    out_oth_ref,
    mixed_own_ref,
    mixed_oth_ref,
    probs_own_ref,
    probs_oth_ref,
    context_own_ref,
    context_oth_ref,
    own_grad,
    oth_grad,
    tokens_grad_ref,
    table_ref,
    gm_ref,
    grad_ref,
):
    rows, width = tokens_ref.shape
    half_width = width // 2
    blocks = rows // W_LONG
    windows = read_windows(win_ref, blocks)
    hidden_low = hidden_rows(tokens_ref, pos_ref, windows).astype(BF16)
    grad_low = grad_resid_ref[...].astype(BF16)
    grad_ref[...] = grad_resid_ref[...]
    for weight, out_w, mixed, probs, context, grads in (
        (w_oth_ref, out_oth_ref, mixed_oth_ref, probs_oth_ref, context_oth_ref, oth_grad),
        (w_own_ref, out_own_ref, mixed_own_ref, probs_own_ref, context_own_ref, own_grad),
    ):
        grads[width + half_width :, :] = mm_tn(context[...], grad_low).astype(BF16)
        grad_context = mm_nt(grad_low, out_w[...]).astype(BF16)
        attend_backward(grad_context, mixed, probs, blocks, gm_ref)
        grads[0:width, 0:half_width] = mm_tn(hidden_low, gm_ref[0]).astype(BF16)
        grads[0:width, half_width:] = mm_tn(hidden_low, gm_ref[1]).astype(BF16)
        value_grad = mm_tn(hidden_low, gm_ref[2]).astype(BF16)
        grads[width : width + half_width, 0:half_width] = value_grad[0:half_width, :]
        grads[width : width + half_width, half_width:] = value_grad[half_width:, :]
        grad_ref[...] += (
            mm_nt(gm_ref[0], weight[0]) + mm_nt(gm_ref[1], weight[1]) + mm_nt(gm_ref[2], weight[2])
        )
    grad = grad_ref[...]
    tokens_grad_ref[...] = grad.astype(BF16)
    first, second = None, None
    for block, is_long in enumerate(windows):
        top = grad[block * W_LONG : block * W_LONG + W_SHORT]
        bottom = grad[block * W_LONG + W_SHORT : (block + 1) * W_LONG]
        zero = jnp.zeros_like(top)
        part_first = top + jnp.where(is_long, zero, bottom)
        part_second = jnp.where(is_long, bottom, zero)
        first = part_first if first is None else first + part_first
        second = part_second if second is None else second + part_second
    table_ref[0:W_SHORT, :] = first.astype(BF16)
    table_ref[W_SHORT:, :] = second.astype(BF16)


def per_device(
    tokens,
    pos_table,
    qkv_weight,
    out_weight,
    out_bias,
    norm1_gain,
    norm1_shift,
    up_weight,
    up_bias,
    down_weight,
    down_bias,
    norm2_gain,
    norm2_shift,
    window,
    cotangent,
):
    rows, width = tokens.shape
    blocks = rows // W_LONG
    half_width = width // 2
    heads_half = half_width // HD
    starts = lax.axis_index("mp") * rows + jnp.arange(blocks, dtype=jnp.int32) * W_LONG
    win = window[starts // ROW]
    vectors = jnp.stack(
        [out_bias, norm1_gain, norm1_shift, down_bias, norm2_gain, norm2_shift]
    ).astype(F32)

    qkv = lax.all_gather(jnp.transpose(qkv_weight, (1, 0, 2)), "mp", axis=2, tiled=True)
    out_w = lax.all_gather(out_weight, "mp", axis=0, tiled=True)
    up_w = lax.all_gather(up_weight, "mp", axis=1, tiled=True)
    bias = lax.all_gather(up_bias, "mp", axis=0, tiled=True)
    down_w = lax.all_gather(down_weight, "mp", axis=0, tiled=True)
    units = up_w.shape[1] // 2
    w_own, w_oth = qkv[:, :, :half_width], qkv[:, :, half_width:]
    out_own, out_oth = out_w[:half_width], out_w[half_width:]
    up_own, up_oth = up_w[:, :units], up_w[:, units:]
    down_own, down_oth = down_w[:units], down_w[units:]
    bias2 = bias.reshape(2, units).astype(F32)

    mixed_shape = ((3, rows, half_width), BF16)
    probs_shape = ((blocks * heads_half * 3, W_SHORT, W_SHORT), BF16)
    context_shape = ((rows, half_width), BF16)
    wide = ((rows, width), F32)
    mixed_own, probs_own, context_own = call(
        first_kernel,
        [mixed_shape, probs_shape, context_shape],
        [win, tokens, pos_table, w_own],
        [smem, vmem, vmem, vmem],
        name="attend_first",
    )
    mixed_oth, probs_oth, context_oth, resid = call(
        second_kernel,
        [mixed_shape, probs_shape, context_shape, wide],
        [win, tokens, pos_table, w_oth, context_own, out_own, out_oth, vectors],
        [smem] + [vmem] * 7,
        name="attend_second",
    )
    package = ((width * 2, width), BF16)
    layer_out, down_own_g, down_oth_g, up_own_g, up_oth_g, small, bias_g, grad_resid = call(
        ffn_kernel,
        [
            ((rows, width), BF16),
            package,
            package,
            package,
            package,
            ((8, width), F32),
            ((2, units), F32),
            wide,
        ],
        [resid, cotangent, up_own, up_oth, down_own, down_oth, bias2, vectors],
        scratch=[
            pltpu.VMEM((2, rows, units), BF16),
            pltpu.VMEM((2, rows, units), F32),
            pltpu.VMEM((rows, width), BF16),
            pltpu.VMEM((rows, width), F32),
            pltpu.VMEM((rows, width), F32),
        ],
        name="feed_forward",
    )
    att_own_g, att_oth_g, grad_tokens, table = call(
        last_kernel,
        [package, package, ((rows, width), BF16), ((W_LONG, width), BF16)],
        [
            win,
            tokens,
            pos_table,
            grad_resid,
            w_own,
            w_oth,
            out_own,
            out_oth,
            mixed_own,
            mixed_oth,
            probs_own,
            probs_oth,
            context_own,
            context_oth,
        ],
        [smem] + [vmem] * 13,
        scratch=[pltpu.VMEM((3, rows, half_width), BF16), pltpu.VMEM((rows, width), F32)],
        name="attend_backward",
    )

    def summed(own, oth, make, dim):
        whole = jnp.concatenate([make(own), make(oth)], axis=dim)
        part = lax.psum_scatter(whole, "mp", scatter_dimension=dim, tiled=True)
        return lax.psum(part, "dp").astype(F32)

    def qkv_part(g):
        value = jnp.concatenate(
            [g[width : width + half_width, :half_width], g[width : width + half_width, half_width:]],
            axis=0,
        )
        return jnp.stack([g[:width, :half_width], g[:width, half_width:], value])

    def up_part(g):
        return jnp.concatenate([g[s : s + width] for s in range(0, g.shape[0], width)], axis=1)

    qkv_g = jnp.transpose(summed(att_own_g, att_oth_g, qkv_part, 2), (1, 0, 2))
    out_g = summed(att_own_g, att_oth_g, lambda g: g[width + half_width :], 0)
    up_g = summed(up_own_g, up_oth_g, up_part, 1)
    down_g = summed(down_own_g, down_oth_g, lambda g: g, 0)
    bias_part = lax.psum_scatter(bias_g.reshape(-1), "mp", scatter_dimension=0, tiled=True)
    bias_sum = lax.psum(bias_part, "dp")
    small = lax.psum(small, ("dp", "mp"))
    table = lax.psum(table.astype(F32), ("dp", "mp"))
    return (
        layer_out,
        grad_tokens,
        table,
        qkv_g,
        out_g,
        small[0],
        small[1],
        small[2],
        up_g,
        bias_sum,
        down_g,
        small[3],
        small[4],
        small[5],
    )


def solution(mesh):
    placed = (
        P(("dp", "mp"), None),
        P(),
        P(None, None, "mp"),
        P("mp", None),
        P(),
        P(),
        P(),
        P(None, "mp"),
        P("mp"),
        P("mp", None),
        P(),
        P(),
        P(),
        P("dp"),
        P(("dp", "mp"), None),
    )
    return jax.shard_map(
        per_device,
        mesh=mesh,
        in_specs=placed,
        out_specs=(
            P(("dp", "mp"), None),
            P(("dp", "mp"), None),
            P(),
            P(None, None, "mp"),
            P("mp", None),
            P(),
            P(),
            P(),
            P(None, "mp"),
            P("mp"),
            P("mp", None),
            P(),
            P(),
            P(),
        ),
        check_vma=False,
    )
```

```python
import functools

import jax
import jax.numpy as jnp
from jax import lax
from jax.experimental import pallas as pl
from jax.experimental.pallas import tpu as pltpu
from jax.sharding import Mesh
from jax.sharding import PartitionSpec as P

HD = 64
W_SHORT = 256
W_LONG = 512
ROW = 1024
LANES = 128
EXTRA = 16
CHUNK = 256
EPSILON = 1e-05
MASKED = -1e30
F32 = jnp.float32
BF16 = jnp.bfloat16
MIB = 1024 * 1024
FLOPS_PER_US = 10**9

vmem = pl.BlockSpec(memory_space=pltpu.VMEM)
smem = pl.BlockSpec(memory_space=pltpu.SMEM)
anywhere = pl.BlockSpec(memory_space=pl.ANY)


def call(kernel, outs, args, after=(), scratch=(), us=1, mib=32, smem_args=0, name=None):
    flat, tree = jax.tree.flatten(tuple(args))
    count, extra = len(flat), len(after)

    def flat_kernel(*refs):
        kernel(*jax.tree.unflatten(tree, refs[:count]), *refs[count + extra :])

    return pl.pallas_call(
        flat_kernel,
        out_shape=[
            jax.ShapeDtypeStruct(out, BF16) if isinstance(out[0], int) else jax.ShapeDtypeStruct(*out)
            for out in outs
        ],
        in_specs=[smem] * smem_args + [vmem] * (count - smem_args) + [anywhere] * extra,
        out_specs=[vmem] * len(outs),
        scratch_shapes=[pltpu.VMEM(shape, dtype) for shape, dtype in scratch],
        compiler_params=pltpu.CompilerParams(vmem_limit_bytes=mib * MIB),
        cost_estimate=pl.CostEstimate(
            flops=us * FLOPS_PER_US, bytes_accessed=0, transcendentals=0
        ),
        name=name,
    )(*flat, *after)


def place(axis):
    return lax.axis_index(axis)


def row(ref, start=0, size=None):
    size = ref.shape[0] if size is None else size
    return ref[start : start + size].astype(F32).reshape(1, size)


def mm(a, b):
    return lax.dot_general(a, b, (((1,), (0,)), ((), ())), preferred_element_type=F32)


def mm_nt(a, b):
    return lax.dot_general(a, b, (((1,), (1,)), ((), ())), preferred_element_type=F32)


def mm_tn(a, b):
    return lax.dot_general(a, b, (((0,), (0,)), ((), ())), preferred_element_type=F32)


def position_rows(pos_ref, is_long):
    first = pos_ref[0:W_SHORT, :].astype(F32)
    second = jnp.where(is_long, pos_ref[W_SHORT:W_LONG, :].astype(F32), first)
    return first, second


def hidden_rows(tokens_ref, pos_ref, windows):
    parts = []
    for block, is_long in enumerate(windows):
        first, second = position_rows(pos_ref, is_long)
        start = block * W_LONG
        parts.append(tokens_ref[start : start + W_SHORT, :].astype(F32) + first)
        parts.append(tokens_ref[start + W_SHORT : start + W_LONG, :].astype(F32) + second)
    return jnp.concatenate(parts, axis=0)


def read_windows(win_ref, rows):
    first = place("mp") * rows
    return [
        win_ref[lax.div(first + block * W_LONG, ROW)] == W_LONG for block in range(rows // W_LONG)
    ]


def norm_stats(values):
    average = jnp.mean(values, axis=-1, keepdims=True)
    centred = values - average
    variance = jnp.mean(centred * centred, axis=-1, keepdims=True)
    scale = lax.rsqrt(variance + EPSILON)
    return centred * scale, scale


def norm_grad(grad_hat, hat, scale):
    mean_grad = jnp.mean(grad_hat, axis=-1, keepdims=True)
    mean_both = jnp.mean(grad_hat * hat, axis=-1, keepdims=True)
    return scale * (grad_hat - mean_grad - hat * mean_both)


def head_mask(rows):
    return lax.broadcasted_iota(jnp.int32, (rows, LANES), 1) < HD


def own_head(value, is_low, head):
    zero = jnp.zeros_like(value)
    return jnp.where(is_low, value, zero) if head == 0 else jnp.where(is_low, zero, value)


def attend_forward(hidden_low, weight_ref, windows, mixed_ref, probs_ref, context_ref):
    rows, width = context_ref.shape
    for c in range(3):
        part = mm(hidden_low, weight_ref[c]).astype(BF16)
        mixed_ref[c] = part * BF16(HD**-0.5) if c == 0 else part
    causal = lax.broadcasted_iota(jnp.int32, (W_SHORT, W_SHORT), 0) >= lax.broadcasted_iota(
        jnp.int32, (W_SHORT, W_SHORT), 1
    )
    is_low = head_mask(W_SHORT)
    for block, is_long in enumerate(windows):
        lo = slice(block * W_LONG, block * W_LONG + W_SHORT)
        hi = slice(block * W_LONG + W_SHORT, (block + 1) * W_LONG)
        for pair in range(width // LANES):
            lanes = slice(pair * LANES, (pair + 1) * LANES)
            key_lo, key_hi = mixed_ref[1, lo, lanes], mixed_ref[1, hi, lanes]
            val_lo, val_hi = mixed_ref[2, lo, lanes], mixed_ref[2, hi, lanes]
            query_lo, query_hi = mixed_ref[0, lo, lanes], mixed_ref[0, hi, lanes]
            results = []
            for head in range(2):
                slot = ((block * (width // LANES) + pair) * 2 + head) * 3
                q_lo = own_head(query_lo, is_low, head)
                q_hi = own_head(query_hi, is_low, head)
                s_a = jnp.where(causal, mm_nt(q_lo, key_lo), MASKED)
                e_a = jnp.exp(s_a - jnp.max(s_a, axis=-1, keepdims=True))
                p_a = (e_a * (1.0 / jnp.sum(e_a, axis=-1, keepdims=True))).astype(BF16)
                s_b = jnp.where(is_long, mm_nt(q_hi, key_lo), MASKED)
                s_c = jnp.where(causal, mm_nt(q_hi, key_hi), MASKED)
                top = jnp.max(jnp.maximum(s_b, s_c), axis=-1, keepdims=True)
                e_b = jnp.exp(s_b - top)
                e_c = jnp.exp(s_c - top)
                inverse = 1.0 / jnp.sum(e_b + e_c, axis=-1, keepdims=True)
                p_b = (e_b * inverse).astype(BF16)
                p_c = (e_c * inverse).astype(BF16)
                probs_ref[slot] = p_a
                probs_ref[slot + 1] = p_b
                probs_ref[slot + 2] = p_c
                results.append((mm(p_a, val_lo), mm(p_b, val_lo) + mm(p_c, val_hi)))
            context_ref[lo, lanes] = jnp.where(is_low, results[0][0], results[1][0]).astype(BF16)
            context_ref[hi, lanes] = jnp.where(is_low, results[0][1], results[1][1]).astype(BF16)


def attend_backward(grad_context, mixed_ref, probs_ref, blocks, grad_mixed_ref):
    width = mixed_ref.shape[2]
    is_low = head_mask(W_SHORT)
    for block in range(blocks):
        lo = slice(block * W_LONG, block * W_LONG + W_SHORT)
        hi = slice(block * W_LONG + W_SHORT, (block + 1) * W_LONG)
        for pair in range(width // LANES):
            lanes = slice(pair * LANES, (pair + 1) * LANES)
            q_lo, q_hi = mixed_ref[0, lo, lanes], mixed_ref[0, hi, lanes]
            k_lo, k_hi = mixed_ref[1, lo, lanes], mixed_ref[1, hi, lanes]
            v_lo, v_hi = mixed_ref[2, lo, lanes], mixed_ref[2, hi, lanes]
            g_lo, g_hi = grad_context[lo, lanes], grad_context[hi, lanes]
            results = []
            for head in range(2):
                slot = ((block * (width // LANES) + pair) * 2 + head) * 3
                gm_lo = own_head(g_lo, is_low, head)
                gm_hi = own_head(g_hi, is_low, head)
                pb_a, pb_b, pb_c = probs_ref[slot], probs_ref[slot + 1], probs_ref[slot + 2]
                p_a, p_b, p_c = pb_a.astype(F32), pb_b.astype(F32), pb_c.astype(F32)
                g_a = mm_nt(gm_lo, v_lo)
                g_b = mm_nt(gm_hi, v_lo)
                g_c = mm_nt(gm_hi, v_hi)
                inner_a = jnp.sum(p_a * g_a, axis=-1, keepdims=True)
                inner_b = jnp.sum(p_b * g_b + p_c * g_c, axis=-1, keepdims=True)
                s_a = (p_a * (g_a - inner_a)).astype(BF16)
                s_b = (p_b * (g_b - inner_b)).astype(BF16)
                s_c = (p_c * (g_c - inner_b)).astype(BF16)
                results.append(
                    (
                        mm(s_a, k_lo),
                        mm(s_b, k_lo) + mm(s_c, k_hi),
                        mm_tn(s_a, q_lo) + mm_tn(s_b, q_hi),
                        mm_tn(s_c, q_hi),
                        mm_tn(pb_a, g_lo) + mm_tn(pb_b, g_hi),
                        mm_tn(pb_c, g_hi),
                    )
                )
            both = [jnp.where(is_low, a, b) for a, b in zip(*results)]
            grad_mixed_ref[0, lo, lanes] = (both[0] * HD**-0.5).astype(BF16)
            grad_mixed_ref[0, hi, lanes] = (both[1] * HD**-0.5).astype(BF16)
            grad_mixed_ref[1, lo, lanes] = both[2].astype(BF16)
            grad_mixed_ref[1, hi, lanes] = both[3].astype(BF16)
            grad_mixed_ref[2, lo, lanes] = both[4].astype(BF16)
            grad_mixed_ref[2, hi, lanes] = both[5].astype(BF16)


def normal_parts(x):
    density = jnp.exp(x * x * -0.5)
    t = 1.0 / (1.0 + jnp.abs(x) * 0.23164189)
    poly = t * (
        0.127414796
        + t * (-0.142248368 + t * (0.7107068705 + t * (-0.7265760135 + t * 0.5307027145)))
    )
    tail = poly * density
    return jnp.where(x > 0, 1.0 - tail, tail), density * 0.3989422804


def first_kernel(win_ref, tokens_ref, pos_ref, weight_ref, mixed_ref, probs_ref, context_ref):
    windows = read_windows(win_ref, tokens_ref.shape[0])
    hidden_low = hidden_rows(tokens_ref, pos_ref, windows).astype(BF16)
    attend_forward(hidden_low, weight_ref, windows, mixed_ref, probs_ref, context_ref)


def quarter():
    return place("core") * 2 + place("x")


def part(index, size):
    return pl.ds(pl.multiple_of(index * size, size), size)


def pack_attend_kernel(qkv_ref, out_ref, bias_ref, send_ref):
    _, width, half = qkv_ref.shape
    depth, mine = width // 4, quarter()
    send_ref[0:depth, 0:half] = qkv_ref[0, part(mine, depth), :]
    send_ref[0:depth, half:] = qkv_ref[1, part(mine, depth), :]
    value = qkv_ref[2, part(mine, depth), :]
    send_ref[depth : depth + depth // 2, 0:half] = value[0 : depth // 2]
    send_ref[depth : depth + depth // 2, half:] = value[depth // 2 :]
    start = depth + depth // 2
    send_ref[start : 2 * depth, :] = out_ref[part(mine, depth // 2), :]
    for i in range(EXTRA):
        index = i if (i + 1) * width <= bias_ref.shape[0] else 0
        send_ref[2 * depth + i : 2 * depth + i + 1, :] = row(bias_ref, index * width, width).astype(
            BF16
        )


def pack_ffn_kernel(up_ref, down_ref, up_to, down_to):
    width, units = up_ref.shape
    depth, mine = width // 4, quarter()
    for i in range(units // width):
        up_to[i * depth : (i + 1) * depth, :] = up_ref[
            part(mine, depth), i * width : (i + 1) * width
        ]
    down_to[...] = down_ref[part(mine, units // 4), :]


def places(pieces):
    x, core = place("x"), place("core")
    from_y, from_x, core_y, core_x = pieces
    return (
        (from_y, core * 2 + x),
        (from_x, core * 2 + 1 - x),
        (core_y, (1 - core) * 2 + x),
        (core_x, (1 - core) * 2 + 1 - x),
    )


def second_kernel(
    win_ref,
    tokens_ref,
    pos_ref,
    pieces,
    context_own_ref,
    out_own_ref,
    out_bias_ref,
    mixed_ref,
    probs_ref,
    context_ref,
    resid_ref,
    w_oth_ref,
    out_oth_ref,
    bias_oth_ref,
):
    width = tokens_ref.shape[1]
    half, depth = width // 2, width // 4
    windows = read_windows(win_ref, tokens_ref.shape[0])
    if len(pieces) == 4:
        for ref, index in places(pieces):
            rows = part(index, depth)
            w_oth_ref[0, rows, :] = ref[0:depth, 0:half]
            w_oth_ref[1, rows, :] = ref[0:depth, half:]
            middle = depth + depth // 2
            w_oth_ref[2, part(index * 2, depth // 2), :] = ref[depth:middle, 0:half]
            w_oth_ref[2, part(index * 2 + 1, depth // 2), :] = ref[depth:middle, half:]
            out_oth_ref[part(index, depth // 2), :] = ref[middle : 2 * depth, :]
        for i in range(bias_oth_ref.shape[0] // width):
            bias_row = pieces[0][2 * depth + i : 2 * depth + i + 1, :].astype(F32)
            bias_oth_ref[i * width : (i + 1) * width] = bias_row.reshape(width)
    else:
        w_oth_ref[...] = pieces[0][...]
        out_oth_ref[...] = pieces[1][...]
        bias_oth_ref[...] = pieces[2][...].astype(F32)
    hidden_in = hidden_rows(tokens_ref, pos_ref, windows)
    attend_forward(
        hidden_in.astype(BF16), w_oth_ref, windows, mixed_ref, probs_ref, context_ref
    )
    branch = mm(context_own_ref[...], out_own_ref[...]) + mm(context_ref[...], out_oth_ref[...])
    hidden_in = hidden_rows(tokens_ref, pos_ref, windows)
    resid_ref[...] = hidden_in + branch + row(out_bias_ref)


def core_split(whole_ref, keep_ref, send_ref, start, split):
    half = whole_ref.shape[0] // 2
    core = place("core") if split else 0
    keep_ref[start : start + half, :] = whole_ref[part(core, half), :]
    send_ref[start : start + half, :] = whole_ref[part(1 - core, half), :]


def ffn_forward(low_ref, up_ref, bias_ref, act_ref, slope_ref):
    for start in range(0, up_ref.shape[1], CHUNK):
        cols = slice(start, start + CHUNK)
        pre = mm(low_ref[...], up_ref[:, cols]) + row(bias_ref, start, CHUNK)
        total, density = normal_parts(pre)
        act_ref[:, cols] = (pre * total).astype(BF16)
        slope_ref[:, cols] = (total + pre * density).astype(BF16)


def ffn_own_kernel(
    resid_ref,
    up_ref,
    down_ref,
    bias_ref,
    gain_ref,
    shift_ref,
    low_ref,
    act_ref,
    slope_ref,
    branch_ref,
):
    hat, _ = norm_stats(resid_ref[...])
    normed = hat * row(gain_ref) + row(shift_ref)
    low_ref[...] = normed.astype(BF16)
    ffn_forward(low_ref, up_ref, bias_ref, act_ref, slope_ref)
    branch_ref[...] = normed + mm(act_ref[...], down_ref[...])


def ffn_other_kernel(
    split,
    cot_ref,
    low_ref,
    act_own_ref,
    branch_ref,
    up_refs,
    down_refs,
    bias_ref,
    down_bias_ref,
    gain_ref,
    shift_ref,
    layer_ref,
    keep_ref,
    send_ref,
    slope_ref,
    up_ref,
    down_ref,
    grad_ref,
    vec_ref,
    act_ref,
    package_ref,
):
    width = cot_ref.shape[1]
    units = up_ref.shape[1]
    if len(up_refs) == 4:
        for ref, index in places(up_refs):
            depth = ref.shape[0] * width // units
            for i in range(units // width):
                up_ref[part(index, depth), i * width : (i + 1) * width] = ref[
                    i * depth : (i + 1) * depth, :
                ]
        for ref, index in places(down_refs):
            down_ref[part(index, ref.shape[0]), :] = ref[...]
    else:
        up_ref[...] = up_refs[0][...]
        down_ref[...] = down_refs[0][...]
    ffn_forward(low_ref, up_ref, bias_ref, act_ref, slope_ref)
    resid = branch_ref[...] + mm(act_ref[...], down_ref[...]) + row(down_bias_ref)
    hat, scale = norm_stats(resid)
    layer_ref[...] = (hat * row(gain_ref) + row(shift_ref)).astype(BF16)
    cot = cot_ref[...].astype(F32)
    vec_ref[1:2, :] = jnp.sum(cot * hat, axis=0, keepdims=True)
    vec_ref[2:3, :] = jnp.sum(cot, axis=0, keepdims=True)
    grad = norm_grad(cot * row(gain_ref), hat, scale)
    vec_ref[0:1, :] = jnp.sum(grad, axis=0, keepdims=True)
    grad_ref[...] = grad
    grad_low = grad.astype(BF16)
    for half, act in ((0, act_own_ref), (1, act_ref)):
        for start in range(0, units, CHUNK):
            cols = slice(start, start + CHUNK)
            package_ref[cols, :] = mm_tn(act[:, cols], grad_low).astype(BF16)
        core_split(package_ref, keep_ref, send_ref, half * (units // 2), split)


def ffn_back_kernel(
    split,
    resid_ref,
    grad_ref,
    low_ref,
    slopes,
    ups,
    downs,
    vec_ref,
    gain_ref,
    keep_ref,
    send_ref,
    small_ref,
    grad_resid_ref,
    work_ref,
    total_ref,
    package_ref,
    bias_sum_ref,
):
    width = resid_ref.shape[1]
    units = ups[0].shape[1]
    grad_low = grad_ref[...].astype(BF16)
    for half in range(2):
        for start in range(0, units, CHUNK):
            cols = slice(start, start + CHUNK)
            grad_act = mm_nt(grad_low, downs[half][cols, :])
            pre_grad = (grad_act * slopes[half][:, cols].astype(F32)).astype(BF16)
            work_ref[:, cols] = pre_grad
            at = half * (units // width) + start // width
            bias_sum_ref[at : at + 1, start % width : start % width + CHUNK] = jnp.sum(
                pre_grad.astype(F32), axis=0, keepdims=True
            )
        for start in range(0, units, width):
            cols = slice(start, start + width)
            package_ref[cols, :] = mm_tn(low_ref[...], work_ref[:, cols]).astype(BF16)
        core_split(package_ref, keep_ref, send_ref, half * (units // 2), split)
        before = grad_ref[...] if half == 0 else total_ref[...]
        total_ref[...] = before + mm_nt(work_ref[...], ups[half][...])
    grad = total_ref[...]
    hat, scale = norm_stats(resid_ref[...])
    small_ref[1:2, :] = jnp.sum(grad * hat, axis=0, keepdims=True)
    small_ref[2:3, :] = jnp.sum(grad, axis=0, keepdims=True)
    grad = norm_grad(grad * row(gain_ref), hat, scale)
    small_ref[0:1, :] = jnp.sum(grad, axis=0, keepdims=True)
    small_ref[3:6, :] = vec_ref[0:3, :]
    span = units // width
    first_half = (place("mp") if split else 0) == 0
    ours, theirs = bias_sum_ref[0:span, :], bias_sum_ref[span : 2 * span, :]
    small_ref[6 : 6 + span, :] = jnp.where(first_half, ours, theirs)
    small_ref[6 + span : 6 + 2 * span, :] = jnp.where(first_half, theirs, ours)
    used = 6 + 2 * span
    small_ref[used:, :] = jnp.zeros((small_ref.shape[0] - used, width), F32)
    keep_ref[units:, :] = small_ref[...].astype(BF16)
    send_ref[units:, :] = small_ref[...].astype(BF16)
    grad_resid_ref[...] = grad


def half_backward(
    split,
    hidden_low,
    grad_low,
    weight_ref,
    out_ref,
    mixed_ref,
    probs_ref,
    context_ref,
    keep_ref,
    send_ref,
    gm_ref,
    package_ref,
):
    rows, width = hidden_low.shape
    half_width = width // 2
    package_ref[width + half_width :, :] = mm_tn(context_ref[...], grad_low).astype(BF16)
    grad_context = mm_nt(grad_low, out_ref[...]).astype(BF16)
    attend_backward(grad_context, mixed_ref, probs_ref, rows // W_LONG, gm_ref)
    package_ref[0:width, 0:half_width] = mm_tn(hidden_low, gm_ref[0]).astype(BF16)
    package_ref[0:width, half_width:] = mm_tn(hidden_low, gm_ref[1]).astype(BF16)
    value_grad = mm_tn(hidden_low, gm_ref[2]).astype(BF16)
    package_ref[width : width + half_width, 0:half_width] = value_grad[0:half_width, :]
    package_ref[width : width + half_width, half_width:] = value_grad[half_width:, :]
    core_split(package_ref, keep_ref, send_ref, 0, split)
    return (
        mm_nt(gm_ref[0], weight_ref[0])
        + mm_nt(gm_ref[1], weight_ref[1])
        + mm_nt(gm_ref[2], weight_ref[2])
    )


def attend_back_kernel(
    split,
    win_ref,
    tokens_ref,
    pos_ref,
    grad_resid_ref,
    own_refs,
    other_refs,
    other_keep_ref,
    other_send_ref,
    own_keep_ref,
    own_send_ref,
    table_keep_ref,
    table_send_ref,
    tokens_grad_ref,
    grad_ref,
    gm_ref,
    package_ref,
    table_ref,
):
    rows, width = tokens_ref.shape
    windows = read_windows(win_ref, rows)
    hidden_low = hidden_rows(tokens_ref, pos_ref, windows).astype(BF16)
    grad_low = grad_resid_ref[...].astype(BF16)
    for before_ref, refs, to_refs in (
        (grad_resid_ref, other_refs, (other_keep_ref, other_send_ref)),
        (grad_ref, own_refs, (own_keep_ref, own_send_ref)),
    ):
        part_grad = half_backward(
            split, hidden_low, grad_low, *refs, *to_refs, gm_ref, package_ref
        )
        grad_ref[...] = before_ref[...] + part_grad
    grad = grad_ref[...]
    tokens_grad_ref[...] = grad.astype(BF16)
    first, second = None, None
    for block, is_long in enumerate(windows):
        top = grad[block * W_LONG : block * W_LONG + W_SHORT]
        bottom = grad[block * W_LONG + W_SHORT : (block + 1) * W_LONG]
        zero = jnp.zeros_like(top)
        part_first = top + jnp.where(is_long, zero, bottom)
        part_second = jnp.where(is_long, bottom, zero)
        first = part_first if first is None else first + part_first
        second = part_second if second is None else second + part_second
    table_ref[0:W_SHORT, :] = first.astype(BF16)
    table_ref[W_SHORT:, :] = second.astype(BF16)
    core_split(table_ref, table_keep_ref, table_send_ref, 0, split)


def total_of(*values):
    total = values[0].astype(F32)
    for value in values[1:]:
        total = total + value.astype(F32)
    return total


def bit_split(bit, value, work_ref, keep_ref, send_ref, start=0):
    half = value.shape[0] // 2
    work_ref[...] = value.astype(BF16)
    keep_ref[start : start + half, :] = work_ref[part(bit, half), :]
    send_ref[start : start + half, :] = work_ref[part(1 - bit, half), :]


def z_bit():
    return lax.rem(place("z"), 2)


def other_half_kernel(keep_ref, recv_ref, send_ref):
    start = keep_ref.shape[0] - send_ref.shape[0]
    send_ref[...] = total_of(keep_ref[start:, :], recv_ref[start:, :]).astype(BF16)


def down_split_kernel(keep_ref, recv_ref, from_y_ref, x_keep_ref, x_send_ref, work_ref):
    rows = from_y_ref.shape[0]
    total = total_of(keep_ref[0:rows, :], recv_ref[0:rows, :], from_y_ref[...])
    bit_split(place("x"), total, work_ref, x_keep_ref, x_send_ref)


def pair_kernel(a_ref, b_ref, out_ref):
    out_ref[...] = total_of(a_ref[...], b_ref[...]).astype(BF16)


def spread_kernel(parts_ref, out_ref):
    total = total_of(*[parts_ref[i] for i in range(parts_ref.shape[0])]).astype(BF16)
    for i in range(out_ref.shape[0]):
        out_ref[i] = total


def up_split_kernel(keep_ref, recv_ref, x_keep_ref, x_send_ref, work_ref):
    rows = work_ref.shape[0]
    for half in range(2):
        rows_of = slice(half * rows, (half + 1) * rows)
        total = total_of(keep_ref[rows_of, :], recv_ref[rows_of, :])
        start = half * (rows // 2)
        bit_split(place("x"), total, work_ref, x_keep_ref, x_send_ref, start)
    small = total_of(keep_ref[2 * rows :, :], recv_ref[2 * rows :, :]).astype(BF16)
    x_keep_ref[rows:, :] = small
    x_send_ref[rows:, :] = small


def down_x_kernel(keep_ref, recv_ref, z_keep_ref, z_send_ref, work_ref):
    bit_split(z_bit(), total_of(keep_ref[...], recv_ref[...]), work_ref, z_keep_ref, z_send_ref)


def up_x_kernel(keep_ref, recv_ref, z_keep_ref, z_send_ref, work_ref):
    rows = work_ref.shape[0]
    for half in range(2):
        rows_of = slice(half * rows, (half + 1) * rows)
        total = total_of(keep_ref[rows_of, :], recv_ref[rows_of, :])
        bit_split(z_bit(), total, work_ref, z_keep_ref, z_send_ref, half * (rows // 2))
    small = total_of(keep_ref[2 * rows :, :], recv_ref[2 * rows :, :]).astype(BF16)
    z_keep_ref[rows:, :] = small
    z_send_ref[rows:, :] = small


def up_z_kernel(keep_ref, recv_ref, y_keep_ref, y_send_ref):
    rows = y_keep_ref.shape[0] - EXTRA
    y_keep_ref[0:rows, :] = total_of(keep_ref[0:rows, :], recv_ref[0:rows, :]).astype(BF16)
    y_send_ref[...] = total_of(keep_ref[rows:, :], recv_ref[rows:, :]).astype(BF16)
    y_keep_ref[rows:, :] = y_send_ref[rows:, :]


def up_last_kernel(own_ref, recv_ref, out_ref, *small_refs):
    *vector_refs, bias_ref, work_ref = small_refs
    rows, width = out_ref.shape
    out_ref[...] = total_of(own_ref[0:rows, :], recv_ref[0:rows, :]).astype(BF16)
    work_ref[...] = total_of(own_ref[rows:, :], recv_ref[rows:, :])
    for i, ref in enumerate(vector_refs):
        ref[...] = work_ref[i : i + 1, :].reshape(width)
    span = bias_ref.shape[0] // width
    for i in range(span):
        value = work_ref[pl.ds(6 + place("mp") * span + i, 1), :]
        bias_ref[i * width : (i + 1) * width] = value.reshape(width)


def join_kernel(own_ref, recv_ref, out_ref):
    rows = own_ref.shape[0]
    out_ref[part(z_bit(), rows), :] = own_ref[...]
    out_ref[part(1 - z_bit(), rows), :] = recv_ref[...]


def attend_core_kernel(
    keep_ref, recv_ref, table_keep_ref, table_recv_ref, to_y_ref, table_ref, work_ref
):
    rows = keep_ref.shape[0]
    to_y_ref[0:rows, :] = total_of(keep_ref[...], recv_ref[...]).astype(BF16)
    total = total_of(table_keep_ref[...], table_recv_ref[...])
    bit_split(place("mp"), total, work_ref, table_ref, to_y_ref.at[rows:, :])


def attend_pieces_kernel(keep_ref, recv_ref, from_y_ref, table_ref, out_ref):
    devices, rows, _ = out_ref.shape
    size = keep_ref.shape[0]
    piece = size // devices
    spare = rows - piece
    for i in range(devices):
        rows_of = slice(i * piece, (i + 1) * piece)
        out_ref[i, 0:piece, :] = total_of(
            keep_ref[rows_of, :], recv_ref[rows_of, :], from_y_ref[rows_of, :]
        ).astype(BF16)
        rows_of = slice(i * spare, (i + 1) * spare)
        other = from_y_ref[size + i * spare : size + (i + 1) * spare, :]
        out_ref[i, piece:, :] = total_of(table_ref[rows_of, :], other).astype(BF16)


def spread_kernel(parts_ref, out_ref):
    total = total_of(*[parts_ref[i] for i in range(parts_ref.shape[0])]).astype(BF16)
    for i in range(out_ref.shape[0]):
        out_ref[i] = total


def cut_kernel(parts_ref, out_ref):
    devices, rows, _ = parts_ref.shape
    size = out_ref.shape[0] // devices
    for i in range(devices):
        out_ref[i * size : (i + 1) * size, :] = parts_ref[i, rows - size :, :]


def down_out_kernel(own_ref, from_x_ref, core_own_ref, core_x_ref, out_ref):
    x, core = place("x"), place("core")
    rows = own_ref.shape[0]
    for ref, at_x, at_core in (
        (own_ref, x, core),
        (from_x_ref, 1 - x, core),
        (core_own_ref, x, 1 - core),
        (core_x_ref, 1 - x, 1 - core),
    ):
        start = pl.multiple_of((at_core * 2 + at_x) * rows, rows)
        out_ref[pl.ds(start, rows), :] = ref[...].astype(F32)


def up_out_kernel(own_ref, from_x_ref, core_own_ref, core_x_ref, out_ref):
    x, core = place("x"), place("core")
    rows, width = own_ref.shape
    for index in range(2):
        cols = slice(index * width, (index + 1) * width)
        mine = core == index
        for a_ref, b_ref, at_x in ((own_ref, core_own_ref, x), (from_x_ref, core_x_ref, 1 - x)):
            start = pl.multiple_of(at_x * rows, rows)
            out_ref[pl.ds(start, rows), cols] = jnp.where(
                mine, a_ref[...].astype(F32), b_ref[...].astype(F32)
            )


def attend_out_kernel(own_ref, recv_ref, qkv_ref, out_ref):
    first_core = place("core") == 0
    devices, rows, width = own_ref.shape
    half = width // 2
    piece = width // devices
    for i in range(devices):
        ours, theirs = own_ref[i, 0:piece].astype(F32), recv_ref[i, 0:piece].astype(F32)
        low = jnp.where(first_core, ours, theirs)
        high = jnp.where(first_core, theirs, ours)
        rows_of = slice(i * piece, (i + 1) * piece)
        qkv_ref[0, rows_of, :] = low[:, 0:half]
        qkv_ref[1, rows_of, :] = low[:, half:]
        if i < devices // 2:
            qkv_ref[2, rows_of, :] = high[:, 0:half]
            qkv_ref[2, half + i * piece : half + (i + 1) * piece, :] = high[:, half:]
        else:
            out_ref[(i - devices // 2) * piece : (i - devices // 2 + 1) * piece, :] = high


def table_out_kernel(own_ref, from_y_ref, core_own_ref, core_y_ref, out_ref):
    y, core = place("mp"), place("core")
    rows = own_ref.shape[0]
    for ref, at_y, at_core in (
        (own_ref, y, core),
        (from_y_ref, 1 - y, core),
        (core_own_ref, y, 1 - core),
        (core_y_ref, 1 - y, 1 - core),
    ):
        out_ref[part(at_core * 2 + at_y, rows), :] = ref[...].astype(F32)


def swap(value, axis, name="swap", distance=1):
    pairs = [(i, i ^ distance) for i in range(lax.axis_size(axis))]
    with jax.named_scope(f"{name}_{axis}{distance}"):
        return lax.ppermute(value, axis, pairs)


def exchange(value, axes, name="exchange"):
    with jax.named_scope(name):
        return lax.all_to_all(value, axes, 0, 0, tiled=True)


class Chain:
    def __init__(self):
        self.last = ()

    def gate(self, value):
        value = pl.pallas_call(
            lambda *refs: None,
            out_shape=jax.ShapeDtypeStruct(value.shape, value.dtype),
            in_specs=[anywhere] * (1 + len(self.last)),
            out_specs=anywhere,
            input_output_aliases={0: 0},
            compiler_params=pltpu.CompilerParams(vmem_limit_bytes=MIB),
            cost_estimate=pl.CostEstimate(
                flops=FLOPS_PER_US, bytes_accessed=0, transcendentals=0
            ),
            name="gate",
        )(value, *self.last)
        self.last = (value,)
        return value

    def __call__(self, kernel, outs, args, us, name, scratch=(), smem_args=0):
        mib = 28 if us > 2 else 8
        results = call(kernel, outs, args, self.last, scratch, us, mib, smem_args, name)
        self.last = (min(results, key=lambda value: value.size),)
        return results


def per_device(
    fast,
    mp_size,
    tokens,
    pos_table,
    qkv_weight,
    out_weight,
    out_bias,
    norm1_gain,
    norm1_shift,
    up_weight,
    up_bias,
    down_weight,
    down_bias,
    norm2_gain,
    norm2_shift,
    window,
    cotangent,
):
    step = Chain()
    rows, width = tokens.shape
    blocks = rows // W_LONG
    half_width = width // 2
    units = up_weight.shape[1] * mp_size // 2
    n, spare = width, W_LONG // 2
    qkv_weight = jnp.transpose(qkv_weight, (1, 0, 2))
    wide = ((rows, width), F32)

    attend_outs = [
        (3, rows, half_width),
        (blocks * half_width // HD * 3, W_SHORT, W_SHORT),
        (rows, half_width),
    ]

    def attend_own():
        return step(
            first_kernel,
            attend_outs,
            [window, tokens, pos_table, w_own],
            3,
            "attend_first",
            smem_args=1,
        )

    def attend_other():
        return step(
            second_kernel,
            attend_outs
            + [wide, (3, width, half_width), (half_width, width), ((units,), F32)],
            [window, tokens, pos_table, attend_in, context_own, out_own, out_bias],
            5,
            "attend_second",
            smem_args=1,
        )

    def ffn_own():
        return step(
            ffn_own_kernel,
            [(rows, width), (rows, units), (rows, units), wide],
            [resid, up_own, down_own, bias_own, norm1_gain, norm1_shift],
            4,
            "ffn_own",
        )

    if fast:
        w_own, out_own, up_own, down_own = qkv_weight, out_weight, up_weight, down_weight
        bias_own = up_bias
        (message,) = step(
            pack_attend_kernel,
            [(width // 2 + EXTRA, width)],
            [qkv_weight, out_weight, up_bias],
            1,
            "pack_attend",
        )
        attend_y = swap(message, "mp", "attend_y")
        up_message, down_message = step(
            pack_ffn_kernel,
            [(units // 4, width), (units // 4, width)],
            [up_weight, down_weight],
            1,
            "pack_ffn",
        )
        up_y = swap(up_message, "mp", "up_y")
        down_y = swap(down_message, "mp", "down_y")
        attend_y = step.gate(attend_y)
        attend_x = swap(attend_y, "x", "attend_x")
        attend_cy = swap(attend_y, "core", "attend_cy")
        mixed_own, probs_own, context_own = attend_own()
        up_y = step.gate(up_y)
        up_x = swap(up_y, "x", "up_x")
        up_cy = swap(up_y, "core", "up_cy")
        attend_x = step.gate(attend_x)
        attend_cx = swap(attend_x, "core", "attend_cx")
        down_y = step.gate(down_y)
        down_x = swap(down_y, "x", "down_x")
        down_cy = swap(down_y, "core", "down_cy")
        attend_in = (attend_y, attend_x, attend_cy, attend_cx)
        mixed_oth, probs_oth, context_oth, resid, w_oth, out_oth, bias_oth = attend_other()
        up_x = step.gate(up_x)
        up_cx = swap(up_x, "core", "up_cx")
        low, act_own, slope_own, branch = ffn_own()
        down_x = step.gate(down_x)
        down_cx = swap(down_x, "core", "down_cx")
        up_in = (up_y, up_x, up_cy, up_cx)
        down_in = (down_y, down_x, down_cy, down_cx)
    else:
        qkv = lax.all_gather(qkv_weight, "mp", axis=2, tiled=True)
        out_w = lax.all_gather(out_weight, "mp", axis=0, tiled=True)
        up_w = lax.all_gather(up_weight, "mp", axis=1, tiled=True)
        bias = lax.all_gather(up_bias, "mp", axis=0, tiled=True)
        down_w = lax.all_gather(down_weight, "mp", axis=0, tiled=True)
        w_own, out_own = qkv[:, :, :half_width], out_w[:half_width]
        attend_in = (qkv[:, :, half_width:], out_w[half_width:], bias[units:])
        up_own, up_in = up_w[:, :units], (up_w[:, units:],)
        down_own, down_in = down_w[:units], (down_w[units:],)
        bias_own = bias[:units]
        mixed_own, probs_own, context_own = attend_own()
        mixed_oth, probs_oth, context_oth, resid, w_oth, out_oth, bias_oth = attend_other()
        low, act_own, slope_own, branch = ffn_own()

    layer_out, down_keep, down_send, slope_oth, up_oth, down_oth, grad2, vec = step(
        functools.partial(ffn_other_kernel, fast),
        [
            (rows, width),
            (units, width),
            (units, width),
            (rows, units),
            (width, units),
            (units, width),
            wide,
            ((8, width), F32),
        ],
        [
            cotangent,
            low,
            act_own,
            branch,
            up_in,
            down_in,
            bias_oth,
            down_bias,
            norm2_gain,
            norm2_shift,
        ],
        6,
        "ffn_other",
        scratch=[((rows, units), BF16), ((units, width), BF16)],
    )
    down_recv = swap(down_send, "core", "down_recv") if fast else None
    up_keep, up_send, small, grad1 = step(
        functools.partial(ffn_back_kernel, fast),
        [
            (units + EXTRA, width),
            (units + EXTRA, width),
            ((EXTRA, width), F32),
            wide,
        ],
        [
            resid,
            grad2,
            low,
            (slope_own, slope_oth),
            (up_own, up_oth),
            (down_own, down_oth),
            vec,
            norm1_gain,
        ],
        6,
        "ffn_back",
        scratch=[
            ((rows, units), BF16),
            ((rows, width), F32),
            ((units, width), BF16),
            ((8, width), F32),
        ],
    )

    def attend_back():
        return step(
            functools.partial(attend_back_kernel, fast),
            [(n, width)] * 4 + [(spare, width)] * 2 + [(rows, width)],
            [
                window,
                tokens,
                pos_table,
                grad1,
                (w_own, out_own, mixed_own, probs_own, context_own),
                (w_oth, out_oth, mixed_oth, probs_oth, context_oth),
            ],
            13,
            "attend_back",
            scratch=[
                ((rows, width), F32),
                ((3, rows, half_width), BF16),
                ((2 * n, width), BF16),
                ((W_LONG, width), BF16),
            ],
            smem_args=1,
        )

    if not fast:
        *att_parts, grad_tokens = attend_back()
        qkv_g, out_g, up_g, down_g, small, table = reduce_plain(
            n, width, down_keep, down_send, up_keep, up_send, small, *att_parts
        )
        vectors = [small[i] for i in range(6)]
        bias_all = small[6 : 6 + 2 * units // width].reshape(-1)
        start = lax.axis_index("mp") * up_bias.shape[0]
        bias_g = lax.dynamic_slice_in_dim(bias_all, start, up_bias.shape[0])
    else:
        zx = lax.axis_size("z") * lax.axis_size("x")
        half, piece, strip = n // 2, n // 4, spare // 2
        up_recv = swap(up_send, "core", "up_recv")
        (to_y,) = step(other_half_kernel, [(n, width)], [down_keep, down_recv], 1, "down_core")
        down_from_y = swap(to_y, "mp", "down_from_y")
        up_x, to_x = step(
            up_split_kernel,
            [(n + EXTRA, width)] * 2,
            [up_keep, up_recv],
            2,
            "up_core",
            scratch=[((n, width), BF16)],
        )
        up_from_x = swap(to_x, "x", "up_from_x")
        oth_keep, oth_send, own_keep, own_send, tab_keep, tab_send, grad_tokens = attend_back()
        oth_recv = swap(oth_send, "core", "oth_recv")
        tab_recv = swap(tab_send, "core", "tab_recv")
        own_recv = swap(own_send, "core", "own_recv")
        down_x, to_x = step(
            down_split_kernel,
            [(half, width)] * 2,
            [down_keep, down_recv, down_from_y],
            1,
            "down_mp",
            scratch=[((n, width), BF16)],
        )
        down_from_x = swap(to_x, "x", "down_from_x")
        up_z, to_z = step(
            up_x_kernel,
            [(half + EXTRA, width)] * 2,
            [up_x, up_from_x],
            1,
            "up_x",
            scratch=[((half, width), BF16)],
        )
        up_from_z = swap(to_z, "z", "up_from_z")
        to_y, table = step(
            attend_core_kernel,
            [(n + strip, width), (strip, width)],
            [oth_keep, oth_recv, tab_keep, tab_recv],
            1,
            "attend_core",
            scratch=[((spare, width), BF16)],
        )
        att_from_y = swap(to_y, "mp", "att_from_y")
        down_z, to_z = step(
            down_x_kernel,
            [(piece, width)] * 2,
            [down_x, down_from_x],
            1,
            "down_x",
            scratch=[((half, width), BF16)],
        )
        down_from_z = swap(to_z, "z", "down_from_z")
        up_y, to_y = step(
            up_z_kernel, [(piece + EXTRA, width)] * 2, [up_z, up_from_z], 1, "up_z"
        )
        up_from_y = swap(to_y, "mp", "up_from_y")
        (down_z,) = step(pair_kernel, [(piece, width)], [down_z, down_from_z], 1, "down_z")
        down_far = swap(down_z, "z", "down_far", 2)
        (att,) = step(
            attend_pieces_kernel,
            [(zx, (n + strip) // zx, width)],
            [own_keep, own_recv, att_from_y, table],
            1,
            "attend_mp",
        )
        att = exchange(att, ("z", "x"), "att_parts")
        (up_y,) = step(pair_kernel, [(piece + EXTRA, width)], [up_y, up_from_y], 1, "up_mp")
        up_far = swap(up_y, "z", "up_far", 2)
        (down_z,) = step(pair_kernel, [(piece, width)], [down_z, down_far], 1, "down_far")
        down_near = swap(down_z, "z", "down_near")
        (down_z,) = step(join_kernel, [(half, width)], [down_z, down_near], 1, "down_join")
        down_x = swap(down_z, "x", "down_x")
        up_z, *vectors, bias_g = step(
            up_last_kernel,
            [(piece, width)] + [((width,), F32)] * 6 + [((up_bias.shape[0],), F32)],
            [up_y, up_far],
            1,
            "up_far",
            scratch=[((EXTRA, width), F32)],
        )
        up_near = swap(up_z, "z", "up_near")
        (att,) = step(spread_kernel, [att.shape], [att], 1, "attend_sum")
        att = exchange(att, ("z", "x"), "att_sums")
        (up_z,) = step(join_kernel, [(half, width)], [up_z, up_near], 1, "up_join")
        up_x = swap(up_z, "x", "up_x")
        down_x = step.gate(down_x)
        (down_g,) = step(
            down_out_kernel,
            [((2 * n, width), F32)],
            [
                down_z,
                down_x,
                swap(down_z, "core", "down_core"),
                swap(down_x, "core", "down_core_x"),
            ],
            2,
            "down_out",
        )
        up_x = step.gate(up_x)
        (up_g,) = step(
            up_out_kernel,
            [((width, 2 * n), F32)],
            [up_z, up_x, swap(up_z, "core", "up_core"), swap(up_x, "core", "up_core_x")],
            2,
            "up_out",
        )
        (table,) = step(cut_kernel, [(strip, width)], [att], 1, "table_cut")
        table_y = swap(table, "mp", "table_y")
        qkv_g, out_g = step(
            attend_out_kernel,
            [((3, width, half_width), F32), ((half_width, width), F32)],
            [att, swap(att, "core", "att_core")],
            2,
            "attend_out",
        )
        (table,) = step(
            table_out_kernel,
            [((W_LONG, width), F32)],
            [
                table,
                table_y,
                swap(table, "core", "table_core"),
                swap(table_y, "core", "table_core_y"),
            ],
            1,
            "table_out",
        )
    return (
        layer_out,
        grad_tokens,
        table,
        jnp.transpose(qkv_g, (1, 0, 2)),
        out_g,
        vectors[0],
        vectors[1],
        vectors[2],
        up_g,
        bias_g,
        down_g,
        vectors[3],
        vectors[4],
        vectors[5],
    )


def reduce_plain(
    n,
    width,
    down_keep,
    down_send,
    up_keep,
    up_send,
    small,
    other_keep,
    other_send,
    own_keep,
    own_send,
    table_keep,
    table_send,
):
    def halves(keep, send):
        first = jnp.concatenate([keep[:n], send[:n]], axis=0)
        second = jnp.concatenate([keep[n : 2 * n], send[n : 2 * n]], axis=0)
        return first, second

    def summed(own, oth, make, dim):
        whole = jnp.concatenate([make(own), make(oth)], axis=dim)
        part = lax.psum_scatter(whole, "mp", scatter_dimension=dim, tiled=True)
        return lax.psum(part, "dp").astype(F32)

    def qkv_part(g):
        value = jnp.concatenate(
            [g[n : n + n // 2, : n // 2], g[n : n + n // 2, n // 2 :]], axis=0
        )
        return jnp.stack([g[:n, : n // 2], g[:n, n // 2 :], value])

    def up_part(g):
        return jnp.concatenate([g[s : s + n] for s in range(0, g.shape[0], n)], axis=1)

    att_oth = jnp.concatenate([other_keep, other_send], axis=0)
    att_own = jnp.concatenate([own_keep, own_send], axis=0)
    up_own, up_oth = halves(up_keep, up_send)
    down_own, down_oth = halves(down_keep, down_send)
    table = jnp.concatenate([table_keep, table_send], axis=0).astype(F32)
    return (
        summed(att_own, att_oth, qkv_part, 2),
        summed(att_own, att_oth, lambda g: g[n + n // 2 :], 0),
        summed(up_own, up_oth, up_part, 1),
        summed(down_own, down_oth, lambda g: g, 0),
        lax.psum(small, ("dp", "mp")),
        lax.psum(table, ("dp", "mp")),
    )


def solution(mesh):
    mp_size = mesh.shape["mp"]
    fast = mp_size == 2 and mesh.shape["dp"] == 16
    dp = "dp"
    if fast:
        shape = (mesh.shape["dp"] // 4, 2, 2, mp_size)
        mesh = Mesh(mesh.devices.reshape(shape), ("z", "x", "core", "mp"))
        dp = ("z", "x", "core")
    both = P((*dp, "mp") if fast else (dp, "mp"), None)
    placed = (
        both,
        P(),
        P(None, None, "mp"),
        P("mp", None),
        P(),
        P(),
        P(),
        P(None, "mp"),
        P("mp"),
        P("mp", None),
        P(),
        P(),
        P(),
        P(dp),
        both,
    )
    return jax.shard_map(
        functools.partial(per_device, fast, mp_size),
        mesh=mesh,
        in_specs=placed,
        out_specs=(
            both,
            both,
            P(),
            P(None, None, "mp"),
            P("mp", None),
            P(),
            P(),
            P(),
            P(None, "mp"),
            P("mp"),
            P("mp", None),
            P(),
            P(),
            P(),
        ),
        check_vma=False,
    )
```

```python
import functools

import jax
import jax.numpy as jnp
from jax import lax
from jax.experimental import pallas as pl
from jax.experimental.pallas import tpu as pltpu
from jax.sharding import Mesh
from jax.sharding import PartitionSpec as P

HD = 64
W_SHORT = 256
W_LONG = 512
ROW = 1024
LANES = 128
EXTRA = 16
CHUNK = 256
EPSILON = 1e-05
MASKED = -1e30
F32 = jnp.float32
BF16 = jnp.bfloat16
MIB = 1024 * 1024
FLOPS_PER_US = 10**9

vmem = pl.BlockSpec(memory_space=pltpu.VMEM)
smem = pl.BlockSpec(memory_space=pltpu.SMEM)
anywhere = pl.BlockSpec(memory_space=pl.ANY)


def call(
    kernel, outs, args, after=(), scratch=(), us=1, mib=32, smem_args=0, hbm_args=0, copies=0, name=None
):
    flat, tree = jax.tree.flatten(tuple(args))
    count, extra = len(flat), len(after)

    def flat_kernel(*refs):
        kernel(*jax.tree.unflatten(tree, refs[:count]), *refs[count + extra :])

    return pl.pallas_call(
        flat_kernel,
        out_shape=[
            jax.ShapeDtypeStruct(out, BF16) if isinstance(out[0], int) else jax.ShapeDtypeStruct(*out)
            for out in outs
        ],
        in_specs=[smem] * smem_args
        + [vmem] * (count - smem_args - hbm_args)
        + [anywhere] * (hbm_args + extra),
        out_specs=[vmem] * len(outs),
        scratch_shapes=[pltpu.VMEM(shape, dtype) for shape, dtype in scratch]
        + [pltpu.SemaphoreType.DMA((copies,))] * (copies > 0),
        compiler_params=pltpu.CompilerParams(vmem_limit_bytes=mib * MIB),
        cost_estimate=pl.CostEstimate(
            flops=us * FLOPS_PER_US, bytes_accessed=0, transcendentals=0
        ),
        name=name,
    )(*flat, *after)


def place(axis):
    return lax.axis_index(axis)


def row(ref, start=0, size=None):
    size = ref.shape[0] if size is None else size
    return ref[start : start + size].astype(F32).reshape(1, size)


def mm(a, b):
    return lax.dot_general(a, b, (((1,), (0,)), ((), ())), preferred_element_type=F32)


def mm_nt(a, b):
    return lax.dot_general(a, b, (((1,), (1,)), ((), ())), preferred_element_type=F32)


def mm_tn(a, b):
    return lax.dot_general(a, b, (((0,), (0,)), ((), ())), preferred_element_type=F32)


def position_rows(pos_ref, is_long):
    first = pos_ref[0:W_SHORT, :].astype(F32)
    second = jnp.where(is_long, pos_ref[W_SHORT:W_LONG, :].astype(F32), first)
    return first, second


def hidden_rows(tokens_ref, pos_ref, windows):
    parts = []
    for block, is_long in enumerate(windows):
        first, second = position_rows(pos_ref, is_long)
        start = block * W_LONG
        parts.append(tokens_ref[start : start + W_SHORT, :].astype(F32) + first)
        parts.append(tokens_ref[start + W_SHORT : start + W_LONG, :].astype(F32) + second)
    return jnp.concatenate(parts, axis=0)


def read_windows(win_ref, rows):
    first = place("mp") * rows
    return [
        win_ref[lax.div(first + block * W_LONG, ROW)] == W_LONG for block in range(rows // W_LONG)
    ]


def norm_stats(values):
    average = jnp.mean(values, axis=-1, keepdims=True)
    centred = values - average
    variance = jnp.mean(centred * centred, axis=-1, keepdims=True)
    scale = lax.rsqrt(variance + EPSILON)
    return centred * scale, scale


def norm_grad(grad_hat, hat, scale):
    mean_grad = jnp.mean(grad_hat, axis=-1, keepdims=True)
    mean_both = jnp.mean(grad_hat * hat, axis=-1, keepdims=True)
    return scale * (grad_hat - mean_grad - hat * mean_both)


def head_mask(rows):
    return lax.broadcasted_iota(jnp.int32, (rows, LANES), 1) < HD


def own_head(value, is_low, head):
    zero = jnp.zeros_like(value)
    return jnp.where(is_low, value, zero) if head == 0 else jnp.where(is_low, zero, value)


def attend_forward(hidden_low, weight_ref, windows, mixed_ref, probs_ref, context_ref):
    rows, width = context_ref.shape
    for c in range(3):
        part = mm(hidden_low, weight_ref[c]).astype(BF16)
        mixed_ref[c] = part * BF16(HD**-0.5) if c == 0 else part
    causal = lax.broadcasted_iota(jnp.int32, (W_SHORT, W_SHORT), 0) >= lax.broadcasted_iota(
        jnp.int32, (W_SHORT, W_SHORT), 1
    )
    is_low = head_mask(W_SHORT)
    for block, is_long in enumerate(windows):
        lo = slice(block * W_LONG, block * W_LONG + W_SHORT)
        hi = slice(block * W_LONG + W_SHORT, (block + 1) * W_LONG)
        for pair in range(width // LANES):
            lanes = slice(pair * LANES, (pair + 1) * LANES)
            key_lo, key_hi = mixed_ref[1, lo, lanes], mixed_ref[1, hi, lanes]
            val_lo, val_hi = mixed_ref[2, lo, lanes], mixed_ref[2, hi, lanes]
            query_lo, query_hi = mixed_ref[0, lo, lanes], mixed_ref[0, hi, lanes]
            results = []
            for head in range(2):
                slot = ((block * (width // LANES) + pair) * 2 + head) * 3
                q_lo = own_head(query_lo, is_low, head)
                q_hi = own_head(query_hi, is_low, head)
                s_a = jnp.where(causal, mm_nt(q_lo, key_lo), MASKED)
                e_a = jnp.exp(s_a - jnp.max(s_a, axis=-1, keepdims=True))
                p_a = (e_a * (1.0 / jnp.sum(e_a, axis=-1, keepdims=True))).astype(BF16)
                s_b = jnp.where(is_long, mm_nt(q_hi, key_lo), MASKED)
                s_c = jnp.where(causal, mm_nt(q_hi, key_hi), MASKED)
                top = jnp.max(jnp.maximum(s_b, s_c), axis=-1, keepdims=True)
                e_b = jnp.exp(s_b - top)
                e_c = jnp.exp(s_c - top)
                inverse = 1.0 / jnp.sum(e_b + e_c, axis=-1, keepdims=True)
                p_b = (e_b * inverse).astype(BF16)
                p_c = (e_c * inverse).astype(BF16)
                probs_ref[slot] = p_a
                probs_ref[slot + 1] = p_b
                probs_ref[slot + 2] = p_c
                results.append((mm(p_a, val_lo), mm(p_b, val_lo) + mm(p_c, val_hi)))
            context_ref[lo, lanes] = jnp.where(is_low, results[0][0], results[1][0]).astype(BF16)
            context_ref[hi, lanes] = jnp.where(is_low, results[0][1], results[1][1]).astype(BF16)


def attend_backward(grad_context, mixed_ref, probs_ref, blocks, grad_mixed_ref):
    width = mixed_ref.shape[2]
    is_low = head_mask(W_SHORT)
    for block in range(blocks):
        lo = slice(block * W_LONG, block * W_LONG + W_SHORT)
        hi = slice(block * W_LONG + W_SHORT, (block + 1) * W_LONG)
        for pair in range(width // LANES):
            lanes = slice(pair * LANES, (pair + 1) * LANES)
            q_lo, q_hi = mixed_ref[0, lo, lanes], mixed_ref[0, hi, lanes]
            k_lo, k_hi = mixed_ref[1, lo, lanes], mixed_ref[1, hi, lanes]
            v_lo, v_hi = mixed_ref[2, lo, lanes], mixed_ref[2, hi, lanes]
            g_lo, g_hi = grad_context[lo, lanes], grad_context[hi, lanes]
            results = []
            for head in range(2):
                slot = ((block * (width // LANES) + pair) * 2 + head) * 3
                gm_lo = own_head(g_lo, is_low, head)
                gm_hi = own_head(g_hi, is_low, head)
                pb_a, pb_b, pb_c = probs_ref[slot], probs_ref[slot + 1], probs_ref[slot + 2]
                p_a, p_b, p_c = pb_a.astype(F32), pb_b.astype(F32), pb_c.astype(F32)
                g_a = mm_nt(gm_lo, v_lo)
                g_b = mm_nt(gm_hi, v_lo)
                g_c = mm_nt(gm_hi, v_hi)
                inner_a = jnp.sum(p_a * g_a, axis=-1, keepdims=True)
                inner_b = jnp.sum(p_b * g_b + p_c * g_c, axis=-1, keepdims=True)
                s_a = (p_a * (g_a - inner_a)).astype(BF16)
                s_b = (p_b * (g_b - inner_b)).astype(BF16)
                s_c = (p_c * (g_c - inner_b)).astype(BF16)
                results.append(
                    (
                        mm(s_a, k_lo),
                        mm(s_b, k_lo) + mm(s_c, k_hi),
                        mm_tn(s_a, q_lo) + mm_tn(s_b, q_hi),
                        mm_tn(s_c, q_hi),
                        mm_tn(pb_a, g_lo) + mm_tn(pb_b, g_hi),
                        mm_tn(pb_c, g_hi),
                    )
                )
            both = [jnp.where(is_low, a, b) for a, b in zip(*results)]
            grad_mixed_ref[0, lo, lanes] = (both[0] * HD**-0.5).astype(BF16)
            grad_mixed_ref[0, hi, lanes] = (both[1] * HD**-0.5).astype(BF16)
            grad_mixed_ref[1, lo, lanes] = both[2].astype(BF16)
            grad_mixed_ref[1, hi, lanes] = both[3].astype(BF16)
            grad_mixed_ref[2, lo, lanes] = both[4].astype(BF16)
            grad_mixed_ref[2, hi, lanes] = both[5].astype(BF16)


def normal_parts(x):
    density = jnp.exp(x * x * -0.5)
    t = 1.0 / (1.0 + jnp.abs(x) * 0.23164189)
    poly = t * (
        0.127414796
        + t * (-0.142248368 + t * (0.7107068705 + t * (-0.7265760135 + t * 0.5307027145)))
    )
    tail = poly * density
    return jnp.where(x > 0, 1.0 - tail, tail), density * 0.3989422804


def first_kernel(win_ref, tokens_ref, pos_ref, weight_ref, mixed_ref, probs_ref, context_ref):
    windows = read_windows(win_ref, tokens_ref.shape[0])
    hidden_low = hidden_rows(tokens_ref, pos_ref, windows).astype(BF16)
    attend_forward(hidden_low, weight_ref, windows, mixed_ref, probs_ref, context_ref)


def z_bit():
    return lax.rem(place("z"), 2)


def quarter(bit):
    return place("core") * 2 + bit


def part(index, size):
    return pl.ds(pl.multiple_of(index * size, size), size)


def copy_all(pairs, sems):
    copies = [
        pltpu.make_async_copy(src, dst, sems.at[i]) for i, (src, dst) in enumerate(pairs)
    ]
    for copy in copies:
        copy.start()
    for copy in copies:
        copy.wait()


def pack_attend_kernel(bias_ref, qkv_ref, out_ref, send_ref, sems):
    _, width, half = qkv_ref.shape
    depth, mine = width // 4, quarter(place("x"))
    for i in range(EXTRA):
        index = i if (i + 1) * width <= bias_ref.shape[0] else 0
        send_ref[2 * depth + i : 2 * depth + i + 1, :] = row(bias_ref, index * width, width).astype(
            BF16
        )
    middle = depth + depth // 2
    low, high = pl.ds(0, half), pl.ds(half, half)
    upper, lower = part(mine * 2, depth // 2), part(mine * 2 + 1, depth // 2)
    copy_all(
        [
            (qkv_ref.at[0, part(mine, depth), :], send_ref.at[pl.ds(0, depth), low]),
            (qkv_ref.at[1, part(mine, depth), :], send_ref.at[pl.ds(0, depth), high]),
            (qkv_ref.at[2, upper, :], send_ref.at[pl.ds(depth, depth // 2), low]),
            (qkv_ref.at[2, lower, :], send_ref.at[pl.ds(depth, depth // 2), high]),
            (out_ref.at[part(mine, depth // 2), :], send_ref.at[pl.ds(middle, depth // 2), :]),
        ],
        sems,
    )


def pack_ffn_kernel(up_ref, down_ref, up_to, down_to, sems):
    width, units = up_ref.shape
    depth, mine = width // 4, quarter(place("x"))
    columns = [
        (up_ref.at[part(mine, depth), pl.ds(i * width, width)], up_to.at[pl.ds(i * depth, depth), :])
        for i in range(units // width)
    ]
    copy_all([*columns, (down_ref.at[part(quarter(z_bit()), units // 4), :], down_to)], sems)


def places(pieces, bit):
    from_y, from_near, core_y, core_near = pieces
    core = place("core")
    return (
        (from_y, core * 2 + bit),
        (from_near, core * 2 + 1 - bit),
        (core_y, (1 - core) * 2 + bit),
        (core_near, (1 - core) * 2 + 1 - bit),
    )


def second_kernel(
    win_ref,
    tokens_ref,
    pos_ref,
    pieces,
    context_own_ref,
    out_own_ref,
    out_bias_ref,
    mixed_ref,
    probs_ref,
    context_ref,
    resid_ref,
    w_oth_ref,
    out_oth_ref,
    bias_oth_ref,
):
    width = tokens_ref.shape[1]
    half, depth = width // 2, width // 4
    windows = read_windows(win_ref, tokens_ref.shape[0])
    if len(pieces) == 4:
        for ref, index in places(pieces, place("x")):
            rows = part(index, depth)
            w_oth_ref[0, rows, :] = ref[0:depth, 0:half]
            w_oth_ref[1, rows, :] = ref[0:depth, half:]
            middle = depth + depth // 2
            w_oth_ref[2, part(index * 2, depth // 2), :] = ref[depth:middle, 0:half]
            w_oth_ref[2, part(index * 2 + 1, depth // 2), :] = ref[depth:middle, half:]
            out_oth_ref[part(index, depth // 2), :] = ref[middle : 2 * depth, :]
        for i in range(bias_oth_ref.shape[0] // width):
            bias_row = pieces[0][2 * depth + i : 2 * depth + i + 1, :].astype(F32)
            bias_oth_ref[i * width : (i + 1) * width] = bias_row.reshape(width)
    else:
        w_oth_ref[...] = pieces[0][...]
        out_oth_ref[...] = pieces[1][...]
        bias_oth_ref[...] = pieces[2][...].astype(F32)
    hidden_in = hidden_rows(tokens_ref, pos_ref, windows)
    attend_forward(
        hidden_in.astype(BF16), w_oth_ref, windows, mixed_ref, probs_ref, context_ref
    )
    branch = mm(context_own_ref[...], out_own_ref[...]) + mm(context_ref[...], out_oth_ref[...])
    hidden_in = hidden_rows(tokens_ref, pos_ref, windows)
    resid_ref[...] = hidden_in + branch + row(out_bias_ref)


def core_split(whole_ref, keep_ref, send_ref, start, split):
    half = whole_ref.shape[0] // 2
    core = place("core") if split else 0
    keep_ref[start : start + half, :] = whole_ref[part(core, half), :]
    send_ref[start : start + half, :] = whole_ref[part(1 - core, half), :]


def ffn_forward(low_ref, up_ref, bias_ref, act_ref, slope_ref):
    for start in range(0, up_ref.shape[1], CHUNK):
        cols = slice(start, start + CHUNK)
        pre = mm(low_ref[...], up_ref[:, cols]) + row(bias_ref, start, CHUNK)
        total, density = normal_parts(pre)
        act_ref[:, cols] = (pre * total).astype(BF16)
        slope_ref[:, cols] = (total + pre * density).astype(BF16)


def ffn_own_kernel(
    resid_ref,
    up_ref,
    down_ref,
    bias_ref,
    gain_ref,
    shift_ref,
    low_ref,
    act_ref,
    slope_ref,
    branch_ref,
):
    hat, _ = norm_stats(resid_ref[...])
    normed = hat * row(gain_ref) + row(shift_ref)
    low_ref[...] = normed.astype(BF16)
    ffn_forward(low_ref, up_ref, bias_ref, act_ref, slope_ref)
    branch_ref[...] = normed + mm(act_ref[...], down_ref[...])


def ffn_other_kernel(
    split,
    cot_ref,
    low_ref,
    act_own_ref,
    branch_ref,
    up_refs,
    down_refs,
    bias_ref,
    down_bias_ref,
    gain_ref,
    shift_ref,
    layer_ref,
    keep_ref,
    send_ref,
    slope_ref,
    up_ref,
    down_ref,
    grad_ref,
    vec_ref,
    act_ref,
    package_ref,
):
    width = cot_ref.shape[1]
    units = up_ref.shape[1]
    if len(up_refs) == 4:
        for ref, index in places(up_refs, place("x")):
            depth = ref.shape[0] * width // units
            for i in range(units // width):
                up_ref[part(index, depth), i * width : (i + 1) * width] = ref[
                    i * depth : (i + 1) * depth, :
                ]
        for ref, index in places(down_refs, z_bit()):
            down_ref[part(index, ref.shape[0]), :] = ref[...]
    else:
        up_ref[...] = up_refs[0][...]
        down_ref[...] = down_refs[0][...]
    ffn_forward(low_ref, up_ref, bias_ref, act_ref, slope_ref)
    resid = branch_ref[...] + mm(act_ref[...], down_ref[...]) + row(down_bias_ref)
    hat, scale = norm_stats(resid)
    layer_ref[...] = (hat * row(gain_ref) + row(shift_ref)).astype(BF16)
    cot = cot_ref[...].astype(F32)
    vec_ref[1:2, :] = jnp.sum(cot * hat, axis=0, keepdims=True)
    vec_ref[2:3, :] = jnp.sum(cot, axis=0, keepdims=True)
    grad = norm_grad(cot * row(gain_ref), hat, scale)
    vec_ref[0:1, :] = jnp.sum(grad, axis=0, keepdims=True)
    grad_ref[...] = grad
    grad_low = grad.astype(BF16)
    for half, act in ((0, act_own_ref), (1, act_ref)):
        for start in range(0, units, CHUNK):
            cols = slice(start, start + CHUNK)
            package_ref[cols, :] = mm_tn(act[:, cols], grad_low).astype(BF16)
        core_split(package_ref, keep_ref, send_ref, half * (units // 2), split)


def ffn_back_kernel(
    split,
    resid_ref,
    grad_ref,
    low_ref,
    slopes,
    ups,
    downs,
    contexts,
    vec_ref,
    gain_ref,
    keep_ref,
    send_ref,
    small_ref,
    grad_resid_ref,
    work_ref,
    total_ref,
    package_ref,
    bias_sum_ref,
    out_ref,
):
    width = resid_ref.shape[1]
    units = ups[0].shape[1]
    half_width = width // 2
    group = (units + half_width) // 2
    grad_low = grad_ref[...].astype(BF16)
    for half in range(2):
        for start in range(0, units, CHUNK):
            cols = slice(start, start + CHUNK)
            grad_act = mm_nt(grad_low, downs[half][cols, :])
            pre_grad = (grad_act * slopes[half][:, cols].astype(F32)).astype(BF16)
            work_ref[:, cols] = pre_grad
            at = half * (units // width) + start // width
            bias_sum_ref[at : at + 1, start % width : start % width + CHUNK] = jnp.sum(
                pre_grad.astype(F32), axis=0, keepdims=True
            )
        for start in range(0, units, width):
            cols = slice(start, start + width)
            package_ref[cols, :] = mm_tn(low_ref[...], work_ref[:, cols]).astype(BF16)
        core_split(package_ref, keep_ref, send_ref, half * group, split)
        before = grad_ref[...] if half == 0 else total_ref[...]
        total_ref[...] = before + mm_nt(work_ref[...], ups[half][...])
    grad = total_ref[...]
    hat, scale = norm_stats(resid_ref[...])
    small_ref[1:2, :] = jnp.sum(grad * hat, axis=0, keepdims=True)
    small_ref[2:3, :] = jnp.sum(grad, axis=0, keepdims=True)
    grad = norm_grad(grad * row(gain_ref), hat, scale)
    small_ref[0:1, :] = jnp.sum(grad, axis=0, keepdims=True)
    grad_low = grad.astype(BF16)
    for half in range(2):
        out_ref[...] = mm_tn(contexts[half][...], grad_low).astype(BF16)
        core_split(out_ref, keep_ref, send_ref, half * group + units // 2, split)
    small_ref[3:6, :] = vec_ref[0:3, :]
    span = units // width
    first_half = (place("mp") if split else 0) == 0
    ours, theirs = bias_sum_ref[0:span, :], bias_sum_ref[span : 2 * span, :]
    small_ref[6 : 6 + span, :] = jnp.where(first_half, ours, theirs)
    small_ref[6 + span : 6 + 2 * span, :] = jnp.where(first_half, theirs, ours)
    used = 6 + 2 * span
    small_ref[used:, :] = jnp.zeros((small_ref.shape[0] - used, width), F32)
    keep_ref[2 * group :, :] = small_ref[...].astype(BF16)
    send_ref[2 * group :, :] = small_ref[...].astype(BF16)
    grad_resid_ref[...] = grad


def half_backward(
    split,
    hidden_low,
    grad_low,
    weight_ref,
    out_ref,
    mixed_ref,
    probs_ref,
    keep_ref,
    send_ref,
    gm_ref,
    package_ref,
):
    rows, width = hidden_low.shape
    half_width = width // 2
    grad_context = mm_nt(grad_low, out_ref[...]).astype(BF16)
    attend_backward(grad_context, mixed_ref, probs_ref, rows // W_LONG, gm_ref)
    package_ref[0:width, 0:half_width] = mm_tn(hidden_low, gm_ref[0]).astype(BF16)
    package_ref[0:width, half_width:] = mm_tn(hidden_low, gm_ref[1]).astype(BF16)
    value_grad = mm_tn(hidden_low, gm_ref[2]).astype(BF16)
    package_ref[width : width + half_width, 0:half_width] = value_grad[0:half_width, :]
    package_ref[width : width + half_width, half_width:] = value_grad[half_width:, :]
    core_split(package_ref, keep_ref, send_ref, 0, split)
    return (
        mm_nt(gm_ref[0], weight_ref[0])
        + mm_nt(gm_ref[1], weight_ref[1])
        + mm_nt(gm_ref[2], weight_ref[2])
    )


def attend_back_kernel(
    split,
    win_ref,
    tokens_ref,
    pos_ref,
    grad_resid_ref,
    own_refs,
    other_refs,
    other_keep_ref,
    other_send_ref,
    own_keep_ref,
    own_send_ref,
    table_keep_ref,
    table_send_ref,
    tokens_grad_ref,
    grad_ref,
    gm_ref,
    package_ref,
    table_ref,
):
    rows, width = tokens_ref.shape
    windows = read_windows(win_ref, rows)
    hidden_low = hidden_rows(tokens_ref, pos_ref, windows).astype(BF16)
    grad_low = grad_resid_ref[...].astype(BF16)
    for before_ref, refs, to_refs in (
        (grad_resid_ref, other_refs, (other_keep_ref, other_send_ref)),
        (grad_ref, own_refs, (own_keep_ref, own_send_ref)),
    ):
        part_grad = half_backward(
            split, hidden_low, grad_low, *refs, *to_refs, gm_ref, package_ref
        )
        grad_ref[...] = before_ref[...] + part_grad
    grad = grad_ref[...]
    tokens_grad_ref[...] = grad.astype(BF16)
    first, second = None, None
    for block, is_long in enumerate(windows):
        top = grad[block * W_LONG : block * W_LONG + W_SHORT]
        bottom = grad[block * W_LONG + W_SHORT : (block + 1) * W_LONG]
        zero = jnp.zeros_like(top)
        part_first = top + jnp.where(is_long, zero, bottom)
        part_second = jnp.where(is_long, bottom, zero)
        first = part_first if first is None else first + part_first
        second = part_second if second is None else second + part_second
    table_ref[0:W_SHORT, :] = first.astype(BF16)
    table_ref[W_SHORT:, :] = second.astype(BF16)
    core_split(table_ref, table_keep_ref, table_send_ref, 0, split)


def total_of(*values):
    total = values[0].astype(F32)
    for value in values[1:]:
        total = total + value.astype(F32)
    return total


def bit_split(bit, value, work_ref, keep_ref, send_ref, start=0):
    half = value.shape[0] // 2
    work_ref[...] = value.astype(BF16)
    keep_ref[start : start + half, :] = work_ref[part(bit, half), :]
    send_ref[start : start + half, :] = work_ref[part(1 - bit, half), :]


def other_half_kernel(keep_ref, recv_ref, send_ref):
    start = keep_ref.shape[0] - send_ref.shape[0]
    send_ref[...] = total_of(keep_ref[start:, :], recv_ref[start:, :]).astype(BF16)


def down_split_kernel(keep_ref, recv_ref, from_y_ref, x_keep_ref, x_send_ref, work_ref):
    rows = from_y_ref.shape[0]
    total = total_of(keep_ref[0:rows, :], recv_ref[0:rows, :], from_y_ref[...])
    bit_split(place("x"), total, work_ref, x_keep_ref, x_send_ref)


def pair_kernel(a_ref, b_ref, out_ref):
    out_ref[...] = total_of(a_ref[...], b_ref[...]).astype(BF16)


def up_split_kernel(keep_ref, recv_ref, x_keep_ref, x_send_ref, work_ref):
    rows = work_ref.shape[0]
    for half in range(2):
        rows_of = slice(half * rows, (half + 1) * rows)
        total = total_of(keep_ref[rows_of, :], recv_ref[rows_of, :])
        start = half * (rows // 2)
        bit_split(z_bit(), total, work_ref, x_keep_ref, x_send_ref, start)
    small = total_of(keep_ref[2 * rows :, :], recv_ref[2 * rows :, :]).astype(BF16)
    x_keep_ref[rows:, :] = small
    x_send_ref[rows:, :] = small


def down_x_kernel(keep_ref, recv_ref, z_keep_ref, z_send_ref, work_ref):
    bit_split(z_bit(), total_of(keep_ref[...], recv_ref[...]), work_ref, z_keep_ref, z_send_ref)


def up_x_kernel(keep_ref, recv_ref, z_keep_ref, z_send_ref, work_ref):
    rows = work_ref.shape[0]
    for half in range(2):
        rows_of = slice(half * rows, (half + 1) * rows)
        total = total_of(keep_ref[rows_of, :], recv_ref[rows_of, :])
        bit_split(place("x"), total, work_ref, z_keep_ref, z_send_ref, half * (rows // 2))
    small = total_of(keep_ref[2 * rows :, :], recv_ref[2 * rows :, :]).astype(BF16)
    z_keep_ref[rows:, :] = small
    z_send_ref[rows:, :] = small


def up_z_kernel(keep_ref, recv_ref, y_keep_ref, y_send_ref):
    rows = y_keep_ref.shape[0] - EXTRA
    y_keep_ref[0:rows, :] = total_of(keep_ref[0:rows, :], recv_ref[0:rows, :]).astype(BF16)
    y_send_ref[...] = total_of(keep_ref[rows:, :], recv_ref[rows:, :]).astype(BF16)
    y_keep_ref[rows:, :] = y_send_ref[rows:, :]


def up_last_kernel(own_ref, recv_ref, out_ref, *small_refs):
    *vector_refs, bias_ref, work_ref = small_refs
    rows, width = out_ref.shape
    out_ref[...] = total_of(own_ref[0:rows, :], recv_ref[0:rows, :]).astype(BF16)
    work_ref[...] = total_of(own_ref[rows:, :], recv_ref[rows:, :])
    for i, ref in enumerate(vector_refs):
        ref[...] = work_ref[i : i + 1, :].reshape(width)
    span = bias_ref.shape[0] // width
    for i in range(span):
        value = work_ref[pl.ds(6 + place("mp") * span + i, 1), :]
        bias_ref[i * width : (i + 1) * width] = value.reshape(width)


def join_kernel(axis, own_ref, recv_ref, out_ref):
    rows = own_ref.shape[0]
    bit = z_bit() if axis == "z" else place("x")
    out_ref[part(bit, rows), :] = own_ref[...]
    out_ref[part(1 - bit, rows), :] = recv_ref[...]


def attend_core_kernel(
    keep_ref, recv_ref, table_keep_ref, table_recv_ref, to_y_ref, table_ref, work_ref
):
    rows = keep_ref.shape[0]
    to_y_ref[0:rows, :] = total_of(keep_ref[...], recv_ref[...]).astype(BF16)
    total = total_of(table_keep_ref[...], table_recv_ref[...])
    bit_split(place("mp"), total, work_ref, table_ref, to_y_ref.at[rows:, :])


def attend_mp_kernel(
    keep_ref, recv_ref, from_y_ref, table_ref, x_keep_ref, x_send_ref, work_ref, spare_ref
):
    rows = keep_ref.shape[0]
    total = total_of(keep_ref[...], recv_ref[...], from_y_ref[0:rows, :])
    bit_split(place("x"), total, work_ref, x_keep_ref, x_send_ref)
    total = total_of(table_ref[...], from_y_ref[rows:, :])
    bit_split(place("x"), total, spare_ref, x_keep_ref, x_send_ref, rows // 2)


def attend_x_kernel(keep_ref, recv_ref, z_keep_ref, z_send_ref, work_ref, spare_ref):
    rows = work_ref.shape[0]
    total = total_of(keep_ref[0:rows, :], recv_ref[0:rows, :])
    bit_split(z_bit(), total, work_ref, z_keep_ref, z_send_ref)
    total = total_of(keep_ref[rows:, :], recv_ref[rows:, :])
    bit_split(z_bit(), total, spare_ref, z_keep_ref, z_send_ref, rows // 2)


def attend_join_kernel(own_ref, recv_ref, out_ref, table_ref):
    spare = table_ref.shape[0] // 2
    rows = own_ref.shape[0] - spare
    for ref, bit in ((own_ref, z_bit()), (recv_ref, 1 - z_bit())):
        out_ref[part(bit, rows), :] = ref[0:rows, :]
        table_ref[part(bit, spare), :] = ref[rows:, :]
    out_ref[2 * rows :, :] = table_ref[...]


def corners(parts, bit):
    own_ref, near_ref, core_own_ref, core_near_ref = parts
    core = place("core")
    return (
        (own_ref, core * 2 + bit),
        (near_ref, core * 2 + 1 - bit),
        (core_own_ref, (1 - core) * 2 + bit),
        (core_near_ref, (1 - core) * 2 + 1 - bit),
    )


def down_out_kernel(*refs):
    *parts, out_ref, token_ref = refs
    token_ref[...] = jnp.zeros(token_ref.shape, F32)
    for ref, index in corners(parts, place("x")):
        out_ref[part(index, ref.shape[0]), :] = ref[...].astype(F32)


def up_out_kernel(*refs):
    *parts, up_ref, out_ref, token_ref, work_ref = refs
    token_ref[...] = jnp.zeros(token_ref.shape, F32)
    for ref, index in corners(parts, z_bit()):
        work_ref[part(index, ref.shape[0]), :] = ref[...]
    width, spare = up_ref.shape[0], out_ref.shape[0] // 2
    for core in range(2):
        start = core * (width + spare)
        up_ref[:, core * width : (core + 1) * width] = work_ref[start : start + width, :].astype(F32)
        start += width
        out_ref[core * spare : (core + 1) * spare, :] = work_ref[start : start + spare, :].astype(F32)


def attend_out_kernel(parts, table_parts, qkv_ref, table_ref, work_ref):
    y = place("mp")
    spare = table_parts[0].shape[0]
    rows = parts[0].shape[0] - spare
    half = qkv_ref.shape[2]
    width = 2 * half
    for ref, index in corners(parts, place("x")):
        work_ref[part(index, rows), :] = ref[0:rows, :]
        core, x = lax.div(index, 2), lax.rem(index, 2)
        table_ref[part(core * 4 + y * 2 + x, spare), :] = ref[rows:, :].astype(F32)
    for ref, index in corners(table_parts, place("x")):
        core, x = lax.div(index, 2), lax.rem(index, 2)
        table_ref[part(core * 4 + (1 - y) * 2 + x, spare), :] = ref[...].astype(F32)
    qkv_ref[0] = work_ref[0:width, 0:half].astype(F32)
    qkv_ref[1] = work_ref[0:width, half:].astype(F32)
    qkv_ref[2, 0:half, :] = work_ref[width : width + half, 0:half].astype(F32)
    qkv_ref[2, half:, :] = work_ref[width : width + half, half:].astype(F32)


def swap(value, axis, name="swap", distance=1):
    pairs = [(i, i ^ distance) for i in range(lax.axis_size(axis))]
    with jax.named_scope(f"{name}_{axis}{distance}"):
        return lax.ppermute(value, axis, pairs)


def swap_corner(value, name):
    with jax.named_scope(name):
        return lax.ppermute(value, ("x", "mp"), [(0, 3), (1, 2), (2, 1), (3, 0)])


class Chain:
    def __init__(self):
        self.last = ()

    def gate(self, value, us=1):
        value = pl.pallas_call(
            lambda *refs: None,
            out_shape=jax.ShapeDtypeStruct(value.shape, value.dtype),
            in_specs=[anywhere] * (1 + len(self.last)),
            out_specs=anywhere,
            input_output_aliases={0: 0},
            compiler_params=pltpu.CompilerParams(vmem_limit_bytes=MIB),
            cost_estimate=pl.CostEstimate(
                flops=us * FLOPS_PER_US, bytes_accessed=0, transcendentals=0
            ),
            name="gate",
        )(value, *self.last)
        self.last = (value,)
        return value

    def __call__(
        self,
        kernel,
        outs,
        args,
        us,
        name,
        scratch=(),
        smem_args=0,
        hbm_args=0,
        copies=0,
        mib=8,
        token=None,
    ):
        results = call(
            kernel, outs, args, self.last, scratch, us, mib, smem_args, hbm_args, copies, name
        )
        if token is None:
            token = min(range(len(results)), key=lambda i: results[i].size)
        self.last = (results[token],)
        return results


def per_device(
    fast,
    mp_size,
    tokens,
    pos_table,
    qkv_weight,
    out_weight,
    out_bias,
    norm1_gain,
    norm1_shift,
    up_weight,
    up_bias,
    down_weight,
    down_bias,
    norm2_gain,
    norm2_shift,
    window,
    cotangent,
):
    step = Chain()
    rows, width = tokens.shape
    blocks = rows // W_LONG
    half_width = width // 2
    units = up_weight.shape[1] * mp_size // 2
    n, spare = width, W_LONG // 2
    group, att = (units + half_width) // 2, 3 * width // 4
    qkv_weight = jnp.transpose(qkv_weight, (1, 0, 2))
    wide = ((rows, width), F32)

    attend_outs = [
        (3, rows, half_width),
        (blocks * half_width // HD * 3, W_SHORT, W_SHORT),
        (rows, half_width),
    ]

    def attend_own():
        return step(
            first_kernel,
            attend_outs,
            [window, tokens, pos_table, w_own],
            3,
            "attend_first",
            mib=28,
            smem_args=1,
        )

    def attend_other():
        return step(
            second_kernel,
            attend_outs
            + [wide, (3, width, half_width), (half_width, width), ((units,), F32)],
            [window, tokens, pos_table, attend_in, context_own, out_own, out_bias],
            5,
            "attend_second",
            mib=28,
            smem_args=1,
        )

    def ffn_own():
        return step(
            ffn_own_kernel,
            [(rows, width), (rows, units), (rows, units), wide],
            [resid, up_own, down_own, bias_own, norm1_gain, norm1_shift],
            4,
            "ffn_own",
            mib=28,
        )

    if fast:
        w_own, out_own, up_own, down_own = qkv_weight, out_weight, up_weight, down_weight
        bias_own = up_bias
        (message,) = step(
            pack_attend_kernel,
            [(width // 2 + EXTRA, width)],
            [up_bias, qkv_weight, out_weight],
            1,
            "pack_attend",
            mib=60,
            hbm_args=2,
            copies=5,
        )
        attend_y = swap(message, "mp", "attend_y")
        up_message, down_message = step(
            pack_ffn_kernel,
            [(units // 4, width), (units // 4, width)],
            [up_weight, down_weight],
            1,
            "pack_ffn",
            mib=60,
            hbm_args=2,
            copies=1 + units // width,
        )
        up_y = swap(up_message, "mp", "up_y")
        down_y = swap(down_message, "mp", "down_y")
        mixed_own, probs_own, context_own = attend_own()
        attend_y = step.gate(attend_y)
        attend_x = swap(attend_y, "x", "attend_x")
        attend_cy = swap(attend_y, "core", "attend_cy")
        up_y = step.gate(up_y)
        up_x = swap(up_y, "x", "up_x")
        up_cy = swap(up_y, "core", "up_cy")
        attend_x = step.gate(attend_x)
        attend_cx = swap(attend_x, "core", "attend_cx")
        down_y = step.gate(down_y)
        down_z = swap(down_y, "z", "down_z")
        down_cy = swap(down_y, "core", "down_cy")
        attend_in = (attend_y, attend_x, attend_cy, attend_cx)
        mixed_oth, probs_oth, context_oth, resid, w_oth, out_oth, bias_oth = attend_other()
        up_x = step.gate(up_x, 0)
        up_cx = swap(up_x, "core", "up_cx")
        low, act_own, slope_own, branch = ffn_own()
        down_z = step.gate(down_z)
        down_cz = swap(down_z, "core", "down_cz")
        up_in = (up_y, up_x, up_cy, up_cx)
        down_in = (down_y, down_z, down_cy, down_cz)
    else:
        qkv = lax.all_gather(qkv_weight, "mp", axis=2, tiled=True)
        out_w = lax.all_gather(out_weight, "mp", axis=0, tiled=True)
        up_w = lax.all_gather(up_weight, "mp", axis=1, tiled=True)
        bias = lax.all_gather(up_bias, "mp", axis=0, tiled=True)
        down_w = lax.all_gather(down_weight, "mp", axis=0, tiled=True)
        w_own, out_own = qkv[:, :, :half_width], out_w[:half_width]
        attend_in = (qkv[:, :, half_width:], out_w[half_width:], bias[units:])
        up_own, up_in = up_w[:, :units], (up_w[:, units:],)
        down_own, down_in = down_w[:units], (down_w[units:],)
        bias_own = bias[:units]
        mixed_own, probs_own, context_own = attend_own()
        mixed_oth, probs_oth, context_oth, resid, w_oth, out_oth, bias_oth = attend_other()
        low, act_own, slope_own, branch = ffn_own()

    layer_out, down_keep, down_send, slope_oth, up_oth, down_oth, grad2, vec = step(
        functools.partial(ffn_other_kernel, fast),
        [
            (rows, width),
            (units, width),
            (units, width),
            (rows, units),
            (width, units),
            (units, width),
            wide,
            ((8, width), F32),
        ],
        [
            cotangent,
            low,
            act_own,
            branch,
            up_in,
            down_in,
            bias_oth,
            down_bias,
            norm2_gain,
            norm2_shift,
        ],
        6,
        "ffn_other",
            mib=28,
        scratch=[((rows, units), BF16), ((units, width), BF16)],
    )
    down_recv = swap(down_send, "core", "down_recv") if fast else None
    up_keep, up_send, small, grad1 = step(
        functools.partial(ffn_back_kernel, fast),
        [
            (2 * group + EXTRA, width),
            (2 * group + EXTRA, width),
            ((EXTRA, width), F32),
            wide,
        ],
        [
            resid,
            grad2,
            low,
            (slope_own, slope_oth),
            (up_own, up_oth),
            (down_own, down_oth),
            (context_own, context_oth),
            vec,
            norm1_gain,
        ],
        6,
        "ffn_back",
            mib=28,
        scratch=[
            ((rows, units), BF16),
            ((rows, width), F32),
            ((units, width), BF16),
            ((8, width), F32),
            ((half_width, width), BF16),
        ],
    )

    def attend_back():
        return step(
            functools.partial(attend_back_kernel, fast),
            [(att, width)] * 4 + [(spare, width)] * 2 + [(rows, width)],
            [
                window,
                tokens,
                pos_table,
                grad1,
                (w_own, out_own, mixed_own, probs_own),
                (w_oth, out_oth, mixed_oth, probs_oth),
            ],
            13,
            "attend_back",
            mib=28,
            scratch=[
                ((rows, width), F32),
                ((3, rows, half_width), BF16),
                ((2 * att, width), BF16),
                ((W_LONG, width), BF16),
            ],
            smem_args=1,
        )

    if not fast:
        *att_parts, grad_tokens = attend_back()
        qkv_g, out_g, up_g, down_g, small, table = reduce_plain(
            n, width, down_keep, down_send, up_keep, up_send, small, *att_parts
        )
        vectors = [small[i] for i in range(6)]
        bias_all = small[6 : 6 + 2 * units // width].reshape(-1)
        start = lax.axis_index("mp") * up_bias.shape[0]
        bias_g = lax.dynamic_slice_in_dim(bias_all, start, up_bias.shape[0])
    else:
        half, piece, strip = n // 2, n // 4, spare // 2
        up_recv = swap(up_send, "core", "up_recv")
        (to_y,) = step(other_half_kernel, [(n, width)], [down_keep, down_recv], 6, "down_core")
        down_from_y = swap(to_y, "mp", "down_from_y")
        up_x, to_x = step(
            up_split_kernel,
            [(group + EXTRA, width)] * 2,
            [up_keep, up_recv],
            1,
            "up_core",
            scratch=[((group, width), BF16)],
        )
        up_from_x = swap(to_x, "z", "up_from_z")
        oth_keep, oth_send, own_keep, own_send, tab_keep, tab_send, grad_tokens = attend_back()
        oth_recv = swap(oth_send, "core", "oth_recv")
        tab_recv = swap(tab_send, "core", "tab_recv")
        own_recv = swap(own_send, "core", "own_recv")
        down_x, to_x = step(
            down_split_kernel,
            [(half, width)] * 2,
            [down_keep, down_recv, down_from_y],
            0,
            "down_mp",
            scratch=[((n, width), BF16)],
        )
        down_from_x = swap(to_x, "x", "down_from_x")
        to_y, table = step(
            attend_core_kernel,
            [(att + strip, width), (strip, width)],
            [oth_keep, oth_recv, tab_keep, tab_recv],
            0,
            "attend_core",
            scratch=[((spare, width), BF16)],
        )
        att_from_y = swap(to_y, "mp", "att_from_y")
        up_z, to_z = step(
            up_x_kernel,
            [(group // 2 + EXTRA, width)] * 2,
            [up_x, up_from_x],
            0,
            "up_x",
            scratch=[((group // 2, width), BF16)],
        )
        up_from_z = swap(to_z, "x", "up_from_x")
        down_z, to_z = step(
            down_x_kernel,
            [(piece, width)] * 2,
            [down_x, down_from_x],
            3,
            "down_x",
            scratch=[((half, width), BF16)],
        )
        down_from_z = swap(to_z, "z", "down_from_z")
        (down_z,) = step(pair_kernel, [(piece, width)], [down_z, down_from_z], 0, "down_z")
        down_far = swap(down_z, "z", "down_far", 2)
        att_x, to_x = step(
            attend_mp_kernel,
            [((att + strip) // 2, width)] * 2,
            [own_keep, own_recv, att_from_y, table],
            0,
            "attend_mp",
            scratch=[((att, width), BF16), ((strip, width), BF16)],
        )
        att_from_x = swap(to_x, "x", "att_from_x")
        up_y, to_y = step(
            up_z_kernel, [(group // 4 + EXTRA, width)] * 2, [up_z, up_from_z], 0, "up_z"
        )
        up_from_y = swap(to_y, "mp", "up_from_y")
        (down_z,) = step(pair_kernel, [(piece, width)], [down_z, down_far], 0, "down_far")
        down_near = swap(down_z, "z", "down_near")
        att_z, to_z = step(
            attend_x_kernel,
            [((att + strip) // 4, width)] * 2,
            [att_x, att_from_x],
            0,
            "attend_x",
            scratch=[((att // 2, width), BF16), ((strip // 2, width), BF16)],
        )
        att_from_z = swap(to_z, "z", "att_from_z")
        (up_y,) = step(pair_kernel, [(group // 4 + EXTRA, width)], [up_y, up_from_y], 0, "up_mp")
        up_far = swap(up_y, "z", "up_far", 2)
        (att_z,) = step(pair_kernel, [att_z.shape], [att_z, att_from_z], 0, "attend_z")
        att_far = swap(att_z, "z", "att_far", 2)
        (down_z,) = step(functools.partial(join_kernel, "z"), [(half, width)], [down_z, down_near], 0, "down_join")
        down_x = swap(down_z, "x", "down_x")
        up_z, *vectors, bias_g = step(
            up_last_kernel,
            [(group // 4, width)] + [((width,), F32)] * 6 + [((up_bias.shape[0],), F32)],
            [up_y, up_far],
            0,
            "up_far",
            token=0,
            scratch=[((EXTRA, width), F32)],
        )
        up_near = swap(up_z, "x", "up_near")
        (att_z,) = step(pair_kernel, [att_z.shape], [att_z, att_far], 0, "attend_far")
        att_near = swap(att_z, "z", "att_near")
        att_half, table = step(
            attend_join_kernel,
            [((att + strip) // 2, width), (strip // 2, width)],
            [att_z, att_near],
            0,
            "attend_join",
        )
        att_x = swap(att_half, "x", "att_x")
        table_y = swap(table, "mp", "table_y")
        table_x = swap_corner(table, "table_x")
        (up_z,) = step(functools.partial(join_kernel, "x"), [(group // 2, width)], [up_z, up_near], 0, "up_join")
        up_x = swap(up_z, "z", "up_last")
        down_x = step.gate(down_x, 0)
        down_g, _ = step(
            down_out_kernel,
            [((2 * n, width), F32), ((8, LANES), F32)],
            [
                down_z,
                down_x,
                swap(down_z, "core", "down_core"),
                swap(down_x, "core", "down_core_x"),
            ],
            0,
            "down_out",
        )
        table_y = step.gate(table_y, 0)
        up_x = step.gate(up_x, 0)
        table_x = step.gate(table_x, 0)
        att_x = step.gate(att_x, 0)
        up_g, out_g, _ = step(
            up_out_kernel,
            [((width, 2 * n), F32), ((half_width, width), F32), ((8, LANES), F32)],
            [up_z, up_x, swap(up_z, "core", "up_core"), swap(up_x, "core", "up_core_x")],
            0,
            "up_out",
            scratch=[((2 * group, width), BF16)],
        )
        qkv_g, table = step(
            attend_out_kernel,
            [((3, width, half_width), F32), ((W_LONG, width), F32)],
            [
                (
                    att_half,
                    att_x,
                    swap(att_half, "core", "att_core"),
                    swap(att_x, "core", "att_core_x"),
                ),
                (
                    table_y,
                    table_x,
                    swap(table_y, "core", "table_core"),
                    swap(table_x, "core", "table_core_x"),
                ),
            ],
            0,
            "attend_out",
            scratch=[((2 * att, width), BF16)],
        )


    return (
        layer_out,
        grad_tokens,
        table,
        jnp.transpose(qkv_g, (1, 0, 2)),
        out_g,
        vectors[0],
        vectors[1],
        vectors[2],
        up_g,
        bias_g,
        down_g,
        vectors[3],
        vectors[4],
        vectors[5],
    )


def reduce_plain(
    n,
    width,
    down_keep,
    down_send,
    up_keep,
    up_send,
    small,
    other_keep,
    other_send,
    own_keep,
    own_send,
    table_keep,
    table_send,
):
    half, spare = n // 2, n // 4
    group = n + spare

    def rows_of(start, size):
        return lambda keep, send: jnp.concatenate(
            [keep[start : start + size], send[start : start + size]], axis=0
        )

    def summed(own, oth, dim):
        whole = jnp.concatenate([own, oth], axis=dim)
        part_sum = lax.psum_scatter(whole, "mp", scatter_dimension=dim, tiled=True)
        return lax.psum(part_sum, "dp").astype(F32)

    def qkv_part(g):
        value = jnp.concatenate([g[n : n + half, :half], g[n : n + half, half:]], axis=0)
        return jnp.stack([g[:n, :half], g[:n, half:], value])

    def up_part(g):
        return jnp.concatenate([g[:n], g[n:]], axis=1)

    down = [rows_of(start, n)(down_keep, down_send) for start in (0, n)]
    up = [up_part(rows_of(start, n)(up_keep, up_send)) for start in (0, group)]
    out = [rows_of(start + n, spare)(up_keep, up_send) for start in (0, group)]
    att = [
        qkv_part(jnp.concatenate(pair, axis=0))
        for pair in ((own_keep, own_send), (other_keep, other_send))
    ]
    table = jnp.concatenate([table_keep, table_send], axis=0).astype(F32)
    return (
        summed(*att, 2),
        summed(*out, 0),
        summed(*up, 1),
        summed(*down, 0),
        lax.psum(small, ("dp", "mp")),
        lax.psum(table, ("dp", "mp")),
    )


def solution(mesh):
    mp_size = mesh.shape["mp"]
    fast = mp_size == 2 and mesh.shape["dp"] == 16
    dp = "dp"
    if fast:
        shape = (mesh.shape["dp"] // 4, 2, 2, mp_size)
        mesh = Mesh(mesh.devices.reshape(shape), ("z", "x", "core", "mp"))
        dp = ("z", "x", "core")
    both = P((*dp, "mp") if fast else (dp, "mp"), None)
    placed = (
        both,
        P(),
        P(None, None, "mp"),
        P("mp", None),
        P(),
        P(),
        P(),
        P(None, "mp"),
        P("mp"),
        P("mp", None),
        P(),
        P(),
        P(),
        P(dp),
        both,
    )
    return jax.shard_map(
        functools.partial(per_device, fast, mp_size),
        mesh=mesh,
        in_specs=placed,
        out_specs=(
            both,
            both,
            P(),
            P(None, None, "mp"),
            P("mp", None),
            P(),
            P(),
            P(),
            P(None, "mp"),
            P("mp"),
            P("mp", None),
            P(),
            P(),
            P(),
        ),
        check_vma=False,
    )
```

```python
import functools

import jax
import jax.numpy as jnp
from jax import lax
from jax.experimental import pallas as pl
from jax.experimental.pallas import tpu as pltpu
from jax.sharding import Mesh
from jax.sharding import PartitionSpec as P

HD = 64
W_SHORT = 256
W_LONG = 512
ROW = 1024
LANES = 128
EXTRA = 16
CHUNK = 256
EPSILON = 1e-05
MASKED = -1e30
F32 = jnp.float32
BF16 = jnp.bfloat16
MIB = 1024 * 1024
FLOPS_PER_US = 10**9

vmem = pl.BlockSpec(memory_space=pltpu.VMEM)
smem = pl.BlockSpec(memory_space=pltpu.SMEM)
anywhere = pl.BlockSpec(memory_space=pl.ANY)


def call(
    kernel, outs, args, after=(), scratch=(), us=1, mib=32, smem_args=0, hbm_args=0, copies=0, hbm_outs=False, name=None
):
    flat, tree = jax.tree.flatten(tuple(args))
    count, extra = len(flat), len(after)

    def flat_kernel(*refs):
        kernel(*jax.tree.unflatten(tree, refs[:count]), *refs[count + extra :])

    return pl.pallas_call(
        flat_kernel,
        out_shape=[
            jax.ShapeDtypeStruct(out, BF16) if isinstance(out[0], int) else jax.ShapeDtypeStruct(*out)
            for out in outs
        ],
        in_specs=[smem] * smem_args
        + [vmem] * (count - smem_args - hbm_args)
        + [anywhere] * (hbm_args + extra),
        out_specs=[anywhere if hbm_outs else vmem] * len(outs),
        scratch_shapes=[pltpu.VMEM(shape, dtype) for shape, dtype in scratch]
        + [pltpu.SemaphoreType.DMA((copies,))] * (copies > 0),
        compiler_params=pltpu.CompilerParams(vmem_limit_bytes=mib * MIB),
        cost_estimate=pl.CostEstimate(
            flops=us * FLOPS_PER_US, bytes_accessed=0, transcendentals=0
        ),
        name=name,
    )(*flat, *after)


def place(axis):
    return lax.axis_index(axis)


def row(ref, start=0, size=None):
    size = ref.shape[0] if size is None else size
    return ref[start : start + size].astype(F32).reshape(1, size)


def mm(a, b):
    return lax.dot_general(a, b, (((1,), (0,)), ((), ())), preferred_element_type=F32)


def mm_nt(a, b):
    return lax.dot_general(a, b, (((1,), (1,)), ((), ())), preferred_element_type=F32)


def mm_tn(a, b):
    return lax.dot_general(a, b, (((0,), (0,)), ((), ())), preferred_element_type=F32)


def position_rows(pos_ref, is_long):
    first = pos_ref[0:W_SHORT, :].astype(F32)
    second = jnp.where(is_long, pos_ref[W_SHORT:W_LONG, :].astype(F32), first)
    return first, second


def hidden_rows(tokens_ref, pos_ref, windows):
    parts = []
    for block, is_long in enumerate(windows):
        first, second = position_rows(pos_ref, is_long)
        start = block * W_LONG
        parts.append(tokens_ref[start : start + W_SHORT, :].astype(F32) + first)
        parts.append(tokens_ref[start + W_SHORT : start + W_LONG, :].astype(F32) + second)
    return jnp.concatenate(parts, axis=0)


def read_windows(win_ref, rows):
    first = place("mp") * rows
    return [
        win_ref[lax.div(first + block * W_LONG, ROW)] == W_LONG for block in range(rows // W_LONG)
    ]


def norm_stats(values):
    average = jnp.mean(values, axis=-1, keepdims=True)
    centred = values - average
    variance = jnp.mean(centred * centred, axis=-1, keepdims=True)
    scale = lax.rsqrt(variance + EPSILON)
    return centred * scale, scale


def norm_grad(grad_hat, hat, scale):
    mean_grad = jnp.mean(grad_hat, axis=-1, keepdims=True)
    mean_both = jnp.mean(grad_hat * hat, axis=-1, keepdims=True)
    return scale * (grad_hat - mean_grad - hat * mean_both)


def head_mask(rows):
    return lax.broadcasted_iota(jnp.int32, (rows, LANES), 1) < HD


def stack_heads(value, is_low):
    zero = jnp.zeros_like(value)
    return jnp.concatenate(
        [jnp.where(is_low, value, zero), jnp.where(is_low, zero, value)], axis=0
    )


def late_rows(value):
    return jnp.concatenate(
        [value[W_SHORT:W_LONG], value[W_LONG + W_SHORT : 2 * W_LONG]], axis=0
    )


def merge_heads(first, late, is_low):
    top = jnp.where(is_low, first[0:W_SHORT], first[W_LONG : W_LONG + W_SHORT])
    bottom = jnp.where(
        is_low,
        first[W_SHORT:W_LONG] + late[0:W_SHORT],
        first[W_LONG + W_SHORT :] + late[W_SHORT:],
    )
    return top, bottom


def attend_forward(hidden_low, weight_ref, windows, mixed_ref, early_ref, late_ref, context_ref):
    rows, width = context_ref.shape
    pairs = width // LANES
    for c in range(3):
        part = mm(hidden_low, weight_ref[c]).astype(BF16)
        mixed_ref[c] = part * BF16(HD**-0.5) if c == 0 else part
    causal = lax.broadcasted_iota(jnp.int32, (W_SHORT, W_SHORT), 0) >= lax.broadcasted_iota(
        jnp.int32, (W_SHORT, W_SHORT), 1
    )
    is_low = head_mask(W_LONG)
    for block, is_long in enumerate(windows):
        both = slice(block * W_LONG, (block + 1) * W_LONG)
        lo = slice(block * W_LONG, block * W_LONG + W_SHORT)
        hi = slice(block * W_LONG + W_SHORT, (block + 1) * W_LONG)
        for pair in range(pairs):
            lanes = slice(pair * LANES, (pair + 1) * LANES)
            slot = block * pairs + pair
            queries = stack_heads(mixed_ref[0, both, lanes], is_low)
            scores = mm_nt(queries, mixed_ref[1, lo, lanes])
            late = mm_nt(late_rows(queries), mixed_ref[1, hi, lanes])
            for head in range(2):
                start = head * W_LONG
                s_a = jnp.where(causal, scores[start : start + W_SHORT], MASKED)
                e_a = jnp.exp(s_a - jnp.max(s_a, axis=-1, keepdims=True))
                p_a = e_a * (1.0 / jnp.sum(e_a, axis=-1, keepdims=True))
                s_b = jnp.where(is_long, scores[start + W_SHORT : start + W_LONG], MASKED)
                s_c = jnp.where(causal, late[head * W_SHORT : (head + 1) * W_SHORT], MASKED)
                top = jnp.max(jnp.maximum(s_b, s_c), axis=-1, keepdims=True)
                e_b = jnp.exp(s_b - top)
                e_c = jnp.exp(s_c - top)
                inverse = 1.0 / jnp.sum(e_b + e_c, axis=-1, keepdims=True)
                early_ref[slot, start : start + W_SHORT, :] = p_a.astype(BF16)
                early_ref[slot, start + W_SHORT : start + W_LONG, :] = (e_b * inverse).astype(BF16)
                late_ref[slot, head * W_SHORT : (head + 1) * W_SHORT, :] = (e_c * inverse).astype(
                    BF16
                )
            top_rows, bottom_rows = merge_heads(
                mm(early_ref[slot], mixed_ref[2, lo, lanes]),
                mm(late_ref[slot], mixed_ref[2, hi, lanes]),
                head_mask(W_SHORT),
            )
            context_ref[lo, lanes] = top_rows.astype(BF16)
            context_ref[hi, lanes] = bottom_rows.astype(BF16)


def attend_backward(grad_context, mixed_ref, early_ref, late_ref, blocks, grad_mixed_ref, work):
    width = mixed_ref.shape[2]
    pairs = width // LANES
    is_low = head_mask(W_LONG)
    early_grad_ref, late_grad_ref = work
    for block in range(blocks):
        both = slice(block * W_LONG, (block + 1) * W_LONG)
        lo = slice(block * W_LONG, block * W_LONG + W_SHORT)
        hi = slice(block * W_LONG + W_SHORT, (block + 1) * W_LONG)
        for pair in range(pairs):
            lanes = slice(pair * LANES, (pair + 1) * LANES)
            slot = block * pairs + pair
            queries = stack_heads(mixed_ref[0, both, lanes], is_low)
            grads = stack_heads(grad_context[both, lanes], is_low)
            grad_early = mm_nt(grads, mixed_ref[2, lo, lanes])
            grad_late = mm_nt(late_rows(grads), mixed_ref[2, hi, lanes])
            for head in range(2):
                start = head * W_LONG
                first = slice(start, start + W_SHORT)
                second = slice(start + W_SHORT, start + W_LONG)
                last = slice(head * W_SHORT, (head + 1) * W_SHORT)
                p_a = early_ref[slot, first, :].astype(F32)
                g_a = grad_early[first]
                inner = jnp.sum(p_a * g_a, axis=-1, keepdims=True)
                early_grad_ref[pair, first, :] = (p_a * (g_a - inner)).astype(BF16)
                p_b, p_c = early_ref[slot, second, :].astype(F32), late_ref[slot, last, :].astype(F32)
                g_b, g_c = grad_early[second], grad_late[last]
                inner = jnp.sum(p_b * g_b + p_c * g_c, axis=-1, keepdims=True)
                early_grad_ref[pair, second, :] = (p_b * (g_b - inner)).astype(BF16)
                late_grad_ref[pair, last, :] = (p_c * (g_c - inner)).astype(BF16)
            top_rows, bottom_rows = merge_heads(
                mm(early_grad_ref[pair], mixed_ref[1, lo, lanes]),
                mm(late_grad_ref[pair], mixed_ref[1, hi, lanes]),
                head_mask(W_SHORT),
            )
            grad_mixed_ref[0, lo, lanes] = (top_rows * HD**-0.5).astype(BF16)
            grad_mixed_ref[0, hi, lanes] = (bottom_rows * HD**-0.5).astype(BF16)
            grad_mixed_ref[1, lo, lanes] = mm_tn(early_grad_ref[pair], queries).astype(BF16)
            grad_mixed_ref[1, hi, lanes] = mm_tn(late_grad_ref[pair], late_rows(queries)).astype(BF16)
            grad_mixed_ref[2, lo, lanes] = mm_tn(early_ref[slot], grads).astype(BF16)
            grad_mixed_ref[2, hi, lanes] = mm_tn(late_ref[slot], late_rows(grads)).astype(BF16)


def normal_parts(x):
    density = jnp.exp2(x * x * -0.7213475204 - 1.3257480647)
    return 0.5 + 0.5 * lax.erf(x * 0.7071067812), density


def first_kernel(
    win_ref, tokens_ref, pos_ref, weight_ref, mixed_ref, early_ref, late_ref, context_ref
):
    windows = read_windows(win_ref, tokens_ref.shape[0])
    hidden_low = hidden_rows(tokens_ref, pos_ref, windows).astype(BF16)
    attend_forward(
        hidden_low, weight_ref, windows, mixed_ref, early_ref, late_ref, context_ref
    )


def z_bit():
    return lax.rem(place("z"), 2)


def quarter(bit):
    return place("core") * 2 + bit


def part(index, size):
    return pl.ds(pl.multiple_of(index * size, size), size)


def copy_all(pairs, sems):
    copies = [
        pltpu.make_async_copy(src, dst, sems.at[i]) for i, (src, dst) in enumerate(pairs)
    ]
    for copy in copies:
        copy.start()
    for copy in copies:
        copy.wait()


def pack_attend_kernel(bias_ref, qkv_ref, out_ref, send_ref, sems):
    _, width, half = qkv_ref.shape
    depth, mine = width // 4, quarter(place("x"))
    for i in range(EXTRA):
        index = i if (i + 1) * width <= bias_ref.shape[0] else 0
        send_ref[2 * depth + i : 2 * depth + i + 1, :] = row(bias_ref, index * width, width).astype(
            BF16
        )
    middle = depth + depth // 2
    low, high = pl.ds(0, half), pl.ds(half, half)
    upper, lower = part(mine * 2, depth // 2), part(mine * 2 + 1, depth // 2)
    copy_all(
        [
            (qkv_ref.at[0, part(mine, depth), :], send_ref.at[pl.ds(0, depth), low]),
            (qkv_ref.at[1, part(mine, depth), :], send_ref.at[pl.ds(0, depth), high]),
            (qkv_ref.at[2, upper, :], send_ref.at[pl.ds(depth, depth // 2), low]),
            (qkv_ref.at[2, lower, :], send_ref.at[pl.ds(depth, depth // 2), high]),
            (out_ref.at[part(mine, depth // 2), :], send_ref.at[pl.ds(middle, depth // 2), :]),
        ],
        sems,
    )


def pack_ffn_kernel(up_ref, down_ref, up_to, down_to, sems):
    width, units = up_ref.shape
    depth = width // 8
    mine = part(quarter(place("x")) * 2 + z_bit(), depth)
    columns = [
        (up_ref.at[mine, pl.ds(i * width, width)], up_to.at[pl.ds(i * depth, depth), :])
        for i in range(units // width)
    ]
    copy_all([*columns, (down_ref.at[part(quarter(z_bit()), units // 4), :], down_to)], sems)


def z_join_kernel(own_ref, near_ref, out_ref):
    depth = own_ref.shape[0] // 2
    for ref, bit in ((own_ref, z_bit()), (near_ref, 1 - z_bit())):
        for i in range(2):
            rows = pl.ds(pl.multiple_of(i * 2 * depth + bit * depth, depth), depth)
            out_ref[rows, :] = ref[i * depth : (i + 1) * depth, :]


def places(pieces, bit):
    from_y, from_near, core_y, core_near = pieces
    core = place("core")
    return (
        (from_y, core * 2 + bit),
        (from_near, core * 2 + 1 - bit),
        (core_y, (1 - core) * 2 + bit),
        (core_near, (1 - core) * 2 + 1 - bit),
    )


def second_kernel(
    win_ref,
    tokens_ref,
    pos_ref,
    pieces,
    context_own_ref,
    out_own_ref,
    out_bias_ref,
    mixed_ref,
    early_ref,
    late_ref,
    context_ref,
    resid_ref,
    w_oth_ref,
    out_oth_ref,
    bias_oth_ref,
):
    width = tokens_ref.shape[1]
    half, depth = width // 2, width // 4
    windows = read_windows(win_ref, tokens_ref.shape[0])
    if len(pieces) == 4:
        for ref, index in places(pieces, place("x")):
            rows = part(index, depth)
            w_oth_ref[0, rows, :] = ref[0:depth, 0:half]
            w_oth_ref[1, rows, :] = ref[0:depth, half:]
            middle = depth + depth // 2
            w_oth_ref[2, part(index * 2, depth // 2), :] = ref[depth:middle, 0:half]
            w_oth_ref[2, part(index * 2 + 1, depth // 2), :] = ref[depth:middle, half:]
            out_oth_ref[part(index, depth // 2), :] = ref[middle : 2 * depth, :]
        for i in range(bias_oth_ref.shape[0] // width):
            bias_row = pieces[0][2 * depth + i : 2 * depth + i + 1, :].astype(F32)
            bias_oth_ref[i * width : (i + 1) * width] = bias_row.reshape(width)
    else:
        w_oth_ref[...] = pieces[0][...]
        out_oth_ref[...] = pieces[1][...]
        bias_oth_ref[...] = pieces[2][...].astype(F32)
    hidden_in = hidden_rows(tokens_ref, pos_ref, windows)
    attend_forward(
        hidden_in.astype(BF16),
        w_oth_ref,
        windows,
        mixed_ref,
        early_ref,
        late_ref,
        context_ref,
    )
    branch = mm(context_own_ref[...], out_own_ref[...]) + mm(context_ref[...], out_oth_ref[...])
    hidden_in = hidden_rows(tokens_ref, pos_ref, windows)
    resid_ref[...] = hidden_in + branch + row(out_bias_ref)


def core_split(whole_ref, keep_ref, send_ref, start, split):
    half = whole_ref.shape[0] // 2
    core = place("core") if split else 0
    keep_ref[start : start + half, :] = whole_ref[part(core, half), :]
    send_ref[start : start + half, :] = whole_ref[part(1 - core, half), :]


def ffn_forward(low_ref, up_ref, bias_ref, act_ref, slope_ref):
    for start in range(0, up_ref.shape[1], CHUNK):
        cols = slice(start, start + CHUNK)
        pre = mm(low_ref[...], up_ref[:, cols]) + row(bias_ref, start, CHUNK)
        total, density = normal_parts(pre)
        act_ref[:, cols] = (pre * total).astype(BF16)
        slope_ref[:, cols] = (total + pre * density).astype(BF16)


def ffn_own_kernel(
    resid_ref,
    up_ref,
    down_ref,
    bias_ref,
    gain_ref,
    shift_ref,
    low_ref,
    act_ref,
    slope_ref,
    branch_ref,
):
    hat, _ = norm_stats(resid_ref[...])
    normed = hat * row(gain_ref) + row(shift_ref)
    low_ref[...] = normed.astype(BF16)
    ffn_forward(low_ref, up_ref, bias_ref, act_ref, slope_ref)
    branch_ref[...] = normed + mm(act_ref[...], down_ref[...])


def ffn_other_kernel(
    split,
    cot_ref,
    low_ref,
    act_own_ref,
    branch_ref,
    up_refs,
    down_refs,
    bias_ref,
    down_bias_ref,
    gain_ref,
    shift_ref,
    layer_ref,
    keep_ref,
    send_ref,
    slope_ref,
    up_ref,
    down_ref,
    grad_ref,
    vec_ref,
    act_ref,
    package_ref,
):
    width = cot_ref.shape[1]
    units = up_ref.shape[1]
    if len(up_refs) == 4:
        for ref, index in places(up_refs, place("x")):
            depth = ref.shape[0] * width // units
            for i in range(units // width):
                up_ref[part(index, depth), i * width : (i + 1) * width] = ref[
                    i * depth : (i + 1) * depth, :
                ]
        for ref, index in places(down_refs, z_bit()):
            down_ref[part(index, ref.shape[0]), :] = ref[...]
    else:
        up_ref[...] = up_refs[0][...]
        down_ref[...] = down_refs[0][...]
    ffn_forward(low_ref, up_ref, bias_ref, act_ref, slope_ref)
    resid = branch_ref[...] + mm(act_ref[...], down_ref[...]) + row(down_bias_ref)
    hat, scale = norm_stats(resid)
    layer_ref[...] = (hat * row(gain_ref) + row(shift_ref)).astype(BF16)
    cot = cot_ref[...].astype(F32)
    vec_ref[1:2, :] = jnp.sum(cot * hat, axis=0, keepdims=True)
    vec_ref[2:3, :] = jnp.sum(cot, axis=0, keepdims=True)
    grad = norm_grad(cot * row(gain_ref), hat, scale)
    vec_ref[0:1, :] = jnp.sum(grad, axis=0, keepdims=True)
    grad_ref[...] = grad
    grad_low = grad.astype(BF16)
    for half, act in ((0, act_own_ref), (1, act_ref)):
        for start in range(0, units, CHUNK):
            cols = slice(start, start + CHUNK)
            package_ref[cols, :] = mm_tn(act[:, cols], grad_low).astype(BF16)
        core_split(package_ref, keep_ref, send_ref, half * (units // 2), split)


def ffn_back_kernel(
    split,
    resid_ref,
    grad_ref,
    low_ref,
    slopes,
    ups,
    downs,
    contexts,
    vec_ref,
    gain_ref,
    keep_ref,
    send_ref,
    small_ref,
    grad_resid_ref,
    work_ref,
    total_ref,
    package_ref,
    bias_sum_ref,
    out_ref,
):
    width = resid_ref.shape[1]
    units = ups[0].shape[1]
    half_width = width // 2
    group = (units + half_width) // 2
    grad_low = grad_ref[...].astype(BF16)
    for half in range(2):
        for start in range(0, units, CHUNK):
            cols = slice(start, start + CHUNK)
            grad_act = mm_nt(grad_low, downs[half][cols, :])
            pre_grad = (grad_act * slopes[half][:, cols].astype(F32)).astype(BF16)
            work_ref[:, cols] = pre_grad
            at = half * (units // width) + start // width
            bias_sum_ref[at : at + 1, start % width : start % width + CHUNK] = jnp.sum(
                pre_grad.astype(F32), axis=0, keepdims=True
            )
        for start in range(0, units, width):
            cols = slice(start, start + width)
            package_ref[cols, :] = mm_tn(low_ref[...], work_ref[:, cols]).astype(BF16)
        core_split(package_ref, keep_ref, send_ref, half * group, split)
        before = grad_ref[...] if half == 0 else total_ref[...]
        total_ref[...] = before + mm_nt(work_ref[...], ups[half][...])
    grad = total_ref[...]
    hat, scale = norm_stats(resid_ref[...])
    small_ref[1:2, :] = jnp.sum(grad * hat, axis=0, keepdims=True)
    small_ref[2:3, :] = jnp.sum(grad, axis=0, keepdims=True)
    grad = norm_grad(grad * row(gain_ref), hat, scale)
    small_ref[0:1, :] = jnp.sum(grad, axis=0, keepdims=True)
    grad_low = grad.astype(BF16)
    for half in range(2):
        out_ref[...] = mm_tn(contexts[half][...], grad_low).astype(BF16)
        core_split(out_ref, keep_ref, send_ref, half * group + units // 2, split)
    small_ref[3:6, :] = vec_ref[0:3, :]
    span = units // width
    first_half = (place("mp") if split else 0) == 0
    ours, theirs = bias_sum_ref[0:span, :], bias_sum_ref[span : 2 * span, :]
    small_ref[6 : 6 + span, :] = jnp.where(first_half, ours, theirs)
    small_ref[6 + span : 6 + 2 * span, :] = jnp.where(first_half, theirs, ours)
    used = 6 + 2 * span
    small_ref[used:, :] = jnp.zeros((small_ref.shape[0] - used, width), F32)
    keep_ref[2 * group :, :] = small_ref[...].astype(BF16)
    send_ref[2 * group :, :] = small_ref[...].astype(BF16)
    grad_resid_ref[...] = grad


def half_backward(
    grad_low, weight_ref, out_ref, mixed_ref, early_ref, late_ref, gm_ref, work
):
    grad_context = mm_nt(grad_low, out_ref[...]).astype(BF16)
    attend_backward(
        grad_context, mixed_ref, early_ref, late_ref, grad_low.shape[0] // W_LONG, gm_ref, work
    )
    return (
        mm_nt(gm_ref[0], weight_ref[0])
        + mm_nt(gm_ref[1], weight_ref[1])
        + mm_nt(gm_ref[2], weight_ref[2])
    )


def projection_grads(hidden_low, gm_ref, package_ref, keep_ref, send_ref, split):
    rows, width = hidden_low.shape
    half_width = width // 2
    package_ref[0:width, 0:half_width] = mm_tn(hidden_low, gm_ref[0]).astype(BF16)
    package_ref[0:width, half_width:] = mm_tn(hidden_low, gm_ref[1]).astype(BF16)
    value_grad = mm_tn(hidden_low, gm_ref[2]).astype(BF16)
    package_ref[width : width + half_width, 0:half_width] = value_grad[0:half_width, :]
    package_ref[width : width + half_width, half_width:] = value_grad[half_width:, :]
    core_split(package_ref, keep_ref, send_ref, 0, split)


def attend_back_kernel(
    split,
    win_ref,
    tokens_ref,
    pos_ref,
    grad_resid_ref,
    own_refs,
    other_refs,
    other_keep_ref,
    other_send_ref,
    table_keep_ref,
    table_send_ref,
    tokens_grad_ref,
    hidden_ref,
    own_gm_ref,
    grad_ref,
    gm_ref,
    package_ref,
    table_ref,
    *work,
):
    rows, width = tokens_ref.shape
    windows = read_windows(win_ref, rows)
    hidden_low = hidden_rows(tokens_ref, pos_ref, windows).astype(BF16)
    hidden_ref[...] = hidden_low
    grad_low = grad_resid_ref[...].astype(BF16)
    grad_ref[...] = grad_resid_ref[...] + half_backward(grad_low, *other_refs, gm_ref, work)
    projection_grads(hidden_low, gm_ref, package_ref, other_keep_ref, other_send_ref, split)
    grad_ref[...] += half_backward(grad_low, *own_refs, own_gm_ref, work)
    grad = grad_ref[...]
    tokens_grad_ref[...] = grad.astype(BF16)
    first, second = None, None
    for block, is_long in enumerate(windows):
        top = grad[block * W_LONG : block * W_LONG + W_SHORT]
        bottom = grad[block * W_LONG + W_SHORT : (block + 1) * W_LONG]
        zero = jnp.zeros_like(top)
        part_first = top + jnp.where(is_long, zero, bottom)
        part_second = jnp.where(is_long, bottom, zero)
        first = part_first if first is None else first + part_first
        second = part_second if second is None else second + part_second
    table_ref[0:W_SHORT, :] = first.astype(BF16)
    table_ref[W_SHORT:, :] = second.astype(BF16)
    core_split(table_ref, table_keep_ref, table_send_ref, 0, split)


def project_back_kernel(split, hidden_ref, gm_ref, keep_ref, send_ref, package_ref):
    projection_grads(hidden_ref[...], gm_ref, package_ref, keep_ref, send_ref, split)


def total_of(*values):
    total = values[0].astype(F32)
    for value in values[1:]:
        total = total + value.astype(F32)
    return total


def bit_split(bit, size, terms, keep_ref, send_ref, start=0):
    half = size // 2
    for index, to_ref in ((bit, keep_ref), (1 - bit, send_ref)):
        rows = [pl.ds(pl.multiple_of(first + index * half, 16), half) for _, first in terms]
        to_ref[start : start + half, :] = total_of(
            *[ref[row_range, :] for (ref, _), row_range in zip(terms, rows)]
        ).astype(BF16)


def other_half_kernel(keep_ref, recv_ref, send_ref):
    start = keep_ref.shape[0] - send_ref.shape[0]
    send_ref[...] = total_of(keep_ref[start:, :], recv_ref[start:, :]).astype(BF16)


def down_split_kernel(keep_ref, recv_ref, from_y_ref, x_keep_ref, x_send_ref):
    terms = [(keep_ref, 0), (recv_ref, 0), (from_y_ref, 0)]
    bit_split(place("x"), from_y_ref.shape[0], terms, x_keep_ref, x_send_ref)


def pair_kernel(a_ref, b_ref, out_ref):
    out_ref[...] = total_of(a_ref[...], b_ref[...]).astype(BF16)


def halves_split(bit, keep_ref, recv_ref, to_keep_ref, to_send_ref):
    rows = (keep_ref.shape[0] - EXTRA) // 2
    for half in range(2):
        terms = [(keep_ref, half * rows), (recv_ref, half * rows)]
        bit_split(bit, rows, terms, to_keep_ref, to_send_ref, half * (rows // 2))
    small = total_of(keep_ref[2 * rows :, :], recv_ref[2 * rows :, :]).astype(BF16)
    to_keep_ref[rows:, :] = small
    to_send_ref[rows:, :] = small


def up_split_kernel(keep_ref, recv_ref, z_keep_ref, z_send_ref):
    halves_split(z_bit(), keep_ref, recv_ref, z_keep_ref, z_send_ref)


def down_x_kernel(keep_ref, recv_ref, z_keep_ref, z_send_ref):
    terms = [(keep_ref, 0), (recv_ref, 0)]
    bit_split(z_bit(), keep_ref.shape[0], terms, z_keep_ref, z_send_ref)


def up_x_kernel(keep_ref, recv_ref, x_keep_ref, x_send_ref):
    halves_split(place("x"), keep_ref, recv_ref, x_keep_ref, x_send_ref)


def up_z_kernel(keep_ref, recv_ref, y_keep_ref, y_send_ref):
    rows = y_keep_ref.shape[0] - EXTRA
    y_keep_ref[0:rows, :] = total_of(keep_ref[0:rows, :], recv_ref[0:rows, :]).astype(BF16)
    y_send_ref[...] = total_of(keep_ref[rows:, :], recv_ref[rows:, :]).astype(BF16)
    y_keep_ref[rows:, :] = y_send_ref[rows:, :]


def up_last_kernel(own_ref, recv_ref, out_ref, small_ref):
    rows = out_ref.shape[0]
    out_ref[...] = total_of(own_ref[0:rows, :], recv_ref[0:rows, :]).astype(BF16)
    small_ref[...] = total_of(own_ref[rows:, :], recv_ref[rows:, :])


def small_out_kernel(small_ref, *refs):
    *vector_refs, bias_ref, token_ref = refs
    width = small_ref.shape[1]
    token_ref[...] = jnp.zeros(token_ref.shape, F32)
    for i, ref in enumerate(vector_refs):
        ref[...] = small_ref[i : i + 1, :].reshape(width)
    span = bias_ref.shape[0] // width
    for i in range(span):
        value = small_ref[pl.ds(6 + place("mp") * span + i, 1), :]
        bias_ref[i * width : (i + 1) * width] = value.reshape(width)


def join_kernel(axis, own_ref, recv_ref, out_ref):
    rows = own_ref.shape[0]
    bit = z_bit() if axis == "z" else place("x")
    out_ref[part(bit, rows), :] = own_ref[...]
    out_ref[part(1 - bit, rows), :] = recv_ref[...]


def attend_core_kernel(keep_ref, recv_ref, table_keep_ref, table_recv_ref, to_y_ref, table_ref):
    rows = keep_ref.shape[0]
    to_y_ref[0:rows, :] = total_of(keep_ref[...], recv_ref[...]).astype(BF16)
    terms = [(table_keep_ref, 0), (table_recv_ref, 0)]
    size = table_keep_ref.shape[0]
    bit_split(place("mp"), size, terms, table_ref, to_y_ref.at[rows:, :])


def attend_mp_kernel(keep_ref, recv_ref, from_y_ref, table_ref, x_keep_ref, x_send_ref):
    rows, spare = keep_ref.shape[0], table_ref.shape[0]
    terms = [(keep_ref, 0), (recv_ref, 0), (from_y_ref, 0)]
    bit_split(place("x"), rows, terms, x_keep_ref, x_send_ref)
    terms = [(table_ref, 0), (from_y_ref, rows)]
    bit_split(place("x"), spare, terms, x_keep_ref, x_send_ref, rows // 2)


def attend_x_kernel(spare, keep_ref, recv_ref, z_keep_ref, z_send_ref):
    rows = keep_ref.shape[0] - spare
    for start, size in ((0, rows), (rows, spare)):
        terms = [(keep_ref, start), (recv_ref, start)]
        bit_split(z_bit(), size, terms, z_keep_ref, z_send_ref, start // 2)


def attend_join_kernel(own_ref, recv_ref, out_ref, table_ref):
    spare = table_ref.shape[0] // 2
    rows = own_ref.shape[0] - spare
    for ref, bit in ((own_ref, z_bit()), (recv_ref, 1 - z_bit())):
        out_ref[part(bit, rows), :] = ref[0:rows, :]
        table_ref[part(bit, spare), :] = ref[rows:, :]
    out_ref[2 * rows :, :] = table_ref[...]


def corners(parts, bit):
    own_ref, near_ref, core_own_ref, core_near_ref = parts
    core = place("core")
    return (
        (own_ref, core * 2 + bit),
        (near_ref, core * 2 + 1 - bit),
        (core_own_ref, (1 - core) * 2 + bit),
        (core_near_ref, (1 - core) * 2 + 1 - bit),
    )


def down_out_kernel(*refs):
    *parts, out_ref, token_ref = refs
    token_ref[...] = jnp.zeros(token_ref.shape, F32)
    for ref, index in corners(parts, place("x")):
        out_ref[part(index, ref.shape[0]), :] = ref[...].astype(F32)


def up_out_kernel(*refs):
    *parts, up_ref, out_ref, token_ref, work_ref = refs
    token_ref[...] = jnp.zeros(token_ref.shape, F32)
    for ref, index in corners(parts, z_bit()):
        work_ref[part(index, ref.shape[0]), :] = ref[...]
    width, spare = up_ref.shape[0], out_ref.shape[0] // 2
    for core in range(2):
        start = core * (width + spare)
        up_ref[:, core * width : (core + 1) * width] = work_ref[start : start + width, :].astype(F32)
        start += width
        out_ref[core * spare : (core + 1) * spare, :] = work_ref[start : start + spare, :].astype(F32)


def attend_out_kernel(
    parts, table_parts, qkv_ref, table_ref, work_ref, qkv_out_ref, table_out_ref, sems
):
    y = place("mp")
    spare = table_parts[0].shape[0]
    rows = parts[0].shape[0] - spare
    half = qkv_ref.shape[2]
    width = 2 * half
    for ref, index in corners(parts, place("x")):
        work_ref[part(index, rows), :] = ref[0:rows, :]
        core, x = lax.div(index, 2), lax.rem(index, 2)
        table_out_ref[part(core * 4 + y * 2 + x, spare), :] = ref[rows:, :].astype(F32)
    for ref, index in corners(table_parts, place("x")):
        core, x = lax.div(index, 2), lax.rem(index, 2)
        table_out_ref[part(core * 4 + (1 - y) * 2 + x, spare), :] = ref[...].astype(F32)
    copies = [pltpu.make_async_copy(table_out_ref, table_ref, sems.at[3])]
    copies[0].start()
    for i in range(3):
        if i < 2:
            qkv_out_ref[i] = work_ref[0:width, i * half : (i + 1) * half].astype(F32)
        else:
            qkv_out_ref[i, 0:half, :] = work_ref[width : width + half, 0:half].astype(F32)
            qkv_out_ref[i, half:, :] = work_ref[width : width + half, half:].astype(F32)
        copies.append(pltpu.make_async_copy(qkv_out_ref.at[i], qkv_ref.at[i], sems.at[i]))
        copies[-1].start()
    for copy in copies:
        copy.wait()


def swap(value, axis, name="swap", distance=1):
    pairs = [(i, i ^ distance) for i in range(lax.axis_size(axis))]
    with jax.named_scope(f"{name}_{axis}{distance}"):
        return lax.ppermute(value, axis, pairs)


def swap_corner(value, name):
    with jax.named_scope(name):
        return lax.ppermute(value, ("x", "mp"), [(0, 3), (1, 2), (2, 1), (3, 0)])


class Chain:
    def __init__(self):
        self.last = ()

    def gate(self, value, us=1):
        value = pl.pallas_call(
            lambda *refs: None,
            out_shape=jax.ShapeDtypeStruct(value.shape, value.dtype),
            in_specs=[anywhere] * (1 + len(self.last)),
            out_specs=anywhere,
            input_output_aliases={0: 0},
            compiler_params=pltpu.CompilerParams(vmem_limit_bytes=MIB),
            cost_estimate=pl.CostEstimate(
                flops=us * FLOPS_PER_US, bytes_accessed=0, transcendentals=0
            ),
            name="gate",
        )(value, *self.last)
        self.last = (value,)
        return value

    def __call__(
        self,
        kernel,
        outs,
        args,
        us,
        name,
        scratch=(),
        smem_args=0,
        hbm_args=0,
        copies=0,
        mib=8,
        token=None,
        hbm_outs=False,
    ):
        results = call(
            kernel, outs, args, self.last, scratch, us, mib, smem_args, hbm_args, copies, hbm_outs, name
        )
        if token is None:
            token = min(range(len(results)), key=lambda i: results[i].size)
        self.last = (results[token],)
        return results


def per_device(
    fast,
    mp_size,
    tokens,
    pos_table,
    qkv_weight,
    out_weight,
    out_bias,
    norm1_gain,
    norm1_shift,
    up_weight,
    up_bias,
    down_weight,
    down_bias,
    norm2_gain,
    norm2_shift,
    window,
    cotangent,
):
    step = Chain()
    rows, width = tokens.shape
    blocks = rows // W_LONG
    half_width = width // 2
    units = up_weight.shape[1] * mp_size // 2
    n, spare = width, W_LONG // 2
    group, att = (units + half_width) // 2, 3 * width // 4
    qkv_weight = jnp.transpose(qkv_weight, (1, 0, 2))
    wide = ((rows, width), F32)

    attend_outs = [
        (3, rows, half_width),
        (blocks * half_width // LANES, 2 * W_LONG, W_SHORT),
        (blocks * half_width // LANES, W_LONG, W_SHORT),
        (rows, half_width),
    ]

    def attend_own():
        return step(
            first_kernel,
            attend_outs,
            [window, tokens, pos_table, w_own],
            3,
            "attend_first",
            mib=28,
            smem_args=1,
        )

    def attend_other():
        return step(
            second_kernel,
            attend_outs
            + [wide, (3, width, half_width), (half_width, width), ((units,), F32)],
            [window, tokens, pos_table, attend_in, context_own, out_own, out_bias],
            5,
            "attend_second",
            mib=28,
            smem_args=1,
        )

    def ffn_own():
        return step(
            ffn_own_kernel,
            [(rows, width), (rows, units), (rows, units), wide],
            [resid, up_own, down_own, bias_own, norm1_gain, norm1_shift],
            4,
            "ffn_own",
            mib=28,
        )

    if fast:
        w_own, out_own, up_own, down_own = qkv_weight, out_weight, up_weight, down_weight
        bias_own = up_bias
        (message,) = step(
            pack_attend_kernel,
            [(width // 2 + EXTRA, width)],
            [up_bias, qkv_weight, out_weight],
            1,
            "pack_attend",
            mib=63,
            hbm_args=2,
            copies=5,
        )
        attend_y = swap(message, "mp", "attend_y")
        up_message, down_message = step(
            pack_ffn_kernel,
            [(units // 8, width), (units // 4, width)],
            [up_weight, down_weight],
            1,
            "pack_ffn",
            mib=60,
            hbm_args=2,
            copies=1 + units // width,
        )
        up_y = swap(up_message, "mp", "up_y")
        down_y = swap(down_message, "mp", "down_y")
        mixed_own, early_own, late_own, context_own = attend_own()
        attend_y = step.gate(attend_y, 0)
        attend_x = swap(attend_y, "x", "attend_x")
        attend_cy = swap(attend_y, "core", "attend_cy")
        up_y = step.gate(up_y)
        up_z = swap(up_y, "z", "up_z")
        (up_y,) = step(z_join_kernel, [(units // 4, width)], [up_y, up_z], 0, "up_pair")
        up_x = swap(up_y, "x", "up_x")
        up_cy = swap(up_y, "core", "up_cy")
        attend_x = step.gate(attend_x)
        attend_cx = swap(attend_x, "core", "attend_cx")
        down_y = step.gate(down_y, 2)
        down_z = swap(down_y, "z", "down_z")
        down_cy = swap(down_y, "core", "down_cy")
        attend_in = (attend_y, attend_x, attend_cy, attend_cx)
        mixed_oth, early_oth, late_oth, context_oth, resid, w_oth, out_oth, bias_oth = attend_other()
        low, act_own, slope_own, branch = ffn_own()
        up_x = step.gate(up_x, 0)
        up_cx = swap(up_x, "core", "up_cx")
        down_z = step.gate(down_z, 4)
        down_cz = swap(down_z, "core", "down_cz")
        up_in = (up_y, up_x, up_cy, up_cx)
        down_in = (down_y, down_z, down_cy, down_cz)
    else:
        qkv = lax.all_gather(qkv_weight, "mp", axis=2, tiled=True)
        out_w = lax.all_gather(out_weight, "mp", axis=0, tiled=True)
        up_w = lax.all_gather(up_weight, "mp", axis=1, tiled=True)
        bias = lax.all_gather(up_bias, "mp", axis=0, tiled=True)
        down_w = lax.all_gather(down_weight, "mp", axis=0, tiled=True)
        w_own, out_own = qkv[:, :, :half_width], out_w[:half_width]
        attend_in = (qkv[:, :, half_width:], out_w[half_width:], bias[units:])
        up_own, up_in = up_w[:, :units], (up_w[:, units:],)
        down_own, down_in = down_w[:units], (down_w[units:],)
        bias_own = bias[:units]
        mixed_own, early_own, late_own, context_own = attend_own()
        mixed_oth, early_oth, late_oth, context_oth, resid, w_oth, out_oth, bias_oth = attend_other()
        low, act_own, slope_own, branch = ffn_own()

    layer_out, down_keep, down_send, slope_oth, up_oth, down_oth, grad2, vec = step(
        functools.partial(ffn_other_kernel, fast),
        [
            (rows, width),
            (units, width),
            (units, width),
            (rows, units),
            (width, units),
            (units, width),
            wide,
            ((8, width), F32),
        ],
        [
            cotangent,
            low,
            act_own,
            branch,
            up_in,
            down_in,
            bias_oth,
            down_bias,
            norm2_gain,
            norm2_shift,
        ],
        6,
        "ffn_other",
            mib=28,
        scratch=[((rows, units), BF16), ((units, width), BF16)],
    )
    down_recv = swap(down_send, "core", "down_recv") if fast else None
    up_keep, up_send, small, grad1 = step(
        functools.partial(ffn_back_kernel, fast),
        [
            (2 * group + EXTRA, width),
            (2 * group + EXTRA, width),
            ((EXTRA, width), F32),
            wide,
        ],
        [
            resid,
            grad2,
            low,
            (slope_own, slope_oth),
            (up_own, up_oth),
            (down_own, down_oth),
            (context_own, context_oth),
            vec,
            norm1_gain,
        ],
        6,
        "ffn_back",
            mib=28,
        scratch=[
            ((rows, units), BF16),
            ((rows, width), F32),
            ((units, width), BF16),
            ((8, width), F32),
            ((half_width, width), BF16),
        ],
    )

    def attend_back():
        return step(
            functools.partial(attend_back_kernel, fast),
            [(att, width)] * 2
            + [(spare, width)] * 2
            + [(rows, width)] * 2
            + [(3, rows, half_width)],
            [
                window,
                tokens,
                pos_table,
                grad1,
                (w_own, out_own, mixed_own, early_own, late_own),
                (w_oth, out_oth, mixed_oth, early_oth, late_oth),
            ],
            13,
            "attend_back",
            mib=28,
            scratch=[
                ((rows, width), F32),
                ((3, rows, half_width), BF16),
                ((2 * att, width), BF16),
                ((W_LONG, width), BF16),
                ((half_width // LANES, 2 * W_LONG, W_SHORT), BF16),
                ((half_width // LANES, W_LONG, W_SHORT), BF16),
            ],
            smem_args=1,
        )

    def project_back(hidden, own_gm):
        return step(
            functools.partial(project_back_kernel, fast),
            [(att, width)] * 2,
            [hidden, own_gm],
            0,
            "project_back",
            mib=16,
            scratch=[((2 * att, width), BF16)],
        )

    if not fast:
        *oth_parts, grad_tokens, hidden, own_gm = attend_back()
        att_parts = (*oth_parts[:2], *project_back(hidden, own_gm), *oth_parts[2:])
        qkv_g, out_g, up_g, down_g, small, table = reduce_plain(
            n, width, down_keep, down_send, up_keep, up_send, small, *att_parts
        )
        vectors = [small[i] for i in range(6)]
        bias_all = small[6 : 6 + 2 * units // width].reshape(-1)
        start = lax.axis_index("mp") * up_bias.shape[0]
        bias_g = lax.dynamic_slice_in_dim(bias_all, start, up_bias.shape[0])
    else:
        half, piece, strip = n // 2, n // 4, spare // 2
        up_recv = swap(up_send, "core", "up_recv")
        (to_y,) = step(other_half_kernel, [(n, width)], [down_keep, down_recv], 6, "down_core")
        down_from_y = swap(to_y, "mp", "down_from_y")
        up_x, to_x = step(
            up_split_kernel,
            [(group + EXTRA, width)] * 2,
            [up_keep, up_recv],
            5,
            "up_core",
        )
        up_from_x = swap(to_x, "z", "up_from_z")
        oth_keep, oth_send, tab_keep, tab_send, grad_tokens, hidden, own_gm = attend_back()
        oth_recv = swap(oth_send, "core", "oth_recv")
        tab_recv = swap(tab_send, "core", "tab_recv")
        own_keep, own_send = project_back(hidden, own_gm)
        own_recv = swap(own_send, "core", "own_recv")
        down_x, to_x = step(
            down_split_kernel,
            [(half, width)] * 2,
            [down_keep, down_recv, down_from_y],
            0,
            "down_mp",
        )
        down_from_x = swap(to_x, "x", "down_from_x")
        to_y, table = step(
            attend_core_kernel,
            [(att + strip, width), (strip, width)],
            [oth_keep, oth_recv, tab_keep, tab_recv],
            0,
            "attend_core",
        )
        att_from_y = swap(to_y, "mp", "att_from_y")
        up_z, to_z = step(
            up_x_kernel,
            [(group // 2 + EXTRA, width)] * 2,
            [up_x, up_from_x],
            5,
            "up_x",
        )
        up_from_z = swap(to_z, "x", "up_from_x")
        down_z, to_z = step(
            down_x_kernel,
            [(piece, width)] * 2,
            [down_x, down_from_x],
            3,
            "down_x",
        )
        down_from_z = swap(to_z, "z", "down_from_z")
        (down_z,) = step(pair_kernel, [(piece, width)], [down_z, down_from_z], 0, "down_z")
        down_far = swap(down_z, "z", "down_far", 2)
        att_x, to_x = step(
            attend_mp_kernel,
            [((att + strip) // 2, width)] * 2,
            [own_keep, own_recv, att_from_y, table],
            0,
            "attend_mp",
        )
        att_from_x = swap(to_x, "x", "att_from_x")
        up_y, to_y = step(
            up_z_kernel, [(group // 4 + EXTRA, width)] * 2, [up_z, up_from_z], 3, "up_z"
        )
        up_from_y = swap(to_y, "mp", "up_from_y")
        (down_z,) = step(pair_kernel, [(piece, width)], [down_z, down_far], 0, "down_far")
        down_near = swap(down_z, "z", "down_near")
        att_z, to_z = step(
            functools.partial(attend_x_kernel, strip // 2),
            [((att + strip) // 4, width)] * 2,
            [att_x, att_from_x],
            0,
            "attend_x",
        )
        att_from_z = swap(to_z, "z", "att_from_z")
        (up_y,) = step(pair_kernel, [(group // 4 + EXTRA, width)], [up_y, up_from_y], 0, "up_mp")
        up_far = swap(up_y, "z", "up_far", 2)
        (down_z,) = step(functools.partial(join_kernel, "z"), [(half, width)], [down_z, down_near], 0, "down_join")
        down_x = swap(down_z, "x", "down_x")
        (att_z,) = step(pair_kernel, [att_z.shape], [att_z, att_from_z], 0, "attend_z")
        att_far = swap(att_z, "z", "att_far", 2)
        up_z, small = step(
            up_last_kernel,
            [(group // 4, width), ((EXTRA, width), F32)],
            [up_y, up_far],
            0,
            "up_far",
        )
        up_near = swap(up_z, "x", "up_near")
        (att_z,) = step(pair_kernel, [att_z.shape], [att_z, att_far], 0, "attend_far")
        att_near = swap(att_z, "z", "att_near")
        att_half, table = step(
            attend_join_kernel,
            [((att + strip) // 2, width), (strip // 2, width)],
            [att_z, att_near],
            0,
            "attend_join",
        )
        att_x = swap(att_half, "x", "att_x")
        table_y = swap(table, "mp", "table_y")
        table_x = swap_corner(table, "table_x")
        (up_z,) = step(functools.partial(join_kernel, "x"), [(group // 2, width)], [up_z, up_near], 0, "up_join")
        up_x = swap(up_z, "z", "up_last")
        down_x = step.gate(down_x, 0)
        *vectors, bias_g, _ = step(
            small_out_kernel,
            [((width,), F32)] * 6 + [((up_bias.shape[0],), F32), ((8, LANES), F32)],
            [small],
            0,
            "small_out",
            token=7,
        )
        down_g, _ = step(
            down_out_kernel,
            [((2 * n, width), F32), ((8, LANES), F32)],
            [
                down_z,
                down_x,
                swap(down_z, "core", "down_core"),
                swap(down_x, "core", "down_core_x"),
            ],
            0,
            "down_out",
        )
        table_y = step.gate(table_y, 0)
        up_x = step.gate(up_x, 0)
        table_x = step.gate(table_x, 2)
        att_x = step.gate(att_x, 1)
        up_g, out_g, _ = step(
            up_out_kernel,
            [((width, 2 * n), F32), ((half_width, width), F32), ((8, LANES), F32)],
            [up_z, up_x, swap(up_z, "core", "up_core"), swap(up_x, "core", "up_core_x")],
            0,
            "up_out",
            scratch=[((2 * group, width), BF16)],
        )
        qkv_g, table = step(
            attend_out_kernel,
            [((3, width, half_width), F32), ((W_LONG, width), F32)],
            [
                (
                    att_half,
                    att_x,
                    swap(att_half, "core", "att_core"),
                    swap(att_x, "core", "att_core_x"),
                ),
                (
                    table_y,
                    table_x,
                    swap(table_y, "core", "table_core"),
                    swap(table_x, "core", "table_core_x"),
                ),
            ],
            0,
            "attend_out",
            scratch=[
                ((2 * att, width), BF16),
                ((3, width, half_width), F32),
                ((W_LONG, width), F32),
            ],
            copies=4,
            hbm_outs=True,
        )


    return (
        layer_out,
        grad_tokens,
        table,
        jnp.transpose(qkv_g, (1, 0, 2)),
        out_g,
        vectors[0],
        vectors[1],
        vectors[2],
        up_g,
        bias_g,
        down_g,
        vectors[3],
        vectors[4],
        vectors[5],
    )


def reduce_plain(
    n,
    width,
    down_keep,
    down_send,
    up_keep,
    up_send,
    small,
    other_keep,
    other_send,
    own_keep,
    own_send,
    table_keep,
    table_send,
):
    half, spare = n // 2, n // 4
    group = n + spare

    def rows_of(start, size):
        return lambda keep, send: jnp.concatenate(
            [keep[start : start + size], send[start : start + size]], axis=0
        )

    def summed(own, oth, dim):
        whole = jnp.concatenate([own, oth], axis=dim)
        part_sum = lax.psum_scatter(whole, "mp", scatter_dimension=dim, tiled=True)
        return lax.psum(part_sum, "dp").astype(F32)

    def qkv_part(g):
        value = jnp.concatenate([g[n : n + half, :half], g[n : n + half, half:]], axis=0)
        return jnp.stack([g[:n, :half], g[:n, half:], value])

    def up_part(g):
        return jnp.concatenate([g[:n], g[n:]], axis=1)

    down = [rows_of(start, n)(down_keep, down_send) for start in (0, n)]
    up = [up_part(rows_of(start, n)(up_keep, up_send)) for start in (0, group)]
    out = [rows_of(start + n, spare)(up_keep, up_send) for start in (0, group)]
    att = [
        qkv_part(jnp.concatenate(pair, axis=0))
        for pair in ((own_keep, own_send), (other_keep, other_send))
    ]
    table = jnp.concatenate([table_keep, table_send], axis=0).astype(F32)
    return (
        summed(*att, 2),
        summed(*out, 0),
        summed(*up, 1),
        summed(*down, 0),
        lax.psum(small, ("dp", "mp")),
        lax.psum(table, ("dp", "mp")),
    )


def solution(mesh):
    mp_size = mesh.shape["mp"]
    fast = mp_size == 2 and mesh.shape["dp"] == 16
    dp = "dp"
    if fast:
        shape = (mesh.shape["dp"] // 4, 2, 2, mp_size)
        mesh = Mesh(mesh.devices.reshape(shape), ("z", "x", "core", "mp"))
        dp = ("z", "x", "core")
    both = P((*dp, "mp") if fast else (dp, "mp"), None)
    placed = (
        both,
        P(),
        P(None, None, "mp"),
        P("mp", None),
        P(),
        P(),
        P(),
        P(None, "mp"),
        P("mp"),
        P("mp", None),
        P(),
        P(),
        P(),
        P(dp),
        both,
    )
    return jax.shard_map(
        functools.partial(per_device, fast, mp_size),
        mesh=mesh,
        in_specs=placed,
        out_specs=(
            both,
            both,
            P(),
            P(None, None, "mp"),
            P("mp", None),
            P(),
            P(),
            P(),
            P(None, "mp"),
            P("mp"),
            P("mp", None),
            P(),
            P(),
            P(),
        ),
        check_vma=False,
    )
```

```python
import functools

import jax
import jax.numpy as jnp
from jax import lax
from jax.experimental import pallas as pl
from jax.experimental.pallas import tpu as pltpu
from jax.sharding import Mesh
from jax.sharding import PartitionSpec as P

HD = 64
W_SHORT = 256
W_LONG = 512
ROW = 1024
LANES = 128
EXTRA = 16
CHUNK = 256
EPSILON = 1e-05
MASKED = -1e30
F32 = jnp.float32
BF16 = jnp.bfloat16
MIB = 1024 * 1024
FLOPS_PER_US = 10**9

vmem = pl.BlockSpec(memory_space=pltpu.VMEM)
smem = pl.BlockSpec(memory_space=pltpu.SMEM)
anywhere = pl.BlockSpec(memory_space=pl.ANY)


def call(
    kernel, outs, args, after=(), scratch=(), us=1, mib=32, smem_args=0, hbm_args=0, copies=0, hbm_outs=False, name=None
):
    flat, tree = jax.tree.flatten(tuple(args))
    count, extra = len(flat), len(after)

    def flat_kernel(*refs):
        kernel(*jax.tree.unflatten(tree, refs[:count]), *refs[count + extra :])

    return pl.pallas_call(
        flat_kernel,
        out_shape=[
            jax.ShapeDtypeStruct(out, BF16) if isinstance(out[0], int) else jax.ShapeDtypeStruct(*out)
            for out in outs
        ],
        in_specs=[smem] * smem_args
        + [vmem] * (count - smem_args - hbm_args)
        + [anywhere] * (hbm_args + extra),
        out_specs=[anywhere if hbm_outs else vmem] * len(outs),
        scratch_shapes=[pltpu.VMEM(shape, dtype) for shape, dtype in scratch]
        + [pltpu.SemaphoreType.DMA((copies,))] * (copies > 0),
        compiler_params=pltpu.CompilerParams(vmem_limit_bytes=mib * MIB),
        cost_estimate=pl.CostEstimate(
            flops=us * FLOPS_PER_US, bytes_accessed=0, transcendentals=0
        ),
        name=name,
    )(*flat, *after)


def place(axis):
    return lax.axis_index(axis)


def row(ref, start=0, size=None):
    size = ref.shape[0] if size is None else size
    return ref[start : start + size].astype(F32).reshape(1, size)


def mm(a, b):
    return lax.dot_general(a, b, (((1,), (0,)), ((), ())), preferred_element_type=F32)


def mm_nt(a, b):
    return lax.dot_general(a, b, (((1,), (1,)), ((), ())), preferred_element_type=F32)


def mm_tn(a, b):
    return lax.dot_general(a, b, (((0,), (0,)), ((), ())), preferred_element_type=F32)


def position_rows(pos_ref, is_long):
    first = pos_ref[0:W_SHORT, :].astype(F32)
    second = jnp.where(is_long, pos_ref[W_SHORT:W_LONG, :].astype(F32), first)
    return first, second


def hidden_rows(tokens_ref, pos_ref, windows):
    parts = []
    for block, is_long in enumerate(windows):
        first, second = position_rows(pos_ref, is_long)
        start = block * W_LONG
        parts.append(tokens_ref[start : start + W_SHORT, :].astype(F32) + first)
        parts.append(tokens_ref[start + W_SHORT : start + W_LONG, :].astype(F32) + second)
    return jnp.concatenate(parts, axis=0)


def read_windows(win_ref, rows):
    first = place("mp") * rows
    return [
        win_ref[lax.div(first + block * W_LONG, ROW)] == W_LONG for block in range(rows // W_LONG)
    ]


def norm_stats(values):
    average = jnp.mean(values, axis=-1, keepdims=True)
    centred = values - average
    variance = jnp.mean(centred * centred, axis=-1, keepdims=True)
    scale = lax.rsqrt(variance + EPSILON)
    return centred * scale, scale


def norm_grad(grad_hat, hat, scale):
    mean_grad = jnp.mean(grad_hat, axis=-1, keepdims=True)
    mean_both = jnp.mean(grad_hat * hat, axis=-1, keepdims=True)
    return scale * (grad_hat - mean_grad - hat * mean_both)


def head_mask(rows):
    return lax.broadcasted_iota(jnp.int32, (rows, LANES), 1) < HD


def stack_heads(value, is_low):
    zero = jnp.zeros_like(value)
    return jnp.concatenate(
        [jnp.where(is_low, value, zero), jnp.where(is_low, zero, value)], axis=0
    )


def late_rows(value):
    return jnp.concatenate(
        [value[W_SHORT:W_LONG], value[W_LONG + W_SHORT : 2 * W_LONG]], axis=0
    )


def merge_heads(first, late, is_low):
    top = jnp.where(is_low, first[0:W_SHORT], first[W_LONG : W_LONG + W_SHORT])
    bottom = jnp.where(
        is_low,
        first[W_SHORT:W_LONG] + late[0:W_SHORT],
        first[W_LONG + W_SHORT :] + late[W_SHORT:],
    )
    return top, bottom


def attend_forward(hidden_low, weight_ref, windows, mixed_ref, early_ref, late_ref, context_ref):
    rows, width = context_ref.shape
    pairs = width // LANES
    for c in range(3):
        part = mm(hidden_low, weight_ref[c]).astype(BF16)
        mixed_ref[c] = part * BF16(HD**-0.5) if c == 0 else part
    causal = lax.broadcasted_iota(jnp.int32, (W_SHORT, W_SHORT), 0) >= lax.broadcasted_iota(
        jnp.int32, (W_SHORT, W_SHORT), 1
    )
    is_low = head_mask(W_LONG)
    for block, is_long in enumerate(windows):
        both = slice(block * W_LONG, (block + 1) * W_LONG)
        lo = slice(block * W_LONG, block * W_LONG + W_SHORT)
        hi = slice(block * W_LONG + W_SHORT, (block + 1) * W_LONG)
        for pair in range(pairs):
            lanes = slice(pair * LANES, (pair + 1) * LANES)
            slot = block * pairs + pair
            queries = stack_heads(mixed_ref[0, both, lanes], is_low)
            scores = mm_nt(queries, mixed_ref[1, lo, lanes])
            late = mm_nt(late_rows(queries), mixed_ref[1, hi, lanes])
            for head in range(2):
                start = head * W_LONG
                s_a = jnp.where(causal, scores[start : start + W_SHORT], MASKED)
                e_a = jnp.exp(s_a - jnp.max(s_a, axis=-1, keepdims=True))
                p_a = e_a * (1.0 / jnp.sum(e_a, axis=-1, keepdims=True))
                s_b = jnp.where(is_long, scores[start + W_SHORT : start + W_LONG], MASKED)
                s_c = jnp.where(causal, late[head * W_SHORT : (head + 1) * W_SHORT], MASKED)
                top = jnp.max(jnp.maximum(s_b, s_c), axis=-1, keepdims=True)
                e_b = jnp.exp(s_b - top)
                e_c = jnp.exp(s_c - top)
                inverse = 1.0 / jnp.sum(e_b + e_c, axis=-1, keepdims=True)
                early_ref[slot, start : start + W_SHORT, :] = p_a.astype(BF16)
                early_ref[slot, start + W_SHORT : start + W_LONG, :] = (e_b * inverse).astype(BF16)
                late_ref[slot, head * W_SHORT : (head + 1) * W_SHORT, :] = (e_c * inverse).astype(
                    BF16
                )
            top_rows, bottom_rows = merge_heads(
                mm(early_ref[slot], mixed_ref[2, lo, lanes]),
                mm(late_ref[slot], mixed_ref[2, hi, lanes]),
                head_mask(W_SHORT),
            )
            context_ref[lo, lanes] = top_rows.astype(BF16)
            context_ref[hi, lanes] = bottom_rows.astype(BF16)


def attend_backward(grad_context, mixed_ref, early_ref, late_ref, blocks, grad_mixed_ref, work):
    width = mixed_ref.shape[2]
    pairs = width // LANES
    is_low = head_mask(W_LONG)
    early_grad_ref, late_grad_ref = work
    for block in range(blocks):
        both = slice(block * W_LONG, (block + 1) * W_LONG)
        lo = slice(block * W_LONG, block * W_LONG + W_SHORT)
        hi = slice(block * W_LONG + W_SHORT, (block + 1) * W_LONG)
        for pair in range(pairs):
            lanes = slice(pair * LANES, (pair + 1) * LANES)
            slot = block * pairs + pair
            queries = stack_heads(mixed_ref[0, both, lanes], is_low)
            grads = stack_heads(grad_context[both, lanes], is_low)
            grad_early = mm_nt(grads, mixed_ref[2, lo, lanes])
            grad_late = mm_nt(late_rows(grads), mixed_ref[2, hi, lanes])
            for head in range(2):
                start = head * W_LONG
                first = slice(start, start + W_SHORT)
                second = slice(start + W_SHORT, start + W_LONG)
                last = slice(head * W_SHORT, (head + 1) * W_SHORT)
                p_a = early_ref[slot, first, :].astype(F32)
                g_a = grad_early[first]
                inner = jnp.sum(p_a * g_a, axis=-1, keepdims=True)
                early_grad_ref[pair, first, :] = (p_a * (g_a - inner)).astype(BF16)
                p_b, p_c = early_ref[slot, second, :].astype(F32), late_ref[slot, last, :].astype(F32)
                g_b, g_c = grad_early[second], grad_late[last]
                inner = jnp.sum(p_b * g_b + p_c * g_c, axis=-1, keepdims=True)
                early_grad_ref[pair, second, :] = (p_b * (g_b - inner)).astype(BF16)
                late_grad_ref[pair, last, :] = (p_c * (g_c - inner)).astype(BF16)
            top_rows, bottom_rows = merge_heads(
                mm(early_grad_ref[pair], mixed_ref[1, lo, lanes]),
                mm(late_grad_ref[pair], mixed_ref[1, hi, lanes]),
                head_mask(W_SHORT),
            )
            grad_mixed_ref[0, lo, lanes] = (top_rows * HD**-0.5).astype(BF16)
            grad_mixed_ref[0, hi, lanes] = (bottom_rows * HD**-0.5).astype(BF16)
            grad_mixed_ref[1, lo, lanes] = mm_tn(early_grad_ref[pair], queries).astype(BF16)
            grad_mixed_ref[1, hi, lanes] = mm_tn(late_grad_ref[pair], late_rows(queries)).astype(BF16)
            grad_mixed_ref[2, lo, lanes] = mm_tn(early_ref[slot], grads).astype(BF16)
            grad_mixed_ref[2, hi, lanes] = mm_tn(late_ref[slot], late_rows(grads)).astype(BF16)


def normal_parts(x):
    density = jnp.exp2(x * x * -0.7213475204 - 1.3257480647)
    return 0.5 + 0.5 * lax.erf(x * 0.7071067812), density


def first_kernel(
    win_ref, tokens_ref, pos_ref, weight_ref, mixed_ref, early_ref, late_ref, context_ref
):
    windows = read_windows(win_ref, tokens_ref.shape[0])
    hidden_low = hidden_rows(tokens_ref, pos_ref, windows).astype(BF16)
    attend_forward(
        hidden_low, weight_ref, windows, mixed_ref, early_ref, late_ref, context_ref
    )


def z_bit():
    return lax.rem(place("z"), 2)


def quarter(bit):
    return place("core") * 2 + bit


def part(index, size):
    return pl.ds(pl.multiple_of(index * size, size), size)


def copy_all(pairs, sems):
    copies = [
        pltpu.make_async_copy(src, dst, sems.at[i]) for i, (src, dst) in enumerate(pairs)
    ]
    for copy in copies:
        copy.start()
    for copy in copies:
        copy.wait()


def pack_attend_kernel(bias_ref, qkv_ref, out_ref, send_ref, sems):
    _, width, half = qkv_ref.shape
    depth, mine = width // 4, quarter(place("x"))
    for i in range(EXTRA):
        index = i if (i + 1) * width <= bias_ref.shape[0] else 0
        send_ref[2 * depth + i : 2 * depth + i + 1, :] = row(bias_ref, index * width, width).astype(
            BF16
        )
    middle = depth + depth // 2
    low, high = pl.ds(0, half), pl.ds(half, half)
    upper, lower = part(mine * 2, depth // 2), part(mine * 2 + 1, depth // 2)
    copy_all(
        [
            (qkv_ref.at[0, part(mine, depth), :], send_ref.at[pl.ds(0, depth), low]),
            (qkv_ref.at[1, part(mine, depth), :], send_ref.at[pl.ds(0, depth), high]),
            (qkv_ref.at[2, upper, :], send_ref.at[pl.ds(depth, depth // 2), low]),
            (qkv_ref.at[2, lower, :], send_ref.at[pl.ds(depth, depth // 2), high]),
            (out_ref.at[part(mine, depth // 2), :], send_ref.at[pl.ds(middle, depth // 2), :]),
        ],
        sems,
    )


def pack_ffn_kernel(up_ref, down_ref, up_to, down_to, sems):
    width, units = up_ref.shape
    depth = width // 8
    mine = part(quarter(place("x")) * 2 + z_bit(), depth)
    columns = [
        (up_ref.at[mine, pl.ds(i * width, width)], up_to.at[pl.ds(i * depth, depth), :])
        for i in range(units // width)
    ]
    copy_all([*columns, (down_ref.at[part(quarter(z_bit()), units // 4), :], down_to)], sems)


def z_join_kernel(own_ref, near_ref, out_ref):
    depth = own_ref.shape[0] // 2
    for ref, bit in ((own_ref, z_bit()), (near_ref, 1 - z_bit())):
        for i in range(2):
            rows = pl.ds(pl.multiple_of(i * 2 * depth + bit * depth, depth), depth)
            out_ref[rows, :] = ref[i * depth : (i + 1) * depth, :]


def places(pieces, bit):
    from_y, from_near, core_y, core_near = pieces
    core = place("core")
    return (
        (from_y, core * 2 + bit),
        (from_near, core * 2 + 1 - bit),
        (core_y, (1 - core) * 2 + bit),
        (core_near, (1 - core) * 2 + 1 - bit),
    )


def second_kernel(
    win_ref,
    tokens_ref,
    pos_ref,
    pieces,
    context_own_ref,
    out_own_ref,
    out_bias_ref,
    mixed_ref,
    early_ref,
    late_ref,
    context_ref,
    resid_ref,
    w_oth_ref,
    out_oth_ref,
    bias_oth_ref,
):
    width = tokens_ref.shape[1]
    half, depth = width // 2, width // 4
    windows = read_windows(win_ref, tokens_ref.shape[0])
    if len(pieces) == 4:
        for ref, index in places(pieces, place("x")):
            rows = part(index, depth)
            w_oth_ref[0, rows, :] = ref[0:depth, 0:half]
            w_oth_ref[1, rows, :] = ref[0:depth, half:]
            middle = depth + depth // 2
            w_oth_ref[2, part(index * 2, depth // 2), :] = ref[depth:middle, 0:half]
            w_oth_ref[2, part(index * 2 + 1, depth // 2), :] = ref[depth:middle, half:]
            out_oth_ref[part(index, depth // 2), :] = ref[middle : 2 * depth, :]
        for i in range(bias_oth_ref.shape[0] // width):
            bias_row = pieces[0][2 * depth + i : 2 * depth + i + 1, :].astype(F32)
            bias_oth_ref[i * width : (i + 1) * width] = bias_row.reshape(width)
    else:
        w_oth_ref[...] = pieces[0][...]
        out_oth_ref[...] = pieces[1][...]
        bias_oth_ref[...] = pieces[2][...].astype(F32)
    hidden_in = hidden_rows(tokens_ref, pos_ref, windows)
    attend_forward(
        hidden_in.astype(BF16),
        w_oth_ref,
        windows,
        mixed_ref,
        early_ref,
        late_ref,
        context_ref,
    )
    branch = mm(context_own_ref[...], out_own_ref[...]) + mm(context_ref[...], out_oth_ref[...])
    hidden_in = hidden_rows(tokens_ref, pos_ref, windows)
    resid_ref[...] = hidden_in + branch + row(out_bias_ref)


def core_split(whole_ref, keep_ref, send_ref, start, split):
    half = whole_ref.shape[0] // 2
    core = place("core") if split else 0
    keep_ref[start : start + half, :] = whole_ref[part(core, half), :]
    send_ref[start : start + half, :] = whole_ref[part(1 - core, half), :]


def ffn_forward(low_ref, up_ref, bias_ref, act_ref, slope_ref):
    for start in range(0, up_ref.shape[1], CHUNK):
        cols = slice(start, start + CHUNK)
        pre = mm(low_ref[...], up_ref[:, cols]) + row(bias_ref, start, CHUNK)
        total, density = normal_parts(pre)
        act_ref[:, cols] = (pre * total).astype(BF16)
        slope_ref[:, cols] = (total + pre * density).astype(BF16)


def ffn_own_kernel(
    resid_ref,
    up_ref,
    down_ref,
    bias_ref,
    gain_ref,
    shift_ref,
    low_ref,
    act_ref,
    slope_ref,
    branch_ref,
):
    hat, _ = norm_stats(resid_ref[...])
    normed = hat * row(gain_ref) + row(shift_ref)
    low_ref[...] = normed.astype(BF16)
    ffn_forward(low_ref, up_ref, bias_ref, act_ref, slope_ref)
    branch_ref[...] = normed + mm(act_ref[...], down_ref[...])


def ffn_other_kernel(
    split,
    cot_ref,
    low_ref,
    act_own_ref,
    branch_ref,
    up_refs,
    down_refs,
    bias_ref,
    down_bias_ref,
    gain_ref,
    shift_ref,
    layer_ref,
    keep_ref,
    send_ref,
    slope_ref,
    up_ref,
    down_ref,
    grad_ref,
    vec_ref,
    act_ref,
    package_ref,
):
    width = cot_ref.shape[1]
    units = up_ref.shape[1]
    if len(up_refs) == 4:
        for ref, index in places(up_refs, place("x")):
            depth = ref.shape[0] * width // units
            for i in range(units // width):
                up_ref[part(index, depth), i * width : (i + 1) * width] = ref[
                    i * depth : (i + 1) * depth, :
                ]
        for ref, index in places(down_refs, z_bit()):
            down_ref[part(index, ref.shape[0]), :] = ref[...]
    else:
        up_ref[...] = up_refs[0][...]
        down_ref[...] = down_refs[0][...]
    ffn_forward(low_ref, up_ref, bias_ref, act_ref, slope_ref)
    resid = branch_ref[...] + mm(act_ref[...], down_ref[...]) + row(down_bias_ref)
    hat, scale = norm_stats(resid)
    layer_ref[...] = (hat * row(gain_ref) + row(shift_ref)).astype(BF16)
    cot = cot_ref[...].astype(F32)
    vec_ref[1:2, :] = jnp.sum(cot * hat, axis=0, keepdims=True)
    vec_ref[2:3, :] = jnp.sum(cot, axis=0, keepdims=True)
    grad = norm_grad(cot * row(gain_ref), hat, scale)
    vec_ref[0:1, :] = jnp.sum(grad, axis=0, keepdims=True)
    grad_ref[...] = grad
    grad_low = grad.astype(BF16)
    for half, act in ((0, act_own_ref), (1, act_ref)):
        for start in range(0, units, CHUNK):
            cols = slice(start, start + CHUNK)
            package_ref[cols, :] = mm_tn(act[:, cols], grad_low).astype(BF16)
        core_split(package_ref, keep_ref, send_ref, half * (units // 2), split)


def ffn_back_kernel(
    split,
    resid_ref,
    grad_ref,
    low_ref,
    slopes,
    ups,
    downs,
    contexts,
    vec_ref,
    gain_ref,
    keep_ref,
    send_ref,
    small_ref,
    grad_resid_ref,
    work_ref,
    total_ref,
    package_ref,
    bias_sum_ref,
    out_ref,
):
    width = resid_ref.shape[1]
    units = ups[0].shape[1]
    half_width = width // 2
    group = (units + half_width) // 2
    grad_low = grad_ref[...].astype(BF16)
    for half in range(2):
        for start in range(0, units, CHUNK):
            cols = slice(start, start + CHUNK)
            grad_act = mm_nt(grad_low, downs[half][cols, :])
            pre_grad = (grad_act * slopes[half][:, cols].astype(F32)).astype(BF16)
            work_ref[:, cols] = pre_grad
            at = half * (units // width) + start // width
            bias_sum_ref[at : at + 1, start % width : start % width + CHUNK] = jnp.sum(
                pre_grad.astype(F32), axis=0, keepdims=True
            )
        for start in range(0, units, width):
            cols = slice(start, start + width)
            package_ref[cols, :] = mm_tn(low_ref[...], work_ref[:, cols]).astype(BF16)
        core_split(package_ref, keep_ref, send_ref, half * group, split)
        before = grad_ref[...] if half == 0 else total_ref[...]
        total_ref[...] = before + mm_nt(work_ref[...], ups[half][...])
    grad = total_ref[...]
    hat, scale = norm_stats(resid_ref[...])
    small_ref[1:2, :] = jnp.sum(grad * hat, axis=0, keepdims=True)
    small_ref[2:3, :] = jnp.sum(grad, axis=0, keepdims=True)
    grad = norm_grad(grad * row(gain_ref), hat, scale)
    small_ref[0:1, :] = jnp.sum(grad, axis=0, keepdims=True)
    grad_low = grad.astype(BF16)
    for half in range(2):
        out_ref[...] = mm_tn(contexts[half][...], grad_low).astype(BF16)
        core_split(out_ref, keep_ref, send_ref, half * group + units // 2, split)
    small_ref[3:6, :] = vec_ref[0:3, :]
    span = units // width
    first_half = (place("mp") if split else 0) == 0
    ours, theirs = bias_sum_ref[0:span, :], bias_sum_ref[span : 2 * span, :]
    small_ref[6 : 6 + span, :] = jnp.where(first_half, ours, theirs)
    small_ref[6 + span : 6 + 2 * span, :] = jnp.where(first_half, theirs, ours)
    used = 6 + 2 * span
    small_ref[used:, :] = jnp.zeros((small_ref.shape[0] - used, width), F32)
    keep_ref[2 * group :, :] = small_ref[...].astype(BF16)
    send_ref[2 * group :, :] = small_ref[...].astype(BF16)
    grad_resid_ref[...] = grad


def half_backward(
    grad_low, weight_ref, out_ref, mixed_ref, early_ref, late_ref, gm_ref, work
):
    grad_context = mm_nt(grad_low, out_ref[...]).astype(BF16)
    attend_backward(
        grad_context, mixed_ref, early_ref, late_ref, grad_low.shape[0] // W_LONG, gm_ref, work
    )
    return (
        mm_nt(gm_ref[0], weight_ref[0])
        + mm_nt(gm_ref[1], weight_ref[1])
        + mm_nt(gm_ref[2], weight_ref[2])
    )


def projection_grads(hidden_low, gm_ref, package_ref, keep_ref, send_ref, split):
    rows, width = hidden_low.shape
    half_width = width // 2
    package_ref[0:width, 0:half_width] = mm_tn(hidden_low, gm_ref[0]).astype(BF16)
    package_ref[0:width, half_width:] = mm_tn(hidden_low, gm_ref[1]).astype(BF16)
    value_grad = mm_tn(hidden_low, gm_ref[2]).astype(BF16)
    package_ref[width : width + half_width, 0:half_width] = value_grad[0:half_width, :]
    package_ref[width : width + half_width, half_width:] = value_grad[half_width:, :]
    core_split(package_ref, keep_ref, send_ref, 0, split)


def attend_back_kernel(
    split,
    win_ref,
    tokens_ref,
    pos_ref,
    grad_resid_ref,
    own_refs,
    other_refs,
    other_keep_ref,
    other_send_ref,
    table_keep_ref,
    table_send_ref,
    tokens_grad_ref,
    hidden_ref,
    own_gm_ref,
    grad_ref,
    gm_ref,
    package_ref,
    table_ref,
    *work,
):
    rows, width = tokens_ref.shape
    windows = read_windows(win_ref, rows)
    hidden_low = hidden_rows(tokens_ref, pos_ref, windows).astype(BF16)
    hidden_ref[...] = hidden_low
    grad_low = grad_resid_ref[...].astype(BF16)
    grad_ref[...] = grad_resid_ref[...] + half_backward(grad_low, *other_refs, gm_ref, work)
    projection_grads(hidden_low, gm_ref, package_ref, other_keep_ref, other_send_ref, split)
    grad_ref[...] += half_backward(grad_low, *own_refs, own_gm_ref, work)
    grad = grad_ref[...]
    tokens_grad_ref[...] = grad.astype(BF16)
    first, second = None, None
    for block, is_long in enumerate(windows):
        top = grad[block * W_LONG : block * W_LONG + W_SHORT]
        bottom = grad[block * W_LONG + W_SHORT : (block + 1) * W_LONG]
        zero = jnp.zeros_like(top)
        part_first = top + jnp.where(is_long, zero, bottom)
        part_second = jnp.where(is_long, bottom, zero)
        first = part_first if first is None else first + part_first
        second = part_second if second is None else second + part_second
    table_ref[0:W_SHORT, :] = first.astype(BF16)
    table_ref[W_SHORT:, :] = second.astype(BF16)
    core_split(table_ref, table_keep_ref, table_send_ref, 0, split)


def project_back_kernel(split, hidden_ref, gm_ref, keep_ref, send_ref, package_ref):
    projection_grads(hidden_ref[...], gm_ref, package_ref, keep_ref, send_ref, split)


def total_of(*values):
    total = values[0].astype(F32)
    for value in values[1:]:
        total = total + value.astype(F32)
    return total


def bit_split(bit, size, terms, keep_ref, send_ref, start=0):
    half = size // 2
    for index, to_ref in ((bit, keep_ref), (1 - bit, send_ref)):
        rows = [pl.ds(pl.multiple_of(first + index * half, 16), half) for _, first in terms]
        to_ref[start : start + half, :] = total_of(
            *[ref[row_range, :] for (ref, _), row_range in zip(terms, rows)]
        ).astype(BF16)


def other_half_kernel(keep_ref, recv_ref, send_ref):
    start = keep_ref.shape[0] - send_ref.shape[0]
    send_ref[...] = total_of(keep_ref[start:, :], recv_ref[start:, :]).astype(BF16)


def down_split_kernel(keep_ref, recv_ref, from_y_ref, x_keep_ref, x_send_ref):
    terms = [(keep_ref, 0), (recv_ref, 0), (from_y_ref, 0)]
    bit_split(place("x"), from_y_ref.shape[0], terms, x_keep_ref, x_send_ref)


def pair_kernel(a_ref, b_ref, out_ref):
    out_ref[...] = total_of(a_ref[...], b_ref[...]).astype(BF16)


def halves_split(bit, keep_ref, recv_ref, to_keep_ref, to_send_ref):
    rows = (keep_ref.shape[0] - EXTRA) // 2
    for half in range(2):
        terms = [(keep_ref, half * rows), (recv_ref, half * rows)]
        bit_split(bit, rows, terms, to_keep_ref, to_send_ref, half * (rows // 2))
    small = total_of(keep_ref[2 * rows :, :], recv_ref[2 * rows :, :]).astype(BF16)
    to_keep_ref[rows:, :] = small
    to_send_ref[rows:, :] = small


def up_split_kernel(keep_ref, recv_ref, z_keep_ref, z_send_ref):
    halves_split(z_bit(), keep_ref, recv_ref, z_keep_ref, z_send_ref)


def down_x_kernel(keep_ref, recv_ref, z_keep_ref, z_send_ref):
    terms = [(keep_ref, 0), (recv_ref, 0)]
    bit_split(z_bit(), keep_ref.shape[0], terms, z_keep_ref, z_send_ref)


def up_x_kernel(keep_ref, recv_ref, x_keep_ref, x_send_ref):
    halves_split(place("x"), keep_ref, recv_ref, x_keep_ref, x_send_ref)


def up_z_kernel(keep_ref, recv_ref, y_keep_ref, y_send_ref):
    rows = y_keep_ref.shape[0] - EXTRA
    y_keep_ref[0:rows, :] = total_of(keep_ref[0:rows, :], recv_ref[0:rows, :]).astype(BF16)
    y_send_ref[...] = total_of(keep_ref[rows:, :], recv_ref[rows:, :]).astype(BF16)
    y_keep_ref[rows:, :] = y_send_ref[rows:, :]


def up_last_kernel(own_ref, recv_ref, out_ref, small_ref):
    rows = out_ref.shape[0]
    out_ref[...] = total_of(own_ref[0:rows, :], recv_ref[0:rows, :]).astype(BF16)
    small_ref[...] = total_of(own_ref[rows:, :], recv_ref[rows:, :])


def small_out_kernel(small_ref, *refs):
    *vector_refs, bias_ref, token_ref = refs
    width = small_ref.shape[1]
    token_ref[...] = jnp.zeros(token_ref.shape, F32)
    for i, ref in enumerate(vector_refs):
        ref[...] = small_ref[i : i + 1, :].reshape(width)
    span = bias_ref.shape[0] // width
    for i in range(span):
        value = small_ref[pl.ds(6 + place("mp") * span + i, 1), :]
        bias_ref[i * width : (i + 1) * width] = value.reshape(width)


def join_kernel(axis, own_ref, recv_ref, out_ref):
    rows = own_ref.shape[0]
    bit = z_bit() if axis == "z" else place("x")
    out_ref[part(bit, rows), :] = own_ref[...]
    out_ref[part(1 - bit, rows), :] = recv_ref[...]


def attend_core_kernel(keep_ref, recv_ref, table_keep_ref, table_recv_ref, to_y_ref, table_ref):
    rows = keep_ref.shape[0]
    to_y_ref[0:rows, :] = total_of(keep_ref[...], recv_ref[...]).astype(BF16)
    terms = [(table_keep_ref, 0), (table_recv_ref, 0)]
    size = table_keep_ref.shape[0]
    bit_split(place("mp"), size, terms, table_ref, to_y_ref.at[rows:, :])


def attend_mp_kernel(keep_ref, recv_ref, from_y_ref, table_ref, x_keep_ref, x_send_ref):
    rows, spare = keep_ref.shape[0], table_ref.shape[0]
    terms = [(keep_ref, 0), (recv_ref, 0), (from_y_ref, 0)]
    bit_split(place("x"), rows, terms, x_keep_ref, x_send_ref)
    terms = [(table_ref, 0), (from_y_ref, rows)]
    bit_split(place("x"), spare, terms, x_keep_ref, x_send_ref, rows // 2)


def attend_x_kernel(spare, keep_ref, recv_ref, z_keep_ref, z_send_ref):
    rows = keep_ref.shape[0] - spare
    for start, size in ((0, rows), (rows, spare)):
        terms = [(keep_ref, start), (recv_ref, start)]
        bit_split(z_bit(), size, terms, z_keep_ref, z_send_ref, start // 2)


def attend_join_kernel(own_ref, recv_ref, out_ref, table_ref):
    spare = table_ref.shape[0] // 2
    rows = own_ref.shape[0] - spare
    for ref, bit in ((own_ref, z_bit()), (recv_ref, 1 - z_bit())):
        out_ref[part(bit, rows), :] = ref[0:rows, :]
        table_ref[part(bit, spare), :] = ref[rows:, :]
    out_ref[2 * rows :, :] = table_ref[...]


def corners(parts, bit):
    own_ref, near_ref, core_own_ref, core_near_ref = parts
    core = place("core")
    return (
        (own_ref, core * 2 + bit),
        (near_ref, core * 2 + 1 - bit),
        (core_own_ref, (1 - core) * 2 + bit),
        (core_near_ref, (1 - core) * 2 + 1 - bit),
    )


def down_out_kernel(*refs):
    *parts, out_ref, token_ref = refs
    token_ref[...] = jnp.zeros(token_ref.shape, F32)
    for ref, index in corners(parts, place("x")):
        out_ref[part(index, ref.shape[0]), :] = ref[...].astype(F32)


def up_out_kernel(*refs):
    *parts, up_ref, out_ref, token_ref, work_ref = refs
    token_ref[...] = jnp.zeros(token_ref.shape, F32)
    for ref, index in corners(parts, z_bit()):
        work_ref[part(index, ref.shape[0]), :] = ref[...]
    width, spare = up_ref.shape[0], out_ref.shape[0] // 2
    for core in range(2):
        start = core * (width + spare)
        up_ref[:, core * width : (core + 1) * width] = work_ref[start : start + width, :].astype(F32)
        start += width
        out_ref[core * spare : (core + 1) * spare, :] = work_ref[start : start + spare, :].astype(F32)


def attend_out_kernel(
    parts, table_parts, qkv_ref, table_ref, work_ref, qkv_out_ref, table_out_ref, sems
):
    y = place("mp")
    spare = table_parts[0].shape[0]
    rows = parts[0].shape[0] - spare
    half = qkv_ref.shape[2]
    width = 2 * half
    for ref, index in corners(parts, place("x")):
        work_ref[part(index, rows), :] = ref[0:rows, :]
        core, x = lax.div(index, 2), lax.rem(index, 2)
        table_out_ref[part(core * 4 + y * 2 + x, spare), :] = ref[rows:, :].astype(F32)
    for ref, index in corners(table_parts, place("x")):
        core, x = lax.div(index, 2), lax.rem(index, 2)
        table_out_ref[part(core * 4 + (1 - y) * 2 + x, spare), :] = ref[...].astype(F32)
    copies = [pltpu.make_async_copy(table_out_ref, table_ref, sems.at[3])]
    copies[0].start()
    for i in range(3):
        if i < 2:
            qkv_out_ref[i] = work_ref[0:width, i * half : (i + 1) * half].astype(F32)
        else:
            qkv_out_ref[i, 0:half, :] = work_ref[width : width + half, 0:half].astype(F32)
            qkv_out_ref[i, half:, :] = work_ref[width : width + half, half:].astype(F32)
        copies.append(pltpu.make_async_copy(qkv_out_ref.at[i], qkv_ref.at[i], sems.at[i]))
        copies[-1].start()
    for copy in copies:
        copy.wait()


def swap(value, axis, name="swap", distance=1):
    pairs = [(i, i ^ distance) for i in range(lax.axis_size(axis))]
    with jax.named_scope(f"{name}_{axis}{distance}"):
        return lax.ppermute(value, axis, pairs)


def swap_corner(value, name):
    with jax.named_scope(name):
        return lax.ppermute(value, ("x", "mp"), [(0, 3), (1, 2), (2, 1), (3, 0)])


class Chain:
    def __init__(self):
        self.last = ()

    def gate(self, value, us=1):
        value = pl.pallas_call(
            lambda *refs: None,
            out_shape=jax.ShapeDtypeStruct(value.shape, value.dtype),
            in_specs=[anywhere] * (1 + len(self.last)),
            out_specs=anywhere,
            input_output_aliases={0: 0},
            compiler_params=pltpu.CompilerParams(vmem_limit_bytes=MIB),
            cost_estimate=pl.CostEstimate(
                flops=us * FLOPS_PER_US, bytes_accessed=0, transcendentals=0
            ),
            name="gate",
        )(value, *self.last)
        self.last = (value,)
        return value

    def __call__(
        self,
        kernel,
        outs,
        args,
        us,
        name,
        scratch=(),
        smem_args=0,
        hbm_args=0,
        copies=0,
        mib=8,
        token=None,
        hbm_outs=False,
    ):
        results = call(
            kernel, outs, args, self.last, scratch, us, mib, smem_args, hbm_args, copies, hbm_outs, name
        )
        if token is None:
            token = min(range(len(results)), key=lambda i: results[i].size)
        self.last = (results[token],)
        return results


def per_device(
    fast,
    mp_size,
    tokens,
    pos_table,
    qkv_weight,
    out_weight,
    out_bias,
    norm1_gain,
    norm1_shift,
    up_weight,
    up_bias,
    down_weight,
    down_bias,
    norm2_gain,
    norm2_shift,
    window,
    cotangent,
):
    step = Chain()
    rows, width = tokens.shape
    blocks = rows // W_LONG
    half_width = width // 2
    units = up_weight.shape[1] * mp_size // 2
    n, spare = width, W_LONG // 2
    group, att = (units + half_width) // 2, 3 * width // 4
    qkv_weight = jnp.transpose(qkv_weight, (1, 0, 2))
    wide = ((rows, width), F32)

    attend_outs = [
        (3, rows, half_width),
        (blocks * half_width // LANES, 2 * W_LONG, W_SHORT),
        (blocks * half_width // LANES, W_LONG, W_SHORT),
        (rows, half_width),
    ]

    def attend_own():
        return step(
            first_kernel,
            attend_outs,
            [window, tokens, pos_table, w_own],
            3,
            "attend_first",
            mib=28,
            smem_args=1,
        )

    def attend_other():
        return step(
            second_kernel,
            attend_outs
            + [wide, (3, width, half_width), (half_width, width), ((units,), F32)],
            [window, tokens, pos_table, attend_in, context_own, out_own, out_bias],
            5,
            "attend_second",
            mib=28,
            smem_args=1,
        )

    def ffn_own():
        return step(
            ffn_own_kernel,
            [(rows, width), (rows, units), (rows, units), wide],
            [resid, up_own, down_own, bias_own, norm1_gain, norm1_shift],
            4,
            "ffn_own",
            mib=28,
        )

    if fast:
        w_own, out_own, up_own, down_own = qkv_weight, out_weight, up_weight, down_weight
        bias_own = up_bias
        (message,) = step(
            pack_attend_kernel,
            [(width // 2 + EXTRA, width)],
            [up_bias, qkv_weight, out_weight],
            1,
            "pack_attend",
            mib=63,
            hbm_args=2,
            copies=5,
        )
        attend_y = swap(message, "mp", "attend_y")
        up_message, down_message = step(
            pack_ffn_kernel,
            [(units // 8, width), (units // 4, width)],
            [up_weight, down_weight],
            1,
            "pack_ffn",
            mib=60,
            hbm_args=2,
            copies=1 + units // width,
        )
        up_y = swap(up_message, "mp", "up_y")
        down_y = swap(down_message, "mp", "down_y")
        mixed_own, early_own, late_own, context_own = attend_own()
        attend_y = step.gate(attend_y, 0)
        attend_x = swap(attend_y, "x", "attend_x")
        up_y = step.gate(up_y, 0)
        up_z = swap(up_y, "z", "up_z")
        (up_y,) = step(z_join_kernel, [(units // 4, width)], [up_y, up_z], 0, "up_pair")
        up_x = swap(up_y, "x", "up_x")
        up_cy = swap(up_y, "core", "up_cy")
        down_y = step.gate(down_y, 1)
        down_z = swap(down_y, "z", "down_z")
        attend_x = step.gate(attend_x, 0)
        attend_cx = swap(attend_x, "core", "attend_cx")
        attend_cy = swap(attend_y, "core", "attend_cy")
        attend_in = (attend_y, attend_x, attend_cy, attend_cx)
        mixed_oth, early_oth, late_oth, context_oth, resid, w_oth, out_oth, bias_oth = attend_other()
        low, act_own, slope_own, branch = ffn_own()
        up_x = step.gate(up_x, 0)
        up_cx = swap(up_x, "core", "up_cx")
        down_z = step.gate(down_z, 4)
        down_cy = swap(down_y, "core", "down_cy")
        down_cz = swap(down_z, "core", "down_cz")
        up_in = (up_y, up_x, up_cy, up_cx)
        down_in = (down_y, down_z, down_cy, down_cz)
    else:
        qkv = lax.all_gather(qkv_weight, "mp", axis=2, tiled=True)
        out_w = lax.all_gather(out_weight, "mp", axis=0, tiled=True)
        up_w = lax.all_gather(up_weight, "mp", axis=1, tiled=True)
        bias = lax.all_gather(up_bias, "mp", axis=0, tiled=True)
        down_w = lax.all_gather(down_weight, "mp", axis=0, tiled=True)
        w_own, out_own = qkv[:, :, :half_width], out_w[:half_width]
        attend_in = (qkv[:, :, half_width:], out_w[half_width:], bias[units:])
        up_own, up_in = up_w[:, :units], (up_w[:, units:],)
        down_own, down_in = down_w[:units], (down_w[units:],)
        bias_own = bias[:units]
        mixed_own, early_own, late_own, context_own = attend_own()
        mixed_oth, early_oth, late_oth, context_oth, resid, w_oth, out_oth, bias_oth = attend_other()
        low, act_own, slope_own, branch = ffn_own()

    layer_out, down_keep, down_send, slope_oth, up_oth, down_oth, grad2, vec = step(
        functools.partial(ffn_other_kernel, fast),
        [
            (rows, width),
            (units, width),
            (units, width),
            (rows, units),
            (width, units),
            (units, width),
            wide,
            ((8, width), F32),
        ],
        [
            cotangent,
            low,
            act_own,
            branch,
            up_in,
            down_in,
            bias_oth,
            down_bias,
            norm2_gain,
            norm2_shift,
        ],
        6,
        "ffn_other",
            mib=28,
        scratch=[((rows, units), BF16), ((units, width), BF16)],
    )
    down_recv = swap(down_send, "core", "down_recv") if fast else None
    up_keep, up_send, small, grad1 = step(
        functools.partial(ffn_back_kernel, fast),
        [
            (2 * group + EXTRA, width),
            (2 * group + EXTRA, width),
            ((EXTRA, width), F32),
            wide,
        ],
        [
            resid,
            grad2,
            low,
            (slope_own, slope_oth),
            (up_own, up_oth),
            (down_own, down_oth),
            (context_own, context_oth),
            vec,
            norm1_gain,
        ],
        6,
        "ffn_back",
            mib=28,
        scratch=[
            ((rows, units), BF16),
            ((rows, width), F32),
            ((units, width), BF16),
            ((8, width), F32),
            ((half_width, width), BF16),
        ],
    )

    def attend_back():
        return step(
            functools.partial(attend_back_kernel, fast),
            [(att, width)] * 2
            + [(spare, width)] * 2
            + [(rows, width)] * 2
            + [(3, rows, half_width)],
            [
                window,
                tokens,
                pos_table,
                grad1,
                (w_own, out_own, mixed_own, early_own, late_own),
                (w_oth, out_oth, mixed_oth, early_oth, late_oth),
            ],
            13,
            "attend_back",
            mib=28,
            scratch=[
                ((rows, width), F32),
                ((3, rows, half_width), BF16),
                ((2 * att, width), BF16),
                ((W_LONG, width), BF16),
                ((half_width // LANES, 2 * W_LONG, W_SHORT), BF16),
                ((half_width // LANES, W_LONG, W_SHORT), BF16),
            ],
            smem_args=1,
        )

    def project_back(hidden, own_gm):
        return step(
            functools.partial(project_back_kernel, fast),
            [(att, width)] * 2,
            [hidden, own_gm],
            0,
            "project_back",
            mib=16,
            scratch=[((2 * att, width), BF16)],
        )

    if not fast:
        *oth_parts, grad_tokens, hidden, own_gm = attend_back()
        att_parts = (*oth_parts[:2], *project_back(hidden, own_gm), *oth_parts[2:])
        qkv_g, out_g, up_g, down_g, small, table = reduce_plain(
            n, width, down_keep, down_send, up_keep, up_send, small, *att_parts
        )
        vectors = [small[i] for i in range(6)]
        bias_all = small[6 : 6 + 2 * units // width].reshape(-1)
        start = lax.axis_index("mp") * up_bias.shape[0]
        bias_g = lax.dynamic_slice_in_dim(bias_all, start, up_bias.shape[0])
    else:
        half, piece, strip = n // 2, n // 4, spare // 2
        up_recv = swap(up_send, "core", "up_recv")
        (to_y,) = step(other_half_kernel, [(n, width)], [down_keep, down_recv], 6, "down_core")
        down_from_y = swap(to_y, "mp", "down_from_y")
        up_x, to_x = step(
            up_split_kernel,
            [(group + EXTRA, width)] * 2,
            [up_keep, up_recv],
            5,
            "up_core",
        )
        up_from_x = swap(to_x, "z", "up_from_z")
        oth_keep, oth_send, tab_keep, tab_send, grad_tokens, hidden, own_gm = attend_back()
        oth_recv = swap(oth_send, "core", "oth_recv")
        tab_recv = swap(tab_send, "core", "tab_recv")
        own_keep, own_send = project_back(hidden, own_gm)
        own_recv = swap(own_send, "core", "own_recv")
        down_x, to_x = step(
            down_split_kernel,
            [(half, width)] * 2,
            [down_keep, down_recv, down_from_y],
            0,
            "down_mp",
        )
        down_from_x = swap(to_x, "x", "down_from_x")
        to_y, table = step(
            attend_core_kernel,
            [(att + strip, width), (strip, width)],
            [oth_keep, oth_recv, tab_keep, tab_recv],
            0,
            "attend_core",
        )
        att_from_y = swap(to_y, "mp", "att_from_y")
        up_z, to_z = step(
            up_x_kernel,
            [(group // 2 + EXTRA, width)] * 2,
            [up_x, up_from_x],
            5,
            "up_x",
        )
        up_from_z = swap(to_z, "x", "up_from_x")
        down_z, to_z = step(
            down_x_kernel,
            [(piece, width)] * 2,
            [down_x, down_from_x],
            3,
            "down_x",
        )
        down_from_z = swap(to_z, "z", "down_from_z")
        (down_z,) = step(pair_kernel, [(piece, width)], [down_z, down_from_z], 0, "down_z")
        down_far = swap(down_z, "z", "down_far", 2)
        att_x, to_x = step(
            attend_mp_kernel,
            [((att + strip) // 2, width)] * 2,
            [own_keep, own_recv, att_from_y, table],
            0,
            "attend_mp",
        )
        att_from_x = swap(to_x, "x", "att_from_x")
        up_y, to_y = step(
            up_z_kernel, [(group // 4 + EXTRA, width)] * 2, [up_z, up_from_z], 1, "up_z"
        )
        up_from_y = swap(to_y, "mp", "up_from_y")
        (down_z,) = step(pair_kernel, [(piece, width)], [down_z, down_far], 0, "down_far")
        down_near = swap(down_z, "z", "down_near")
        att_z, to_z = step(
            functools.partial(attend_x_kernel, strip // 2),
            [((att + strip) // 4, width)] * 2,
            [att_x, att_from_x],
            0,
            "attend_x",
        )
        att_from_z = swap(to_z, "z", "att_from_z")
        (up_y,) = step(pair_kernel, [(group // 4 + EXTRA, width)], [up_y, up_from_y], 0, "up_mp")
        up_far = swap(up_y, "z", "up_far", 2)
        (down_z,) = step(functools.partial(join_kernel, "z"), [(half, width)], [down_z, down_near], 7, "down_join")
        down_x = swap(down_z, "x", "down_x")
        (att_z,) = step(pair_kernel, [att_z.shape], [att_z, att_from_z], 0, "attend_z")
        att_far = swap(att_z, "z", "att_far", 2)
        up_z, small = step(
            up_last_kernel,
            [(group // 4, width), ((EXTRA, width), F32)],
            [up_y, up_far],
            0,
            "up_far",
        )
        up_near = swap(up_z, "x", "up_near")
        (att_z,) = step(pair_kernel, [att_z.shape], [att_z, att_far], 0, "attend_far")
        att_near = swap(att_z, "z", "att_near")
        att_half, table = step(
            attend_join_kernel,
            [((att + strip) // 2, width), (strip // 2, width)],
            [att_z, att_near],
            0,
            "attend_join",
        )
        att_x = swap(att_half, "x", "att_x")
        table_y = swap(table, "mp", "table_y")
        table_x = swap_corner(table, "table_x")
        (up_z,) = step(functools.partial(join_kernel, "x"), [(group // 2, width)], [up_z, up_near], 0, "up_join")
        up_x = swap(up_z, "z", "up_last")
        down_x = step.gate(down_x, 0)
        *vectors, bias_g, _ = step(
            small_out_kernel,
            [((width,), F32)] * 6 + [((up_bias.shape[0],), F32), ((8, LANES), F32)],
            [small],
            0,
            "small_out",
            token=7,
        )
        down_g, _ = step(
            down_out_kernel,
            [((2 * n, width), F32), ((8, LANES), F32)],
            [
                down_z,
                down_x,
                swap(down_z, "core", "down_core"),
                swap(down_x, "core", "down_core_x"),
            ],
            0,
            "down_out",
        )
        table_y = step.gate(table_y, 0)
        up_x = step.gate(up_x, 0)
        table_x = step.gate(table_x, 2)
        att_x = step.gate(att_x, 1)
        up_g, out_g, _ = step(
            up_out_kernel,
            [((width, 2 * n), F32), ((half_width, width), F32), ((8, LANES), F32)],
            [up_z, up_x, swap(up_z, "core", "up_core"), swap(up_x, "core", "up_core_x")],
            0,
            "up_out",
            scratch=[((2 * group, width), BF16)],
        )
        qkv_g, table = step(
            attend_out_kernel,
            [((3, width, half_width), F32), ((W_LONG, width), F32)],
            [
                (
                    att_half,
                    att_x,
                    swap(att_half, "core", "att_core"),
                    swap(att_x, "core", "att_core_x"),
                ),
                (
                    table_y,
                    table_x,
                    swap(table_y, "core", "table_core"),
                    swap(table_x, "core", "table_core_x"),
                ),
            ],
            0,
            "attend_out",
            scratch=[
                ((2 * att, width), BF16),
                ((3, width, half_width), F32),
                ((W_LONG, width), F32),
            ],
            copies=4,
            hbm_outs=True,
        )


    return (
        layer_out,
        grad_tokens,
        table,
        jnp.transpose(qkv_g, (1, 0, 2)),
        out_g,
        vectors[0],
        vectors[1],
        vectors[2],
        up_g,
        bias_g,
        down_g,
        vectors[3],
        vectors[4],
        vectors[5],
    )


def reduce_plain(
    n,
    width,
    down_keep,
    down_send,
    up_keep,
    up_send,
    small,
    other_keep,
    other_send,
    own_keep,
    own_send,
    table_keep,
    table_send,
):
    half, spare = n // 2, n // 4
    group = n + spare

    def rows_of(start, size):
        return lambda keep, send: jnp.concatenate(
            [keep[start : start + size], send[start : start + size]], axis=0
        )

    def summed(own, oth, dim):
        whole = jnp.concatenate([own, oth], axis=dim)
        part_sum = lax.psum_scatter(whole, "mp", scatter_dimension=dim, tiled=True)
        return lax.psum(part_sum, "dp").astype(F32)

    def qkv_part(g):
        value = jnp.concatenate([g[n : n + half, :half], g[n : n + half, half:]], axis=0)
        return jnp.stack([g[:n, :half], g[:n, half:], value])

    def up_part(g):
        return jnp.concatenate([g[:n], g[n:]], axis=1)

    down = [rows_of(start, n)(down_keep, down_send) for start in (0, n)]
    up = [up_part(rows_of(start, n)(up_keep, up_send)) for start in (0, group)]
    out = [rows_of(start + n, spare)(up_keep, up_send) for start in (0, group)]
    att = [
        qkv_part(jnp.concatenate(pair, axis=0))
        for pair in ((own_keep, own_send), (other_keep, other_send))
    ]
    table = jnp.concatenate([table_keep, table_send], axis=0).astype(F32)
    return (
        summed(*att, 2),
        summed(*out, 0),
        summed(*up, 1),
        summed(*down, 0),
        lax.psum(small, ("dp", "mp")),
        lax.psum(table, ("dp", "mp")),
    )


def solution(mesh):
    mp_size = mesh.shape["mp"]
    fast = mp_size == 2 and mesh.shape["dp"] == 16
    dp = "dp"
    if fast:
        shape = (mesh.shape["dp"] // 4, 2, 2, mp_size)
        mesh = Mesh(mesh.devices.reshape(shape), ("z", "x", "core", "mp"))
        dp = ("z", "x", "core")
    both = P((*dp, "mp") if fast else (dp, "mp"), None)
    placed = (
        both,
        P(),
        P(None, None, "mp"),
        P("mp", None),
        P(),
        P(),
        P(),
        P(None, "mp"),
        P("mp"),
        P("mp", None),
        P(),
        P(),
        P(),
        P(dp),
        both,
    )
    return jax.shard_map(
        functools.partial(per_device, fast, mp_size),
        mesh=mesh,
        in_specs=placed,
        out_specs=(
            both,
            both,
            P(),
            P(None, None, "mp"),
            P("mp", None),
            P(),
            P(),
            P(),
            P(None, "mp"),
            P("mp"),
            P("mp", None),
            P(),
            P(),
            P(),
        ),
        check_vma=False,
    )
```

```python
import functools

import jax
import jax.numpy as jnp
from jax import lax
from jax.experimental import pallas as pl
from jax.experimental.pallas import tpu as pltpu
from jax.sharding import Mesh
from jax.sharding import PartitionSpec as P

HD = 64
W_SHORT = 256
W_LONG = 512
ROW = 1024
LANES = 128
EXTRA = 16
CHUNK = 256
EPSILON = 1e-05
MASKED = -1e30
F32 = jnp.float32
BF16 = jnp.bfloat16
MIB = 1024 * 1024
FLOPS_PER_US = 10**9

vmem = pl.BlockSpec(memory_space=pltpu.VMEM)
smem = pl.BlockSpec(memory_space=pltpu.SMEM)
anywhere = pl.BlockSpec(memory_space=pl.ANY)


def call(
    kernel, outs, args, after=(), scratch=(), us=1, mib=32, smem_args=0, hbm_args=0, copies=0, hbm_outs=False, name=None
):
    flat, tree = jax.tree.flatten(tuple(args))
    count, extra = len(flat), len(after)

    def flat_kernel(*refs):
        kernel(*jax.tree.unflatten(tree, refs[:count]), *refs[count + extra :])

    return pl.pallas_call(
        flat_kernel,
        out_shape=[
            jax.ShapeDtypeStruct(out, BF16) if isinstance(out[0], int) else jax.ShapeDtypeStruct(*out)
            for out in outs
        ],
        in_specs=[smem] * smem_args
        + [vmem] * (count - smem_args - hbm_args)
        + [anywhere] * (hbm_args + extra),
        out_specs=[anywhere if hbm_outs else vmem] * len(outs),
        scratch_shapes=[pltpu.VMEM(shape, dtype) for shape, dtype in scratch]
        + [pltpu.SemaphoreType.DMA((copies,))] * (copies > 0),
        compiler_params=pltpu.CompilerParams(vmem_limit_bytes=mib * MIB),
        cost_estimate=pl.CostEstimate(
            flops=us * FLOPS_PER_US, bytes_accessed=0, transcendentals=0
        ),
        name=name,
    )(*flat, *after)


def place(axis):
    return lax.axis_index(axis)


def row(ref, start=0, size=None):
    size = ref.shape[0] if size is None else size
    return ref[start : start + size].astype(F32).reshape(1, size)


def mm(a, b):
    return lax.dot_general(a, b, (((1,), (0,)), ((), ())), preferred_element_type=F32)


def mm_nt(a, b):
    return lax.dot_general(a, b, (((1,), (1,)), ((), ())), preferred_element_type=F32)


def mm_tn(a, b):
    return lax.dot_general(a, b, (((0,), (0,)), ((), ())), preferred_element_type=F32)


def position_rows(pos_ref, is_long):
    first = pos_ref[0:W_SHORT, :].astype(F32)
    second = jnp.where(is_long, pos_ref[W_SHORT:W_LONG, :].astype(F32), first)
    return first, second


def hidden_rows(tokens_ref, pos_ref, windows):
    parts = []
    for block, is_long in enumerate(windows):
        first, second = position_rows(pos_ref, is_long)
        start = block * W_LONG
        parts.append(tokens_ref[start : start + W_SHORT, :].astype(F32) + first)
        parts.append(tokens_ref[start + W_SHORT : start + W_LONG, :].astype(F32) + second)
    return jnp.concatenate(parts, axis=0)


def read_windows(win_ref, rows):
    first = place("mp") * rows
    return [
        win_ref[lax.div(first + block * W_LONG, ROW)] == W_LONG for block in range(rows // W_LONG)
    ]


def norm_stats(values):
    average = jnp.mean(values, axis=-1, keepdims=True)
    centred = values - average
    variance = jnp.mean(centred * centred, axis=-1, keepdims=True)
    scale = lax.rsqrt(variance + EPSILON)
    return centred * scale, scale


def norm_grad(grad_hat, hat, scale):
    mean_grad = jnp.mean(grad_hat, axis=-1, keepdims=True)
    mean_both = jnp.mean(grad_hat * hat, axis=-1, keepdims=True)
    return scale * (grad_hat - mean_grad - hat * mean_both)


def head_mask(rows):
    return lax.broadcasted_iota(jnp.int32, (rows, LANES), 1) < HD


def stack_heads(value, is_low):
    zero = jnp.zeros_like(value)
    return jnp.concatenate(
        [jnp.where(is_low, value, zero), jnp.where(is_low, zero, value)], axis=0
    )


def late_rows(value):
    return jnp.concatenate(
        [value[W_SHORT:W_LONG], value[W_LONG + W_SHORT : 2 * W_LONG]], axis=0
    )


def merge_heads(first, late, is_low):
    top = jnp.where(is_low, first[0:W_SHORT], first[W_LONG : W_LONG + W_SHORT])
    bottom = jnp.where(
        is_low,
        first[W_SHORT:W_LONG] + late[0:W_SHORT],
        first[W_LONG + W_SHORT :] + late[W_SHORT:],
    )
    return top, bottom


def attend_forward(hidden_low, weight_ref, windows, mixed_ref, early_ref, late_ref, context_ref):
    rows, width = context_ref.shape
    pairs = width // LANES
    for c in range(3):
        part = mm(hidden_low, weight_ref[c]).astype(BF16)
        mixed_ref[c] = part * BF16(HD**-0.5) if c == 0 else part
    causal = lax.broadcasted_iota(jnp.int32, (W_SHORT, W_SHORT), 0) >= lax.broadcasted_iota(
        jnp.int32, (W_SHORT, W_SHORT), 1
    )
    is_low = head_mask(W_LONG)
    for block, is_long in enumerate(windows):
        both = slice(block * W_LONG, (block + 1) * W_LONG)
        lo = slice(block * W_LONG, block * W_LONG + W_SHORT)
        hi = slice(block * W_LONG + W_SHORT, (block + 1) * W_LONG)
        for pair in range(pairs):
            lanes = slice(pair * LANES, (pair + 1) * LANES)
            slot = block * pairs + pair
            queries = stack_heads(mixed_ref[0, both, lanes], is_low)
            scores = mm_nt(queries, mixed_ref[1, lo, lanes])
            late = mm_nt(late_rows(queries), mixed_ref[1, hi, lanes])
            for head in range(2):
                start = head * W_LONG
                s_a = jnp.where(causal, scores[start : start + W_SHORT], MASKED)
                e_a = jnp.exp(s_a - jnp.max(s_a, axis=-1, keepdims=True))
                p_a = e_a * (1.0 / jnp.sum(e_a, axis=-1, keepdims=True))
                s_b = jnp.where(is_long, scores[start + W_SHORT : start + W_LONG], MASKED)
                s_c = jnp.where(causal, late[head * W_SHORT : (head + 1) * W_SHORT], MASKED)
                top = jnp.max(jnp.maximum(s_b, s_c), axis=-1, keepdims=True)
                e_b = jnp.exp(s_b - top)
                e_c = jnp.exp(s_c - top)
                inverse = 1.0 / jnp.sum(e_b + e_c, axis=-1, keepdims=True)
                early_ref[slot, start : start + W_SHORT, :] = p_a.astype(BF16)
                early_ref[slot, start + W_SHORT : start + W_LONG, :] = (e_b * inverse).astype(BF16)
                late_ref[slot, head * W_SHORT : (head + 1) * W_SHORT, :] = (e_c * inverse).astype(
                    BF16
                )
            top_rows, bottom_rows = merge_heads(
                mm(early_ref[slot], mixed_ref[2, lo, lanes]),
                mm(late_ref[slot], mixed_ref[2, hi, lanes]),
                head_mask(W_SHORT),
            )
            context_ref[lo, lanes] = top_rows.astype(BF16)
            context_ref[hi, lanes] = bottom_rows.astype(BF16)


def attend_backward(grad_context, mixed_ref, early_ref, late_ref, blocks, grad_mixed_ref, work):
    width = mixed_ref.shape[2]
    pairs = width // LANES
    is_low = head_mask(W_LONG)
    early_grad_ref, late_grad_ref = work
    for block in range(blocks):
        both = slice(block * W_LONG, (block + 1) * W_LONG)
        lo = slice(block * W_LONG, block * W_LONG + W_SHORT)
        hi = slice(block * W_LONG + W_SHORT, (block + 1) * W_LONG)
        for pair in range(pairs):
            lanes = slice(pair * LANES, (pair + 1) * LANES)
            slot = block * pairs + pair
            queries = stack_heads(mixed_ref[0, both, lanes], is_low)
            grads = stack_heads(grad_context[both, lanes], is_low)
            grad_early = mm_nt(grads, mixed_ref[2, lo, lanes])
            grad_late = mm_nt(late_rows(grads), mixed_ref[2, hi, lanes])
            for head in range(2):
                start = head * W_LONG
                first = slice(start, start + W_SHORT)
                second = slice(start + W_SHORT, start + W_LONG)
                last = slice(head * W_SHORT, (head + 1) * W_SHORT)
                p_a = early_ref[slot, first, :].astype(F32)
                g_a = grad_early[first]
                inner = jnp.sum(p_a * g_a, axis=-1, keepdims=True)
                early_grad_ref[pair, first, :] = (p_a * (g_a - inner)).astype(BF16)
                p_b, p_c = early_ref[slot, second, :].astype(F32), late_ref[slot, last, :].astype(F32)
                g_b, g_c = grad_early[second], grad_late[last]
                inner = jnp.sum(p_b * g_b + p_c * g_c, axis=-1, keepdims=True)
                early_grad_ref[pair, second, :] = (p_b * (g_b - inner)).astype(BF16)
                late_grad_ref[pair, last, :] = (p_c * (g_c - inner)).astype(BF16)
            top_rows, bottom_rows = merge_heads(
                mm(early_grad_ref[pair], mixed_ref[1, lo, lanes]),
                mm(late_grad_ref[pair], mixed_ref[1, hi, lanes]),
                head_mask(W_SHORT),
            )
            grad_mixed_ref[0, lo, lanes] = (top_rows * HD**-0.5).astype(BF16)
            grad_mixed_ref[0, hi, lanes] = (bottom_rows * HD**-0.5).astype(BF16)
            grad_mixed_ref[1, lo, lanes] = mm_tn(early_grad_ref[pair], queries).astype(BF16)
            grad_mixed_ref[1, hi, lanes] = mm_tn(late_grad_ref[pair], late_rows(queries)).astype(BF16)
            grad_mixed_ref[2, lo, lanes] = mm_tn(early_ref[slot], grads).astype(BF16)
            grad_mixed_ref[2, hi, lanes] = mm_tn(late_ref[slot], late_rows(grads)).astype(BF16)


def normal_parts(x):
    density = jnp.exp2(x * x * -0.7213475204 - 1.3257480647)
    return 0.5 + 0.5 * lax.erf(x * 0.7071067812), density


def first_kernel(
    win_ref, tokens_ref, pos_ref, weight_ref, mixed_ref, early_ref, late_ref, context_ref
):
    windows = read_windows(win_ref, tokens_ref.shape[0])
    hidden_low = hidden_rows(tokens_ref, pos_ref, windows).astype(BF16)
    attend_forward(
        hidden_low, weight_ref, windows, mixed_ref, early_ref, late_ref, context_ref
    )


def z_bit():
    return lax.rem(place("z"), 2)


def quarter(bit):
    return place("core") * 2 + bit


def part(index, size):
    return pl.ds(pl.multiple_of(index * size, size), size)


def copy_all(pairs, sems, meanwhile=None):
    copies = [
        pltpu.make_async_copy(src, dst, sems.at[i]) for i, (src, dst) in enumerate(pairs)
    ]
    for copy in copies:
        copy.start()
    if meanwhile is not None:
        meanwhile()
    for copy in copies:
        copy.wait()


def pack_attend_kernel(bias_ref, qkv_ref, out_ref, send_ref, sems):
    _, width, half = qkv_ref.shape
    depth, mine = width // 4, quarter(place("x"))

    def write_bias():
        used = bias_ref.shape[0] // width
        send_ref[2 * depth :, :] = jnp.zeros((EXTRA, width), BF16)
        for i in range(used):
            at = 2 * depth + i
            send_ref[at : at + 1, :] = row(bias_ref, i * width, width).astype(BF16)

    middle = depth + depth // 2
    low, high = pl.ds(0, half), pl.ds(half, half)
    upper, lower = part(mine * 2, depth // 2), part(mine * 2 + 1, depth // 2)
    copy_all(
        [
            (qkv_ref.at[0, part(mine, depth), :], send_ref.at[pl.ds(0, depth), low]),
            (qkv_ref.at[1, part(mine, depth), :], send_ref.at[pl.ds(0, depth), high]),
            (qkv_ref.at[2, upper, :], send_ref.at[pl.ds(depth, depth // 2), low]),
            (qkv_ref.at[2, lower, :], send_ref.at[pl.ds(depth, depth // 2), high]),
            (out_ref.at[part(mine, depth // 2), :], send_ref.at[pl.ds(middle, depth // 2), :]),
        ],
        sems,
        write_bias,
    )


def pack_ffn_kernel(up_ref, down_ref, up_to, down_to, sems):
    width, units = up_ref.shape
    depth = width // 8
    mine = part(quarter(place("x")) * 2 + z_bit(), depth)
    columns = [
        (up_ref.at[mine, pl.ds(i * width, width)], up_to.at[pl.ds(i * depth, depth), :])
        for i in range(units // width)
    ]
    copy_all([*columns, (down_ref.at[part(quarter(z_bit()), units // 4), :], down_to)], sems)


def z_join_kernel(own_ref, near_ref, out_ref):
    depth = own_ref.shape[0] // 2
    for ref, bit in ((own_ref, z_bit()), (near_ref, 1 - z_bit())):
        for i in range(2):
            rows = pl.ds(pl.multiple_of(i * 2 * depth + bit * depth, depth), depth)
            out_ref[rows, :] = ref[i * depth : (i + 1) * depth, :]


def places(pieces, bit):
    from_y, from_near, core_y, core_near = pieces
    core = place("core")
    return (
        (from_y, core * 2 + bit),
        (from_near, core * 2 + 1 - bit),
        (core_y, (1 - core) * 2 + bit),
        (core_near, (1 - core) * 2 + 1 - bit),
    )


def second_kernel(
    win_ref,
    tokens_ref,
    pos_ref,
    pieces,
    context_own_ref,
    out_own_ref,
    out_bias_ref,
    mixed_ref,
    early_ref,
    late_ref,
    context_ref,
    resid_ref,
    w_oth_ref,
    out_oth_ref,
    bias_oth_ref,
):
    width = tokens_ref.shape[1]
    half, depth = width // 2, width // 4
    windows = read_windows(win_ref, tokens_ref.shape[0])
    if len(pieces) == 4:
        for ref, index in places(pieces, place("x")):
            rows = part(index, depth)
            w_oth_ref[0, rows, :] = ref[0:depth, 0:half]
            w_oth_ref[1, rows, :] = ref[0:depth, half:]
            middle = depth + depth // 2
            w_oth_ref[2, part(index * 2, depth // 2), :] = ref[depth:middle, 0:half]
            w_oth_ref[2, part(index * 2 + 1, depth // 2), :] = ref[depth:middle, half:]
            out_oth_ref[part(index, depth // 2), :] = ref[middle : 2 * depth, :]
        for i in range(bias_oth_ref.shape[0] // width):
            bias_row = pieces[0][2 * depth + i : 2 * depth + i + 1, :].astype(F32)
            bias_oth_ref[i * width : (i + 1) * width] = bias_row.reshape(width)
    else:
        w_oth_ref[...] = pieces[0][...]
        out_oth_ref[...] = pieces[1][...]
        bias_oth_ref[...] = pieces[2][...].astype(F32)
    hidden_in = hidden_rows(tokens_ref, pos_ref, windows)
    attend_forward(
        hidden_in.astype(BF16),
        w_oth_ref,
        windows,
        mixed_ref,
        early_ref,
        late_ref,
        context_ref,
    )
    branch = mm(context_own_ref[...], out_own_ref[...]) + mm(context_ref[...], out_oth_ref[...])
    hidden_in = hidden_rows(tokens_ref, pos_ref, windows)
    resid_ref[...] = hidden_in + branch + row(out_bias_ref)


def core_split(whole_ref, keep_ref, send_ref, start, split):
    half = whole_ref.shape[0] // 2
    core = place("core") if split else 0
    keep_ref[start : start + half, :] = whole_ref[part(core, half), :]
    send_ref[start : start + half, :] = whole_ref[part(1 - core, half), :]


def ffn_forward(low_ref, up_ref, bias_ref, act_ref, slope_ref):
    for start in range(0, up_ref.shape[1], CHUNK):
        cols = slice(start, start + CHUNK)
        pre = mm(low_ref[...], up_ref[:, cols]) + row(bias_ref, start, CHUNK)
        total, density = normal_parts(pre)
        act_ref[:, cols] = (pre * total).astype(BF16)
        slope_ref[:, cols] = (total + pre * density).astype(BF16)


def ffn_own_kernel(
    resid_ref,
    up_ref,
    down_ref,
    bias_ref,
    gain_ref,
    shift_ref,
    low_ref,
    act_ref,
    slope_ref,
    branch_ref,
):
    hat, _ = norm_stats(resid_ref[...])
    normed = hat * row(gain_ref) + row(shift_ref)
    low_ref[...] = normed.astype(BF16)
    ffn_forward(low_ref, up_ref, bias_ref, act_ref, slope_ref)
    branch_ref[...] = normed + mm(act_ref[...], down_ref[...])


def ffn_other_kernel(
    split,
    cot_ref,
    low_ref,
    act_own_ref,
    branch_ref,
    up_refs,
    down_refs,
    bias_ref,
    down_bias_ref,
    gain_ref,
    shift_ref,
    layer_ref,
    keep_ref,
    send_ref,
    slope_ref,
    up_ref,
    down_ref,
    grad_ref,
    vec_ref,
    act_ref,
    package_ref,
):
    width = cot_ref.shape[1]
    units = up_ref.shape[1]
    if len(up_refs) == 4:
        for ref, index in places(up_refs, place("x")):
            depth = ref.shape[0] * width // units
            for i in range(units // width):
                up_ref[part(index, depth), i * width : (i + 1) * width] = ref[
                    i * depth : (i + 1) * depth, :
                ]
        for ref, index in places(down_refs, z_bit()):
            down_ref[part(index, ref.shape[0]), :] = ref[...]
    else:
        up_ref[...] = up_refs[0][...]
        down_ref[...] = down_refs[0][...]
    ffn_forward(low_ref, up_ref, bias_ref, act_ref, slope_ref)
    resid = branch_ref[...] + mm(act_ref[...], down_ref[...]) + row(down_bias_ref)
    hat, scale = norm_stats(resid)
    layer_ref[...] = (hat * row(gain_ref) + row(shift_ref)).astype(BF16)
    cot = cot_ref[...].astype(F32)
    vec_ref[1:2, :] = jnp.sum(cot * hat, axis=0, keepdims=True)
    vec_ref[2:3, :] = jnp.sum(cot, axis=0, keepdims=True)
    grad = norm_grad(cot * row(gain_ref), hat, scale)
    vec_ref[0:1, :] = jnp.sum(grad, axis=0, keepdims=True)
    grad_ref[...] = grad
    grad_low = grad.astype(BF16)
    for half, act in ((0, act_own_ref), (1, act_ref)):
        for start in range(0, units, CHUNK):
            cols = slice(start, start + CHUNK)
            package_ref[cols, :] = mm_tn(act[:, cols], grad_low).astype(BF16)
        core_split(package_ref, keep_ref, send_ref, half * (units // 2), split)


def ffn_back_kernel(
    split,
    resid_ref,
    grad_ref,
    low_ref,
    slopes,
    ups,
    downs,
    contexts,
    vec_ref,
    gain_ref,
    keep_ref,
    send_ref,
    small_ref,
    grad_resid_ref,
    work_ref,
    total_ref,
    package_ref,
    bias_sum_ref,
    out_ref,
):
    width = resid_ref.shape[1]
    units = ups[0].shape[1]
    half_width = width // 2
    group = (units + half_width) // 2
    grad_low = grad_ref[...].astype(BF16)
    for half in range(2):
        for start in range(0, units, CHUNK):
            cols = slice(start, start + CHUNK)
            grad_act = mm_nt(grad_low, downs[half][cols, :])
            pre_grad = (grad_act * slopes[half][:, cols].astype(F32)).astype(BF16)
            work_ref[:, cols] = pre_grad
            at = half * (units // width) + start // width
            bias_sum_ref[at : at + 1, start % width : start % width + CHUNK] = jnp.sum(
                pre_grad.astype(F32), axis=0, keepdims=True
            )
        for start in range(0, units, width):
            cols = slice(start, start + width)
            package_ref[cols, :] = mm_tn(low_ref[...], work_ref[:, cols]).astype(BF16)
        core_split(package_ref, keep_ref, send_ref, half * group, split)
        before = grad_ref[...] if half == 0 else total_ref[...]
        total_ref[...] = before + mm_nt(work_ref[...], ups[half][...])
    grad = total_ref[...]
    hat, scale = norm_stats(resid_ref[...])
    small_ref[1:2, :] = jnp.sum(grad * hat, axis=0, keepdims=True)
    small_ref[2:3, :] = jnp.sum(grad, axis=0, keepdims=True)
    grad = norm_grad(grad * row(gain_ref), hat, scale)
    small_ref[0:1, :] = jnp.sum(grad, axis=0, keepdims=True)
    grad_low = grad.astype(BF16)
    for half in range(2):
        out_ref[...] = mm_tn(contexts[half][...], grad_low).astype(BF16)
        core_split(out_ref, keep_ref, send_ref, half * group + units // 2, split)
    small_ref[3:6, :] = vec_ref[0:3, :]
    span = units // width
    first_half = (place("mp") if split else 0) == 0
    ours, theirs = bias_sum_ref[0:span, :], bias_sum_ref[span : 2 * span, :]
    small_ref[6 : 6 + span, :] = jnp.where(first_half, ours, theirs)
    small_ref[6 + span : 6 + 2 * span, :] = jnp.where(first_half, theirs, ours)
    used = 6 + 2 * span
    small_ref[used:, :] = jnp.zeros((small_ref.shape[0] - used, width), F32)
    keep_ref[2 * group :, :] = small_ref[...].astype(BF16)
    send_ref[2 * group :, :] = small_ref[...].astype(BF16)
    grad_resid_ref[...] = grad


def half_backward(
    grad_low, weight_ref, out_ref, mixed_ref, early_ref, late_ref, gm_ref, work
):
    grad_context = mm_nt(grad_low, out_ref[...]).astype(BF16)
    attend_backward(
        grad_context, mixed_ref, early_ref, late_ref, grad_low.shape[0] // W_LONG, gm_ref, work
    )
    return (
        mm_nt(gm_ref[0], weight_ref[0])
        + mm_nt(gm_ref[1], weight_ref[1])
        + mm_nt(gm_ref[2], weight_ref[2])
    )


def projection_grads(hidden_low, gm_ref, package_ref, keep_ref, send_ref, split):
    rows, width = hidden_low.shape
    half_width = width // 2
    package_ref[0:width, 0:half_width] = mm_tn(hidden_low, gm_ref[0]).astype(BF16)
    package_ref[0:width, half_width:] = mm_tn(hidden_low, gm_ref[1]).astype(BF16)
    value_grad = mm_tn(hidden_low, gm_ref[2]).astype(BF16)
    package_ref[width : width + half_width, 0:half_width] = value_grad[0:half_width, :]
    package_ref[width : width + half_width, half_width:] = value_grad[half_width:, :]
    core_split(package_ref, keep_ref, send_ref, 0, split)


def attend_back_kernel(
    split,
    win_ref,
    tokens_ref,
    pos_ref,
    grad_resid_ref,
    own_refs,
    other_refs,
    other_keep_ref,
    other_send_ref,
    table_keep_ref,
    table_send_ref,
    tokens_grad_ref,
    hidden_ref,
    own_gm_ref,
    grad_ref,
    gm_ref,
    package_ref,
    table_ref,
    *work,
):
    rows, width = tokens_ref.shape
    windows = read_windows(win_ref, rows)
    hidden_low = hidden_rows(tokens_ref, pos_ref, windows).astype(BF16)
    hidden_ref[...] = hidden_low
    grad_low = grad_resid_ref[...].astype(BF16)
    grad_ref[...] = grad_resid_ref[...] + half_backward(grad_low, *other_refs, gm_ref, work)
    projection_grads(hidden_low, gm_ref, package_ref, other_keep_ref, other_send_ref, split)
    grad_ref[...] += half_backward(grad_low, *own_refs, own_gm_ref, work)
    grad = grad_ref[...]
    tokens_grad_ref[...] = grad.astype(BF16)
    first, second = None, None
    for block, is_long in enumerate(windows):
        top = grad[block * W_LONG : block * W_LONG + W_SHORT]
        bottom = grad[block * W_LONG + W_SHORT : (block + 1) * W_LONG]
        zero = jnp.zeros_like(top)
        part_first = top + jnp.where(is_long, zero, bottom)
        part_second = jnp.where(is_long, bottom, zero)
        first = part_first if first is None else first + part_first
        second = part_second if second is None else second + part_second
    table_ref[0:W_SHORT, :] = first.astype(BF16)
    table_ref[W_SHORT:, :] = second.astype(BF16)
    core_split(table_ref, table_keep_ref, table_send_ref, 0, split)


def project_back_kernel(split, hidden_ref, gm_ref, keep_ref, send_ref, package_ref):
    projection_grads(hidden_ref[...], gm_ref, package_ref, keep_ref, send_ref, split)


def total_of(*values):
    total = values[0].astype(F32)
    for value in values[1:]:
        total = total + value.astype(F32)
    return total


def bit_split(bit, size, terms, keep_ref, send_ref, start=0):
    half = size // 2
    for index, to_ref in ((bit, keep_ref), (1 - bit, send_ref)):
        rows = [pl.ds(pl.multiple_of(first + index * half, 16), half) for _, first in terms]
        to_ref[start : start + half, :] = total_of(
            *[ref[row_range, :] for (ref, _), row_range in zip(terms, rows)]
        ).astype(BF16)


def other_half_kernel(keep_ref, recv_ref, send_ref):
    start = keep_ref.shape[0] - send_ref.shape[0]
    send_ref[...] = total_of(keep_ref[start:, :], recv_ref[start:, :]).astype(BF16)


def down_split_kernel(keep_ref, recv_ref, from_y_ref, x_keep_ref, x_send_ref):
    terms = [(keep_ref, 0), (recv_ref, 0), (from_y_ref, 0)]
    bit_split(place("x"), from_y_ref.shape[0], terms, x_keep_ref, x_send_ref)


def pair_kernel(a_ref, b_ref, out_ref):
    out_ref[...] = total_of(a_ref[...], b_ref[...]).astype(BF16)


def halves_split(bit, keep_ref, recv_ref, to_keep_ref, to_send_ref):
    rows = (keep_ref.shape[0] - EXTRA) // 2
    for half in range(2):
        terms = [(keep_ref, half * rows), (recv_ref, half * rows)]
        bit_split(bit, rows, terms, to_keep_ref, to_send_ref, half * (rows // 2))
    small = total_of(keep_ref[2 * rows :, :], recv_ref[2 * rows :, :]).astype(BF16)
    to_keep_ref[rows:, :] = small
    to_send_ref[rows:, :] = small


def up_split_kernel(keep_ref, recv_ref, z_keep_ref, z_send_ref):
    halves_split(z_bit(), keep_ref, recv_ref, z_keep_ref, z_send_ref)


def down_x_kernel(keep_ref, recv_ref, z_keep_ref, z_send_ref):
    terms = [(keep_ref, 0), (recv_ref, 0)]
    bit_split(z_bit(), keep_ref.shape[0], terms, z_keep_ref, z_send_ref)


def up_x_kernel(keep_ref, recv_ref, x_keep_ref, x_send_ref):
    halves_split(place("x"), keep_ref, recv_ref, x_keep_ref, x_send_ref)


def up_z_kernel(keep_ref, recv_ref, y_keep_ref, y_send_ref):
    rows = y_keep_ref.shape[0] - EXTRA
    y_keep_ref[0:rows, :] = total_of(keep_ref[0:rows, :], recv_ref[0:rows, :]).astype(BF16)
    y_send_ref[...] = total_of(keep_ref[rows:, :], recv_ref[rows:, :]).astype(BF16)
    y_keep_ref[rows:, :] = y_send_ref[rows:, :]


def up_last_kernel(own_ref, recv_ref, out_ref, small_ref):
    rows = out_ref.shape[0]
    out_ref[...] = total_of(own_ref[0:rows, :], recv_ref[0:rows, :]).astype(BF16)
    small_ref[...] = total_of(own_ref[rows:, :], recv_ref[rows:, :])


def small_out_kernel(small_ref, *refs):
    *vector_refs, bias_ref, token_ref = refs
    width = small_ref.shape[1]
    token_ref[...] = jnp.zeros(token_ref.shape, F32)
    for i, ref in enumerate(vector_refs):
        ref[...] = small_ref[i : i + 1, :].reshape(width)
    span = bias_ref.shape[0] // width
    for i in range(span):
        value = small_ref[pl.ds(6 + place("mp") * span + i, 1), :]
        bias_ref[i * width : (i + 1) * width] = value.reshape(width)


def join_kernel(axis, own_ref, recv_ref, out_ref):
    rows = own_ref.shape[0]
    bit = z_bit() if axis == "z" else place("x")
    out_ref[part(bit, rows), :] = own_ref[...]
    out_ref[part(1 - bit, rows), :] = recv_ref[...]


def attend_core_kernel(keep_ref, recv_ref, table_keep_ref, table_recv_ref, to_y_ref, table_ref):
    rows = keep_ref.shape[0]
    to_y_ref[0:rows, :] = total_of(keep_ref[...], recv_ref[...]).astype(BF16)
    terms = [(table_keep_ref, 0), (table_recv_ref, 0)]
    size = table_keep_ref.shape[0]
    bit_split(place("mp"), size, terms, table_ref, to_y_ref.at[rows:, :])


def attend_mp_kernel(keep_ref, recv_ref, from_y_ref, table_ref, x_keep_ref, x_send_ref):
    rows, spare = keep_ref.shape[0], table_ref.shape[0]
    terms = [(keep_ref, 0), (recv_ref, 0), (from_y_ref, 0)]
    bit_split(place("x"), rows, terms, x_keep_ref, x_send_ref)
    terms = [(table_ref, 0), (from_y_ref, rows)]
    bit_split(place("x"), spare, terms, x_keep_ref, x_send_ref, rows // 2)


def attend_x_kernel(spare, keep_ref, recv_ref, z_keep_ref, z_send_ref):
    rows = keep_ref.shape[0] - spare
    for start, size in ((0, rows), (rows, spare)):
        terms = [(keep_ref, start), (recv_ref, start)]
        bit_split(z_bit(), size, terms, z_keep_ref, z_send_ref, start // 2)


def attend_join_kernel(own_ref, recv_ref, out_ref, table_ref):
    spare = table_ref.shape[0] // 2
    rows = own_ref.shape[0] - spare
    for ref, bit in ((own_ref, z_bit()), (recv_ref, 1 - z_bit())):
        out_ref[part(bit, rows), :] = ref[0:rows, :]
        table_ref[part(bit, spare), :] = ref[rows:, :]
    out_ref[2 * rows :, :] = table_ref[...]


def corners(parts, bit):
    own_ref, near_ref, core_own_ref, core_near_ref = parts
    core = place("core")
    return (
        (own_ref, core * 2 + bit),
        (near_ref, core * 2 + 1 - bit),
        (core_own_ref, (1 - core) * 2 + bit),
        (core_near_ref, (1 - core) * 2 + 1 - bit),
    )


def down_out_kernel(*refs):
    *parts, out_ref, token_ref = refs
    token_ref[...] = jnp.zeros(token_ref.shape, F32)
    for ref, index in corners(parts, place("x")):
        out_ref[part(index, ref.shape[0]), :] = ref[...].astype(F32)


def up_out_kernel(*refs):
    *parts, up_ref, out_ref, token_ref, work_ref = refs
    token_ref[...] = jnp.zeros(token_ref.shape, F32)
    for ref, index in corners(parts, z_bit()):
        work_ref[part(index, ref.shape[0]), :] = ref[...]
    width, spare = up_ref.shape[0], out_ref.shape[0] // 2
    for core in range(2):
        start = core * (width + spare)
        up_ref[:, core * width : (core + 1) * width] = work_ref[start : start + width, :].astype(F32)
        start += width
        out_ref[core * spare : (core + 1) * spare, :] = work_ref[start : start + spare, :].astype(F32)


def attend_out_kernel(
    parts, table_parts, qkv_ref, table_ref, work_ref, qkv_out_ref, table_out_ref, sems
):
    y = place("mp")
    spare = table_parts[0].shape[0]
    rows = parts[0].shape[0] - spare
    half = qkv_ref.shape[2]
    width = 2 * half
    for ref, index in corners(parts, place("x")):
        work_ref[part(index, rows), :] = ref[0:rows, :]
        core, x = lax.div(index, 2), lax.rem(index, 2)
        table_out_ref[part(core * 4 + y * 2 + x, spare), :] = ref[rows:, :].astype(F32)
    for ref, index in corners(table_parts, place("x")):
        core, x = lax.div(index, 2), lax.rem(index, 2)
        table_out_ref[part(core * 4 + (1 - y) * 2 + x, spare), :] = ref[...].astype(F32)
    copies = [pltpu.make_async_copy(table_out_ref, table_ref, sems.at[3])]
    copies[0].start()
    for i in range(3):
        if i < 2:
            qkv_out_ref[i] = work_ref[0:width, i * half : (i + 1) * half].astype(F32)
        else:
            qkv_out_ref[i, 0:half, :] = work_ref[width : width + half, 0:half].astype(F32)
            qkv_out_ref[i, half:, :] = work_ref[width : width + half, half:].astype(F32)
        copies.append(pltpu.make_async_copy(qkv_out_ref.at[i], qkv_ref.at[i], sems.at[i]))
        copies[-1].start()
    for copy in copies:
        copy.wait()


def swap(value, axis, name="swap", distance=1):
    pairs = [(i, i ^ distance) for i in range(lax.axis_size(axis))]
    with jax.named_scope(f"{name}_{axis}{distance}"):
        return lax.ppermute(value, axis, pairs)


def swap_corner(value, name):
    with jax.named_scope(name):
        return lax.ppermute(value, ("x", "mp"), [(0, 3), (1, 2), (2, 1), (3, 0)])


class Chain:
    def __init__(self):
        self.last = ()

    def gate(self, value, us=1):
        value = pl.pallas_call(
            lambda *refs: None,
            out_shape=jax.ShapeDtypeStruct(value.shape, value.dtype),
            in_specs=[anywhere] * (1 + len(self.last)),
            out_specs=anywhere,
            input_output_aliases={0: 0},
            compiler_params=pltpu.CompilerParams(vmem_limit_bytes=MIB),
            cost_estimate=pl.CostEstimate(
                flops=us * FLOPS_PER_US, bytes_accessed=0, transcendentals=0
            ),
            name="gate",
        )(value, *self.last)
        self.last = (value,)
        return value

    def __call__(
        self,
        kernel,
        outs,
        args,
        us,
        name,
        scratch=(),
        smem_args=0,
        hbm_args=0,
        copies=0,
        mib=8,
        token=None,
        hbm_outs=False,
    ):
        results = call(
            kernel, outs, args, self.last, scratch, us, mib, smem_args, hbm_args, copies, hbm_outs, name
        )
        if token is None:
            token = min(range(len(results)), key=lambda i: results[i].size)
        self.last = (results[token],)
        return results


def per_device(
    fast,
    mp_size,
    tokens,
    pos_table,
    qkv_weight,
    out_weight,
    out_bias,
    norm1_gain,
    norm1_shift,
    up_weight,
    up_bias,
    down_weight,
    down_bias,
    norm2_gain,
    norm2_shift,
    window,
    cotangent,
):
    step = Chain()
    rows, width = tokens.shape
    blocks = rows // W_LONG
    half_width = width // 2
    units = up_weight.shape[1] * mp_size // 2
    n, spare = width, W_LONG // 2
    group, att = (units + half_width) // 2, 3 * width // 4
    qkv_weight = jnp.transpose(qkv_weight, (1, 0, 2))
    wide = ((rows, width), F32)

    attend_outs = [
        (3, rows, half_width),
        (blocks * half_width // LANES, 2 * W_LONG, W_SHORT),
        (blocks * half_width // LANES, W_LONG, W_SHORT),
        (rows, half_width),
    ]

    def attend_own():
        return step(
            first_kernel,
            attend_outs,
            [window, tokens, pos_table, w_own],
            3,
            "attend_first",
            mib=28,
            smem_args=1,
        )

    def attend_other():
        return step(
            second_kernel,
            attend_outs
            + [wide, (3, width, half_width), (half_width, width), ((units,), F32)],
            [window, tokens, pos_table, attend_in, context_own, out_own, out_bias],
            5,
            "attend_second",
            mib=28,
            smem_args=1,
        )

    def ffn_own():
        return step(
            ffn_own_kernel,
            [(rows, width), (rows, units), (rows, units), wide],
            [resid, up_own, down_own, bias_own, norm1_gain, norm1_shift],
            4,
            "ffn_own",
            mib=28,
        )

    if fast:
        w_own, out_own, up_own, down_own = qkv_weight, out_weight, up_weight, down_weight
        bias_own = up_bias
        (message,) = step(
            pack_attend_kernel,
            [(width // 2 + EXTRA, width)],
            [up_bias, qkv_weight, out_weight],
            1,
            "pack_attend",
            mib=63,
            hbm_args=2,
            copies=5,
        )
        attend_y = swap(message, "mp", "attend_y")
        up_message, down_message = step(
            pack_ffn_kernel,
            [(units // 8, width), (units // 4, width)],
            [up_weight, down_weight],
            1,
            "pack_ffn",
            mib=60,
            hbm_args=2,
            copies=1 + units // width,
        )
        up_y = swap(up_message, "mp", "up_y")
        down_y = swap(down_message, "mp", "down_y")
        mixed_own, early_own, late_own, context_own = attend_own()
        attend_y = step.gate(attend_y, 0)
        attend_x = swap(attend_y, "x", "attend_x")
        up_y = step.gate(up_y, 0)
        up_z = swap(up_y, "z", "up_z")
        (up_y,) = step(z_join_kernel, [(units // 4, width)], [up_y, up_z], 0, "up_pair")
        up_x = swap(up_y, "x", "up_x")
        up_cy = swap(up_y, "core", "up_cy")
        down_y = step.gate(down_y, 1)
        down_z = swap(down_y, "z", "down_z")
        attend_x = step.gate(attend_x, 0)
        attend_cx = swap(attend_x, "core", "attend_cx")
        attend_cy = swap(attend_y, "core", "attend_cy")
        attend_in = (attend_y, attend_x, attend_cy, attend_cx)
        mixed_oth, early_oth, late_oth, context_oth, resid, w_oth, out_oth, bias_oth = attend_other()
        low, act_own, slope_own, branch = ffn_own()
        up_x = step.gate(up_x, 0)
        up_cx = swap(up_x, "core", "up_cx")
        down_z = step.gate(down_z, 4)
        down_cy = swap(down_y, "core", "down_cy")
        down_cz = swap(down_z, "core", "down_cz")
        up_in = (up_y, up_x, up_cy, up_cx)
        down_in = (down_y, down_z, down_cy, down_cz)
    else:
        qkv = lax.all_gather(qkv_weight, "mp", axis=2, tiled=True)
        out_w = lax.all_gather(out_weight, "mp", axis=0, tiled=True)
        up_w = lax.all_gather(up_weight, "mp", axis=1, tiled=True)
        bias = lax.all_gather(up_bias, "mp", axis=0, tiled=True)
        down_w = lax.all_gather(down_weight, "mp", axis=0, tiled=True)
        w_own, out_own = qkv[:, :, :half_width], out_w[:half_width]
        attend_in = (qkv[:, :, half_width:], out_w[half_width:], bias[units:])
        up_own, up_in = up_w[:, :units], (up_w[:, units:],)
        down_own, down_in = down_w[:units], (down_w[units:],)
        bias_own = bias[:units]
        mixed_own, early_own, late_own, context_own = attend_own()
        mixed_oth, early_oth, late_oth, context_oth, resid, w_oth, out_oth, bias_oth = attend_other()
        low, act_own, slope_own, branch = ffn_own()

    layer_out, down_keep, down_send, slope_oth, up_oth, down_oth, grad2, vec = step(
        functools.partial(ffn_other_kernel, fast),
        [
            (rows, width),
            (units, width),
            (units, width),
            (rows, units),
            (width, units),
            (units, width),
            wide,
            ((8, width), F32),
        ],
        [
            cotangent,
            low,
            act_own,
            branch,
            up_in,
            down_in,
            bias_oth,
            down_bias,
            norm2_gain,
            norm2_shift,
        ],
        6,
        "ffn_other",
            mib=28,
        scratch=[((rows, units), BF16), ((units, width), BF16)],
    )
    down_recv = swap(down_send, "core", "down_recv") if fast else None
    up_keep, up_send, small, grad1 = step(
        functools.partial(ffn_back_kernel, fast),
        [
            (2 * group + EXTRA, width),
            (2 * group + EXTRA, width),
            ((EXTRA, width), F32),
            wide,
        ],
        [
            resid,
            grad2,
            low,
            (slope_own, slope_oth),
            (up_own, up_oth),
            (down_own, down_oth),
            (context_own, context_oth),
            vec,
            norm1_gain,
        ],
        6,
        "ffn_back",
            mib=28,
        scratch=[
            ((rows, units), BF16),
            ((rows, width), F32),
            ((units, width), BF16),
            ((8, width), F32),
            ((half_width, width), BF16),
        ],
    )

    def attend_back():
        return step(
            functools.partial(attend_back_kernel, fast),
            [(att, width)] * 2
            + [(spare, width)] * 2
            + [(rows, width)] * 2
            + [(3, rows, half_width)],
            [
                window,
                tokens,
                pos_table,
                grad1,
                (w_own, out_own, mixed_own, early_own, late_own),
                (w_oth, out_oth, mixed_oth, early_oth, late_oth),
            ],
            13,
            "attend_back",
            mib=28,
            scratch=[
                ((rows, width), F32),
                ((3, rows, half_width), BF16),
                ((2 * att, width), BF16),
                ((W_LONG, width), BF16),
                ((half_width // LANES, 2 * W_LONG, W_SHORT), BF16),
                ((half_width // LANES, W_LONG, W_SHORT), BF16),
            ],
            smem_args=1,
        )

    def project_back(hidden, own_gm):
        return step(
            functools.partial(project_back_kernel, fast),
            [(att, width)] * 2,
            [hidden, own_gm],
            0,
            "project_back",
            mib=16,
            scratch=[((2 * att, width), BF16)],
        )

    if not fast:
        *oth_parts, grad_tokens, hidden, own_gm = attend_back()
        att_parts = (*oth_parts[:2], *project_back(hidden, own_gm), *oth_parts[2:])
        qkv_g, out_g, up_g, down_g, small, table = reduce_plain(
            n, width, down_keep, down_send, up_keep, up_send, small, *att_parts
        )
        vectors = [small[i] for i in range(6)]
        bias_all = small[6 : 6 + 2 * units // width].reshape(-1)
        start = lax.axis_index("mp") * up_bias.shape[0]
        bias_g = lax.dynamic_slice_in_dim(bias_all, start, up_bias.shape[0])
    else:
        half, piece, strip = n // 2, n // 4, spare // 2
        up_recv = swap(up_send, "core", "up_recv")
        (to_y,) = step(other_half_kernel, [(n, width)], [down_keep, down_recv], 6, "down_core")
        down_from_y = swap(to_y, "mp", "down_from_y")
        up_x, to_x = step(
            up_split_kernel,
            [(group + EXTRA, width)] * 2,
            [up_keep, up_recv],
            5,
            "up_core",
        )
        up_from_x = swap(to_x, "z", "up_from_z")
        oth_keep, oth_send, tab_keep, tab_send, grad_tokens, hidden, own_gm = attend_back()
        oth_recv = swap(oth_send, "core", "oth_recv")
        tab_recv = swap(tab_send, "core", "tab_recv")
        own_keep, own_send = project_back(hidden, own_gm)
        own_recv = swap(own_send, "core", "own_recv")
        down_x, to_x = step(
            down_split_kernel,
            [(half, width)] * 2,
            [down_keep, down_recv, down_from_y],
            0,
            "down_mp",
        )
        down_from_x = swap(to_x, "x", "down_from_x")
        to_y, table = step(
            attend_core_kernel,
            [(att + strip, width), (strip, width)],
            [oth_keep, oth_recv, tab_keep, tab_recv],
            0,
            "attend_core",
        )
        att_from_y = swap(to_y, "mp", "att_from_y")
        up_z, to_z = step(
            up_x_kernel,
            [(group // 2 + EXTRA, width)] * 2,
            [up_x, up_from_x],
            5,
            "up_x",
        )
        up_from_z = swap(to_z, "x", "up_from_x")
        down_z, to_z = step(
            down_x_kernel,
            [(piece, width)] * 2,
            [down_x, down_from_x],
            3,
            "down_x",
        )
        down_from_z = swap(to_z, "z", "down_from_z")
        (down_z,) = step(pair_kernel, [(piece, width)], [down_z, down_from_z], 0, "down_z")
        down_far = swap(down_z, "z", "down_far", 2)
        att_x, to_x = step(
            attend_mp_kernel,
            [((att + strip) // 2, width)] * 2,
            [own_keep, own_recv, att_from_y, table],
            0,
            "attend_mp",
        )
        att_from_x = swap(to_x, "x", "att_from_x")
        up_y, to_y = step(
            up_z_kernel, [(group // 4 + EXTRA, width)] * 2, [up_z, up_from_z], 1, "up_z"
        )
        up_from_y = swap(to_y, "mp", "up_from_y")
        (down_z,) = step(pair_kernel, [(piece, width)], [down_z, down_far], 0, "down_far")
        down_near = swap(down_z, "z", "down_near")
        att_z, to_z = step(
            functools.partial(attend_x_kernel, strip // 2),
            [((att + strip) // 4, width)] * 2,
            [att_x, att_from_x],
            0,
            "attend_x",
        )
        att_from_z = swap(to_z, "z", "att_from_z")
        (up_y,) = step(pair_kernel, [(group // 4 + EXTRA, width)], [up_y, up_from_y], 0, "up_mp")
        up_far = swap(up_y, "z", "up_far", 2)
        (down_z,) = step(functools.partial(join_kernel, "z"), [(half, width)], [down_z, down_near], 7, "down_join")
        down_x = swap(down_z, "x", "down_x")
        (att_z,) = step(pair_kernel, [att_z.shape], [att_z, att_from_z], 0, "attend_z")
        att_far = swap(att_z, "z", "att_far", 2)
        up_z, small = step(
            up_last_kernel,
            [(group // 4, width), ((EXTRA, width), F32)],
            [up_y, up_far],
            0,
            "up_far",
        )
        up_near = swap(up_z, "x", "up_near")
        (att_z,) = step(pair_kernel, [att_z.shape], [att_z, att_far], 0, "attend_far")
        att_near = swap(att_z, "z", "att_near")
        att_half, table = step(
            attend_join_kernel,
            [((att + strip) // 2, width), (strip // 2, width)],
            [att_z, att_near],
            0,
            "attend_join",
        )
        att_x = swap(att_half, "x", "att_x")
        table_y = swap(table, "mp", "table_y")
        table_x = swap_corner(table, "table_x")
        (up_z,) = step(functools.partial(join_kernel, "x"), [(group // 2, width)], [up_z, up_near], 0, "up_join")
        up_x = swap(up_z, "z", "up_last")
        down_x = step.gate(down_x, 0)
        *vectors, bias_g, _ = step(
            small_out_kernel,
            [((width,), F32)] * 6 + [((up_bias.shape[0],), F32), ((8, LANES), F32)],
            [small],
            0,
            "small_out",
            token=7,
        )
        down_g, _ = step(
            down_out_kernel,
            [((2 * n, width), F32), ((8, LANES), F32)],
            [
                down_z,
                down_x,
                swap(down_z, "core", "down_core"),
                swap(down_x, "core", "down_core_x"),
            ],
            0,
            "down_out",
        )
        table_y = step.gate(table_y, 0)
        up_x = step.gate(up_x, 0)
        table_x = step.gate(table_x, 2)
        att_x = step.gate(att_x, 1)
        up_g, out_g, _ = step(
            up_out_kernel,
            [((width, 2 * n), F32), ((half_width, width), F32), ((8, LANES), F32)],
            [up_z, up_x, swap(up_z, "core", "up_core"), swap(up_x, "core", "up_core_x")],
            0,
            "up_out",
            scratch=[((2 * group, width), BF16)],
        )
        qkv_g, table = step(
            attend_out_kernel,
            [((3, width, half_width), F32), ((W_LONG, width), F32)],
            [
                (
                    att_half,
                    att_x,
                    swap(att_half, "core", "att_core"),
                    swap(att_x, "core", "att_core_x"),
                ),
                (
                    table_y,
                    table_x,
                    swap(table_y, "core", "table_core"),
                    swap(table_x, "core", "table_core_x"),
                ),
            ],
            0,
            "attend_out",
            scratch=[
                ((2 * att, width), BF16),
                ((3, width, half_width), F32),
                ((W_LONG, width), F32),
            ],
            copies=4,
            hbm_outs=True,
        )


    return (
        layer_out,
        grad_tokens,
        table,
        jnp.transpose(qkv_g, (1, 0, 2)),
        out_g,
        vectors[0],
        vectors[1],
        vectors[2],
        up_g,
        bias_g,
        down_g,
        vectors[3],
        vectors[4],
        vectors[5],
    )


def reduce_plain(
    n,
    width,
    down_keep,
    down_send,
    up_keep,
    up_send,
    small,
    other_keep,
    other_send,
    own_keep,
    own_send,
    table_keep,
    table_send,
):
    half, spare = n // 2, n // 4
    group = n + spare

    def rows_of(start, size):
        return lambda keep, send: jnp.concatenate(
            [keep[start : start + size], send[start : start + size]], axis=0
        )

    def summed(own, oth, dim):
        whole = jnp.concatenate([own, oth], axis=dim)
        part_sum = lax.psum_scatter(whole, "mp", scatter_dimension=dim, tiled=True)
        return lax.psum(part_sum, "dp").astype(F32)

    def qkv_part(g):
        value = jnp.concatenate([g[n : n + half, :half], g[n : n + half, half:]], axis=0)
        return jnp.stack([g[:n, :half], g[:n, half:], value])

    def up_part(g):
        return jnp.concatenate([g[:n], g[n:]], axis=1)

    down = [rows_of(start, n)(down_keep, down_send) for start in (0, n)]
    up = [up_part(rows_of(start, n)(up_keep, up_send)) for start in (0, group)]
    out = [rows_of(start + n, spare)(up_keep, up_send) for start in (0, group)]
    att = [
        qkv_part(jnp.concatenate(pair, axis=0))
        for pair in ((own_keep, own_send), (other_keep, other_send))
    ]
    table = jnp.concatenate([table_keep, table_send], axis=0).astype(F32)
    return (
        summed(*att, 2),
        summed(*out, 0),
        summed(*up, 1),
        summed(*down, 0),
        lax.psum(small, ("dp", "mp")),
        lax.psum(table, ("dp", "mp")),
    )


def solution(mesh):
    mp_size = mesh.shape["mp"]
    fast = mp_size == 2 and mesh.shape["dp"] == 16
    dp = "dp"
    if fast:
        shape = (mesh.shape["dp"] // 4, 2, 2, mp_size)
        mesh = Mesh(mesh.devices.reshape(shape), ("z", "x", "core", "mp"))
        dp = ("z", "x", "core")
    both = P((*dp, "mp") if fast else (dp, "mp"), None)
    placed = (
        both,
        P(),
        P(None, None, "mp"),
        P("mp", None),
        P(),
        P(),
        P(),
        P(None, "mp"),
        P("mp"),
        P("mp", None),
        P(),
        P(),
        P(),
        P(dp),
        both,
    )
    return jax.shard_map(
        functools.partial(per_device, fast, mp_size),
        mesh=mesh,
        in_specs=placed,
        out_specs=(
            both,
            both,
            P(),
            P(None, None, "mp"),
            P("mp", None),
            P(),
            P(),
            P(),
            P(None, "mp"),
            P("mp"),
            P("mp", None),
            P(),
            P(),
            P(),
        ),
        check_vma=False,
    )
```
